32 devices in a mesh: outer: 4 (over x, core), inner: 8 (over z, y).
Axes of the slice: x: 2, y: 2, z: 4, core: 2. Of those that a mesh axis runs over, the one named last changes fastest.
Arguments:
- inputs: bfloat16 [32768, 1024], P(('outer', 'inner')), may hold values from -6 to 6
- queries: bfloat16 [32768, 1024], P(('outer', 'inner')), may hold values from -6 to 6
- keys: bfloat16 [32768, 1024], P(('outer', 'inner')), may hold values from -6 to 6
- values: bfloat16 [32768, 1024], P(('outer', 'inner')), may hold values from -6 to 6
- out_grad: bfloat16 [32768, 1024], P(('outer', 'inner')), may hold values from -6 to 6
- master: float32 [1024, 1024], P('inner'), may hold values from -0.1875 to 0.1875
- moment1: float32 [1024, 1024], P('inner'), may hold values from -6 to 6
- moment2: float32 [1024, 1024], P('inner'), may hold values from 0.05 to 2
Outputs:
- query_grad: bfloat16 [32768, 1024], P(('outer', 'inner'))
- key_grad: bfloat16 [32768, 1024], P(('outer', 'inner'))
- new_master: float32 [1024, 1024], P('inner')
- new_moment1: float32 [1024, 1024], P('inner')
- new_moment2: float32 [1024, 1024], P('inner')
- weights: bfloat16 [1024, 1024], replicated
The draws below stay inside these ranges and needn't reach their ends.
All inputs are finite; a program needn't handle non-finite values.
Results may differ from the reference program's by a relative error of at most 0.008.
Values may be sent and summed in bfloat16 or wider, within the bound.
No kernel may reach another device: no remote copies, remote signals or barrier semaphores. Data moves between devices by JAX's collectives and lax.ppermute only.
A program may use at most 192 MiB of HBM per device.

```python
import math
import jax
import jax.numpy as jnp
from jax import lax

D = 1024
H = 8
HD = 128
BLK = 512
TOKENS = 32768


def raised(entries, stream_key, source, target, shards_of, factor):
    owner, partner = [(jnp.arange(entries.shape[dim]) // (entries.shape[dim] // shards_of)).reshape([-1 if axis == dim else 1 for axis in range(entries.ndim)]) for dim in (source, target)]
    chosen = jax.random.permutation(stream_key, shards_of)[partner]
    strong = (owner == chosen) | (owner == (partner + shards_of // 2) % shards_of)
    return jnp.where(strong, factor * entries, entries)


def block_levels(own_key, dims, pieces, low, largest):
    def one(axis_at, blocks):
        heights = jax.random.uniform(jax.random.fold_in(jax.random.fold_in(own_key, 6), axis_at), (blocks,), jnp.float32, low / len(pieces), largest / len(pieces))
        return jnp.repeat(jnp.exp(heights), dims[axis_at] // blocks).reshape((-1,) + (1,) * (len(dims) - axis_at - 1))

    factor_of = one(*pieces[0])
    for cut in pieces[1:]:
        factor_of = factor_of * one(*cut)
    return factor_of


def noise(stream_key, dims, width, limit, split=(), held_as=jnp.bfloat16):
    drawn = jax.random.normal(stream_key, dims, jnp.float32) * width
    if len(split) > 0:
        drawn = block_levels(stream_key, dims, split, -0.22, 0.18) * drawn
    return jnp.clip(drawn, min=-limit, max=limit).astype(held_as)


def bell_draw_with(rng, dims, spread, reach, pieces, heavy, kind=jnp.bfloat16):
    drawn = spread * jax.random.normal(rng, dims, jnp.float32)
    if pieces:
        drawn = drawn * block_levels(rng, dims, pieces, -0.22, 0.18)
    return jnp.clip(raised(drawn, jax.random.fold_in(rng, 3), *heavy), -reach, reach).astype(kind)


def setup_inputs(seed: int = 0) -> dict:
    arg_keys = jax.random.split(jax.random.key(seed), 9)
    inputs = bell_draw_with(arg_keys[0], (TOKENS, D), 1.0, 6.0, ((0, 32),), (0, 1, 32, 2.75))
    queries = noise(arg_keys[1], (TOKENS, D), 1.0, 6.0, ((0, 32),))
    keys = noise(arg_keys[2], (TOKENS, D), 1.0, 6.0, ((0, 32),))
    values = noise(arg_keys[3], (TOKENS, D), 1.0, 6.0, ((0, 32),))
    out_grad = noise(arg_keys[4], (TOKENS, D), 1.0, 6.0, ((0, 32),))
    master = noise(arg_keys[5], (D, D), D ** -0.5, 0.1875, ((0, 8),), jnp.float32)
    moment1 = noise(arg_keys[6], (D, D), 1.0, 6.0, ((0, 8),), jnp.float32)
    moment2 = jnp.clip(jnp.exp(math.log(2.0) - 3.6888794 * jax.random.uniform(arg_keys[7], (D, D), jnp.float32) ** block_levels(arg_keys[7], (D, D), ((0, 8),), -0.2, 0.2)), 0.05, 2.0)
    return {"inputs": inputs, "queries": queries, "keys": keys, "values": values, "out_grad": out_grad, "master": master, "moment1": moment1, "moment2": moment2}


def reference(inputs, queries, keys, values, out_grad, master, moment1, moment2):
    blocks = TOKENS // BLK
    att_scale = 1.0 / math.sqrt(HD * TOKENS)
    grad_scale = 1.0 / math.sqrt(TOKENS)
    shape_four = (blocks, BLK, H, HD)
    query_blocks = queries.reshape(shape_four)
    key_blocks = keys.reshape(shape_four)
    value_blocks = values.reshape(shape_four)
    grad_blocks = out_grad.reshape(shape_four)
    highest_setting = lax.Precision.HIGHEST

    def block_states(items):
        query_b, key_block_rows, value_block_rows, block_gradient = [item.astype(jnp.float32) for item in items]
        key_value_state = jnp.einsum('yze,yza->zea', key_block_rows, value_block_rows, precision=highest_setting)
        grad_query = jnp.einsum('thv,thk->hvk', block_gradient, query_b, precision=highest_setting)
        return (key_value_state, grad_query)
    kv_block, qg_block = lax.map(block_states, (query_blocks, key_blocks, value_blocks, grad_blocks))
    zero_state = jnp.zeros((1, H, HD, HD), jnp.float32)
    key_value_prior = jnp.concatenate([zero_state, jnp.cumsum(kv_block, 0)[:-1]], 0)
    qg_reverse = jnp.cumsum(qg_block[::-1], 0)[::-1]
    qg_after = jnp.concatenate([qg_reverse[1:], zero_state], 0)
    causal = jnp.arange(BLK)[:, None] >= jnp.arange(BLK)[None, :]

    def block_grads(items):
        query_b, key_block_rows, value_block_rows, block_gradient, prior_block_state, after_b = items
        query_f = query_b.astype(jnp.float32)
        key_f = key_block_rows.astype(jnp.float32)
        value_f = value_block_rows.astype(jnp.float32)
        flat_gradient = block_gradient.astype(jnp.float32)
        scores = jnp.einsum('thv,shv->hts', flat_gradient, value_f, precision=highest_setting)
        scores = jnp.where(causal[None], scores, 0.0).astype(jnp.bfloat16).astype(jnp.float32)
        query_gradient = jnp.einsum('hts,shk->thk', scores, key_f, precision=highest_setting)
        query_gradient = query_gradient + jnp.einsum('rgn,gfn->rgf', flat_gradient, prior_block_state, precision=highest_setting)
        dkey = jnp.einsum('hts,thk->shk', scores, query_f, precision=highest_setting)
        dkey = dkey + jnp.einsum('shv,hvk->shk', value_f, after_b, precision=highest_setting)
        query_gradient = (query_gradient * att_scale).astype(jnp.bfloat16).reshape(BLK, D)
        dkey = (dkey * att_scale).astype(jnp.bfloat16).reshape(BLK, D)
        return (query_gradient, dkey)
    query_grad, key_grad = lax.map(block_grads, (query_blocks, key_blocks, value_blocks, grad_blocks, key_value_prior, qg_after))
    input_blocks = inputs.reshape(blocks, BLK, D)

    def accumulate(total, items):
        input_b, dkey_b = items
        term = jnp.dot(input_b.astype(jnp.float32).T, dkey_b.astype(jnp.float32), precision=highest_setting)
        return (total + term, None)
    grad, unused = lax.scan(accumulate, jnp.zeros((D, D), jnp.float32), (input_blocks, key_grad))
    grad = grad * grad_scale
    new_moment1 = 0.9 * moment1 + 0.1 * grad
    new_moment2 = 0.95 * moment2 + 0.05 * grad * grad
    new_master = master - 0.01 * (new_moment1 / (jnp.sqrt(new_moment2) + 1e-08) + 0.1 * master)
    return (query_grad.reshape(TOKENS, D), key_grad.reshape(TOKENS, D), new_master, new_moment1, new_moment2, new_master.astype(jnp.bfloat16))
```

```python
import functools
import math

import jax
import jax.numpy as jnp
from jax import lax
from jax.experimental import pallas as pl
from jax.experimental.pallas import tpu as pltpu
from jax.sharding import PartitionSpec as P

HD = 128
SUB = 256
PAIR = 2 * HD
VMEM = 40 * 1024 * 1024
F32 = jnp.float32
BF16 = jnp.bfloat16


def mm(a, b, contract):
    return lax.dot_general(a, b, ((contract[:1], contract[1:]), ((), ())), preferred_element_type=F32)


def params():
    return pltpu.CompilerParams(vmem_limit_bytes=VMEM, dimension_semantics=("arbitrary",))


def cost(macs, moved):
    return pl.CostEstimate(flops=2 * macs, bytes_accessed=moved, transcendentals=0)


def states_body(pick, a_ref, b_ref, out_ref):
    for j in range(2):
        cols = slice(j * HD, (j + 1) * HD)
        out_ref[j] = mm(a_ref[:, cols], b_ref[:, cols], (0, 0)).astype(out_ref.dtype)


def states(a, b, pick, dtype):
    rows = a.shape[0]
    n = pick.shape[0]
    spec = pl.BlockSpec((rows, PAIR), lambda s, pick: (0, pick[s]))
    return pl.pallas_call(
        states_body,
        grid_spec=pltpu.PrefetchScalarGridSpec(
            num_scalar_prefetch=1,
            grid=(n,),
            in_specs=[spec, spec],
            out_specs=pl.BlockSpec((2, HD, HD), lambda s, pick: (s, 0, 0)),
        ),
        out_shape=jax.ShapeDtypeStruct((2 * n, HD, HD), dtype),
        compiler_params=params(),
        cost_estimate=cost(n * rows * 2 * HD * HD, 4 * n * rows * PAIR),
    )(pick, a, b)


def key_inside_body(scale, g_ref, q_ref, v_ref, out_ref):
    rows = g_ref.shape[0]
    later = lax.broadcasted_iota(jnp.int32, (SUB, SUB), 1) >= lax.broadcasted_iota(jnp.int32, (SUB, SUB), 0)
    for j in range(2):
        cols = slice(j * HD, (j + 1) * HD)
        state = None
        for b in reversed(range(rows // SUB)):
            here = slice(b * SUB, (b + 1) * SUB)
            g, q, v = g_ref[here, cols], q_ref[here, cols], v_ref[here, cols]
            scores = jnp.where(later, mm(v, g, (1, 1)), 0.0).astype(BF16)
            total = mm(scores, q, (1, 0))
            if state is not None:
                total = total + mm(v, state.astype(BF16), (1, 0))
            out_ref[here, cols] = (total * scale).astype(out_ref.dtype)
            if b:
                term = mm(g, q, (0, 0))
                state = term if state is None else state + term


def key_inside(g, q, v, scale):
    rows, width = g.shape
    spec = pl.BlockSpec((rows, PAIR), lambda s: (0, s))
    return pl.pallas_call(
        functools.partial(key_inside_body, scale),
        grid=(width // PAIR,),
        in_specs=[spec] * 3,
        out_specs=spec,
        out_shape=jax.ShapeDtypeStruct((rows, width), BF16),
        compiler_params=params(),
        cost_estimate=cost(rows * width * (2 * SUB + 2 * HD), 8 * rows * width),
    )(g, q, v)


def head_of(ref_own, ref_oth, other, at):
    return jnp.where(other, ref_oth[at], ref_own[at])


def query_body(scale, half, g_ref, k_ref, v_ref, own_ref, oth_ref, out_ref):
    rows = g_ref.shape[0]
    step = pl.program_id(0)
    heads_half = own_ref.shape[0]
    earlier = lax.broadcasted_iota(jnp.int32, (SUB, SUB), 0) >= lax.broadcasted_iota(jnp.int32, (SUB, SUB), 1)
    for j in range(2):
        cols = slice(j * HD, (j + 1) * HD)
        head = step * 2 + j
        other = (head // heads_half) != half[0]
        state = head_of(own_ref, oth_ref, other, lax.rem(head, heads_half)).astype(F32)
        for b in range(rows // SUB):
            here = slice(b * SUB, (b + 1) * SUB)
            g, k, v = g_ref[here, cols], k_ref[here, cols], v_ref[here, cols]
            scores = jnp.where(earlier, mm(g, v, (1, 1)), 0.0).astype(BF16)
            total = mm(scores, k, (1, 0)) + mm(g, state.astype(BF16), (1, 0))
            out_ref[here, cols] = (total * scale).astype(out_ref.dtype)
            if b + 1 < rows // SUB:
                state = state + mm(v, k, (0, 0))


def query_side(g, k, v, own, oth, half, scale):
    rows, width = g.shape
    spec = pl.BlockSpec((rows, PAIR), lambda s, half: (0, s))
    whole = pl.BlockSpec(own.shape, lambda s, half: (0, 0, 0))
    return pl.pallas_call(
        functools.partial(query_body, scale),
        grid_spec=pltpu.PrefetchScalarGridSpec(
            num_scalar_prefetch=1,
            grid=(width // PAIR,),
            in_specs=[spec] * 3 + [whole] * 2,
            out_specs=spec,
        ),
        out_shape=jax.ShapeDtypeStruct((rows, width), BF16),
        compiler_params=params(),
        cost_estimate=cost(rows * width * (2 * SUB + 2 * HD), 8 * rows * width),
    )(half, g, k, v, own, oth)


def turned_body(parts, place, in_ref, out_ref):
    step = pl.program_id(0)
    turned = in_ref[...].T
    size = turned.shape[0] // parts
    for j in range(parts):
        at = pl.multiple_of(place[step * parts + j] * size, size)
        out_ref[pl.ds(at, size), :] = turned[j * size : (j + 1) * size, :]


def turned_inputs(inputs, place):
    rows, width = inputs.shape
    block = width // place.shape[0]
    cols = max(block, HD)
    return pl.pallas_call(
        functools.partial(turned_body, cols // block),
        grid_spec=pltpu.PrefetchScalarGridSpec(
            num_scalar_prefetch=1,
            grid=(width // cols,),
            in_specs=[pl.BlockSpec((rows, cols), lambda s, place: (0, s))],
            out_specs=pl.BlockSpec((width, rows), lambda s, place: (0, 0)),
        ),
        out_shape=jax.ShapeDtypeStruct((width, rows), BF16),
        compiler_params=params(),
        cost_estimate=cost(0, 4 * rows * width),
    )(place, inputs)


def key_product_body(scale, grad_scale, n_inner, pick, half, *refs):
    inside_ref, v_ref, own_ref, oth_ref, inputs_ref = refs[:5]
    key_ref, p_ref, q_ref = refs[-3:]
    heads_half = own_ref.shape[0]
    quarter = pick[pl.program_id(0)]
    heads = v_ref.shape[1] // HD
    parts = []
    for j in range(heads):
        cols = slice(j * HD, (j + 1) * HD)
        head = quarter * heads + j
        other = (head // heads_half) != half[0]
        state = head_of(own_ref, oth_ref, other, lax.rem(head, heads_half))
        total = inside_ref[:, cols].astype(F32) + mm(v_ref[:, cols], state, (1, 0)) * scale
        parts.append(total.astype(BF16))
    key_grad = jnp.concatenate(parts, 1)
    key_ref[...] = key_grad
    product = (mm(inputs_ref[...], key_grad, (1, 0)) * grad_scale).astype(BF16)
    size = product.shape[0] // n_inner
    for r in range(n_inner):
        p_ref[0, r] = product[r * size : r * size + size // 2]
        q_ref[0, r] = product[r * size + size // 2 : (r + 1) * size]


def key_product(inside, v, own, oth, turned, pick, half, scale, grad_scale, n_inner, n_outer, before):
    rows, width = v.shape
    cols = width // n_outer
    n = pick.shape[0]
    d = turned.shape[0]
    part = d // n_inner // 2
    spec = pl.BlockSpec((rows, cols), lambda s, pick, half: (0, pick[s]))
    whole = pl.BlockSpec(own.shape, lambda s, pick, half: (0, 0, 0))
    in_specs = [spec, spec, whole, whole, pl.BlockSpec((d, rows), lambda s, pick, half: (0, 0))]
    args = [inside, v, own, oth, turned]
    aliases = {}
    if before is not None:
        in_specs.append(pl.BlockSpec(memory_space=pl.ANY))
        args.append(before)
        aliases = {2 + len(args) - 1: 0}
    piece = pl.BlockSpec((1, n_inner, part, cols), lambda s, pick, half: (s, 0, 0, 0))
    return pl.pallas_call(
        functools.partial(key_product_body, scale, grad_scale, n_inner),
        grid_spec=pltpu.PrefetchScalarGridSpec(
            num_scalar_prefetch=2, grid=(n,), in_specs=in_specs, out_specs=[spec, piece, piece]
        ),
        out_shape=[
            jax.ShapeDtypeStruct((rows, width), BF16),
            jax.ShapeDtypeStruct((n, n_inner, part, cols), BF16),
            jax.ShapeDtypeStruct((n, n_inner, part, cols), BF16),
        ],
        input_output_aliases=aliases,
        compiler_params=params(),
        cost_estimate=cost(n * cols * rows * (d + HD), 2 * rows * (d + 4 * n * cols)),
    )(pick, half, *args)


def adam(grad, master, moment1, moment2):
    new_moment1 = 0.9 * moment1 + 0.1 * grad
    new_moment2 = 0.95 * moment2 + 0.05 * grad * grad
    new_master = master - 0.01 * (new_moment1 / (jnp.sqrt(new_moment2) + 1e-08) + 0.1 * master)
    return new_master, new_moment1, new_moment2


def adam_own_body(pick, keep_ref, came_ref, master_ref, m1_ref, m2_ref, grad_ref, weight_ref):
    part = keep_ref.shape[1]
    for j in range(2):
        here = slice(j * part, (j + 1) * part)
        grad = (keep_ref[j].astype(F32) + came_ref[j].astype(F32)).astype(BF16)
        grad_ref[here, :] = grad
        new_master, _, _ = adam(grad.astype(F32), master_ref[here, :], m1_ref[here, :], m2_ref[here, :])
        weight_ref[j] = new_master.astype(BF16)


def adam_own(keep, came, master, moment1, moment2, pick):
    _, part, cols = keep.shape
    rows = 2 * part
    whole = pl.BlockSpec(keep.shape, lambda s, pick: (0, 0, 0))
    state = pl.BlockSpec((rows, cols), lambda s, pick: (0, pick[s]))
    return pl.pallas_call(
        adam_own_body,
        grid_spec=pltpu.PrefetchScalarGridSpec(
            num_scalar_prefetch=1,
            grid=(1,),
            in_specs=[whole, whole, state, state, state],
            out_specs=[pl.BlockSpec((rows, cols), lambda s, pick: (0, 0)), whole],
        ),
        out_shape=[jax.ShapeDtypeStruct((rows, cols), BF16), jax.ShapeDtypeStruct(keep.shape, BF16)],
        compiler_params=params(),
        cost_estimate=cost(rows * cols, 24 * rows * cols),
    )(pick, keep, came, master, moment1, moment2)


def adam_all_body(pick, grad_ref, master_ref, m1_ref, m2_ref, out_ref, out1_ref, out2_ref):
    out_ref[...], out1_ref[...], out2_ref[...] = adam(
        grad_ref[0].astype(F32), master_ref[...], m1_ref[...], m2_ref[...]
    )


def adam_all(grads, master, moment1, moment2, pick):
    n, rows, cols = grads.shape
    state = pl.BlockSpec((rows, cols), lambda s, pick: (0, pick[s]))
    return pl.pallas_call(
        adam_all_body,
        grid_spec=pltpu.PrefetchScalarGridSpec(
            num_scalar_prefetch=1,
            grid=(n,),
            in_specs=[pl.BlockSpec((1, rows, cols), lambda s, pick: (s, 0, 0)), state, state, state],
            out_specs=[state] * 3,
        ),
        out_shape=[jax.ShapeDtypeStruct(master.shape, F32)] * 3,
        compiler_params=params(),
        cost_estimate=cost(n * rows * cols, 26 * n * rows * cols),
    )(pick, grads, master, moment1, moment2)


def assemble_body(pick, p_place, q_place, *refs):
    p_ref, q_ref, out_ref = refs[0], refs[1], refs[-1]
    _, n_inner, part, _ = p_ref.shape
    for r in range(n_inner):
        at = pl.multiple_of(p_place[r] * (2 * part), 2 * part)
        out_ref[pl.ds(at, part), :] = p_ref[0, r]
        at = pl.multiple_of(q_place[r] * (2 * part) + part, part)
        out_ref[pl.ds(at, part), :] = q_ref[0, r]


def assemble(p, q, pick, p_place, q_place, d, width, before):
    n, n_inner, part, cols = p.shape
    piece = pl.BlockSpec((1, n_inner, part, cols), lambda s, *_: (s, 0, 0, 0))
    in_specs = [piece, piece]
    args = [p, q]
    aliases = {}
    if before is not None:
        in_specs.append(pl.BlockSpec(memory_space=pl.ANY))
        args.append(before)
        aliases = {5: 0}
    return pl.pallas_call(
        assemble_body,
        grid_spec=pltpu.PrefetchScalarGridSpec(
            num_scalar_prefetch=3,
            grid=(n,),
            in_specs=in_specs,
            out_specs=pl.BlockSpec((d, cols), lambda s, pick, *_: (0, pick[s])),
        ),
        out_shape=jax.ShapeDtypeStruct((d, width), BF16),
        input_output_aliases=aliases,
        compiler_params=params(),
        cost_estimate=cost(0, 4 * n * d * cols),
    )(pick, p_place, q_place, *args)


def swap(x, axis, bit):
    n = lax.axis_size(axis)
    return lax.ppermute(x, axis, [(i, i ^ (1 << bit)) for i in range(n)])


def bit_of(axis, bit):
    return (lax.axis_index(axis) >> bit) & 1


def bits(axis):
    return (lax.axis_size(axis) - 1).bit_length()


def scan_states(own, oth_sent, reverse):
    side = 0 if reverse else 1
    mine = bit_of("inner", 0) == side
    came = swap(oth_sent, "inner", 0).astype(F32)
    total = own + came
    outside = jnp.zeros_like(own)
    levels = [("inner", b) for b in range(1, bits("inner"))] + [("outer", b) for b in range(bits("outer"))]
    for n, (axis, bit) in enumerate(levels):
        got = swap(total.astype(BF16), axis, bit).astype(F32)
        outside = outside + jnp.where(bit_of(axis, bit) == side, got, 0.0)
        if n + 1 < len(levels):
            total = total + got
    give = (outside + jnp.where(mine, 0.0, own)).astype(BF16)
    back = swap(give, "inner", 0)
    return (outside + jnp.where(mine, came, 0.0)).astype(BF16), back


def reversed_bits(value, n_bits):
    out = 0
    for b in range(n_bits):
        out = out | (((value >> b) & 1) << (n_bits - 1 - b))
    return out


def fold(x, axis_at, axis, bit):
    size = x.shape[axis_at] // 2
    keep = lax.slice_in_dim(x, 0, size, axis=axis_at)
    got = swap(lax.slice_in_dim(x, size, 2 * size, axis=axis_at).astype(BF16), axis, bit)
    return keep.astype(F32) + got.astype(F32)


def local(inputs, queries, keys, values, out_grad, master, moment1, moment2):
    rows_here, width = queries.shape
    d = inputs.shape[1]
    n_outer = lax.axis_size("outer")
    n_inner = lax.axis_size("inner")
    o_bits, i_bits = bits("outer"), bits("inner")
    total_tokens = rows_here * n_outer * n_inner
    att_scale = 1.0 / math.sqrt(HD * total_tokens)
    grad_scale = 1.0 / math.sqrt(total_tokens)
    outer, inner = lax.axis_index("outer"), lax.axis_index("inner")
    y = bit_of("inner", 0)
    half = jnp.reshape(y, (1,)).astype(jnp.int32)
    pairs = width // PAIR
    own_pairs = (jnp.arange(pairs // 2) + y * (pairs // 2)).astype(jnp.int32)
    oth_pairs = (jnp.arange(pairs // 2) + (1 - y) * (pairs // 2)).astype(jnp.int32)

    qg_sent = states(out_grad, queries, oth_pairs, BF16)
    qg_own = states(out_grad, queries, own_pairs, F32)
    qg_mine, qg_other = scan_states(qg_own, qg_sent, True)

    inside = key_inside(out_grad, queries, values, att_scale)
    position = reversed_bits(jnp.arange(n_inner) ^ inner, i_bits).astype(jnp.int32)
    turned = turned_inputs(inputs, position)

    rel = jnp.arange(n_outer // 2, dtype=jnp.int32) * 2
    far = ((rel + 1) ^ outer).astype(jnp.int32)
    near = (rel ^ outer).astype(jnp.int32)
    ends = (half, att_scale, grad_scale, n_inner, n_outer)
    key_grad, p_far, q_far = key_product(inside, values, qg_mine, qg_other, turned, far, *ends, None)
    key_grad, p_near, q_near = key_product(inside, values, qg_mine, qg_other, turned, near, *ends, key_grad)

    p = p_near.astype(F32) + swap(p_far, "outer", 0).astype(F32)
    q = q_near.astype(F32) + swap(q_far, "outer", 0).astype(F32)
    for b in reversed(range(1, o_bits)):
        p = fold(p, 0, "outer", b)
    p = fold(p, 1, "inner", 0)
    q = fold(q, 1, "inner", 0)
    for b in reversed(range(1, o_bits)):
        q = fold(q, 0, "outer", b)
    both = jnp.stack([p[0], q[0]], 0)
    for b in range(1, i_bits - 1):
        both = fold(both, 1, "inner", b)
    keep = both[:, 0]
    came = swap(both[:, 1].astype(BF16), "inner", i_bits - 1)
    mine = jnp.reshape(outer, (1,)).astype(jnp.int32)
    grad, weight = adam_own(keep, came, master, moment1, moment2, mine)

    both = weight[:, None]
    for b in reversed(range(1, i_bits)):
        both = jnp.concatenate([both, swap(both, "inner", b)], 1)
    p, q = both[0][None], both[1][None]
    p = jnp.concatenate([p, swap(p, "inner", 0)], 1)
    for b in range(1, o_bits):
        p = jnp.concatenate([p, swap(p, "outer", b)], 0)
        q = jnp.concatenate([q, swap(q, "outer", b)], 0)
    q = jnp.concatenate([q, swap(q, "inner", 0)], 1)
    p_more, q_more = swap(p, "outer", 0), swap(q, "outer", 0)
    place = (reversed_bits(jnp.arange(n_inner), i_bits) ^ inner).astype(jnp.int32)
    weights = assemble(p, q, near, place, place, d, width, None)
    weights = assemble(p_more, q_more, far, place, place, d, width, weights)

    grads = grad[None]
    for b in range(1, o_bits):
        grads = jnp.concatenate([grads, swap(grads, "outer", b)], 0)
    grads = jnp.concatenate([grads, swap(grads, "outer", 0)], 0)
    new_master, new_moment1, new_moment2 = adam_all(
        grads, master, moment1, moment2, jnp.concatenate([near, far], 0)
    )

    kv_sent = states(values, keys, oth_pairs, BF16)
    kv_own = states(values, keys, own_pairs, F32)
    kv_mine, kv_other = scan_states(kv_own, kv_sent, False)
    query_grad = query_side(out_grad, keys, values, kv_mine, kv_other, half, att_scale)
    return (query_grad, key_grad, new_master, new_moment1, new_moment2, weights)


def solution(mesh):
    tokens = P(("outer", "inner"), None)
    rows = P("inner", None)
    return jax.shard_map(
        local,
        mesh=mesh,
        in_specs=(tokens,) * 5 + (rows,) * 3,
        out_specs=(tokens, tokens, rows, rows, rows, P()),
        check_vma=False,
    )
```

```python
import functools
import math

import jax
import jax.numpy as jnp
from jax import lax
from jax.experimental import pallas as pl
from jax.experimental.pallas import tpu as pltpu
from jax.sharding import PartitionSpec as P

HD = 128
SUB = 256
PAIR = 2 * HD
VMEM = 16 * 1024 * 1024
F32 = jnp.float32
BF16 = jnp.bfloat16
WHOLE = pl.BlockSpec(memory_space=pltpu.VMEM)
HBM = pl.BlockSpec(memory_space=pltpu.HBM)


def mm(a, b, contract):
    return lax.dot_general(a, b, ((contract[:1], contract[1:]), ((), ())), preferred_element_type=F32)


def far(x):
    return pltpu.with_memory_space_constraint(x, pltpu.HBM)


def call(body, args, specs, outs, macs=0, moved=0, scratch=(), aliases=None):
    args = [far(a) if spec is HBM else a for a, spec in zip(args, specs)]
    return pl.pallas_call(
        body,
        in_specs=specs,
        out_specs=[WHOLE if near else HBM for _, _, near in outs],
        out_shape=[(jax.ShapeDtypeStruct if near else pltpu.HBM)(shape, dtype) for shape, dtype, near in outs],
        scratch_shapes=list(scratch),
        input_output_aliases=aliases or {},
        compiler_params=pltpu.CompilerParams(vmem_limit_bytes=VMEM),
        cost_estimate=pl.CostEstimate(flops=2 * macs, bytes_accessed=moved, transcendentals=0),
    )(*args)


def dma(n):
    return pltpu.SemaphoreType.DMA((n,))


def tie(x, *after):
    return lax.optimization_barrier((x, *after))[0] if after else x


class Here:
    def __init__(self, n_outer, n_inner):
        self.i_bits, self.o_bits = (n_inner - 1).bit_length(), (n_outer - 1).bit_length()
        self.n_outer, self.n_inner = n_outer, n_inner

    def group(self, k):
        return lax.axis_index("outer") ^ k

    def block(self, p):
        return lax.axis_index("inner") ^ reversed_bits(p, self.i_bits)

    def position(self, block):
        return reversed_bits(lax.axis_index("inner") ^ block, self.i_bits)

    def bit(self, axis, b):
        return (lax.axis_index(axis) >> b) & 1

    def y(self):
        return self.bit("inner", 0)


def states_body(at, a_hbm, b_hbm, out_ref, a_buf, b_buf, a_sem, b_sem):
    chunks, rows, cols = a_buf.shape
    at = pl.multiple_of((1 - at.y()) * cols, cols)
    copies = []
    for c in range(chunks):
        here = (pl.ds(c * rows, rows), pl.ds(at, cols))
        pair = (
            pltpu.make_async_copy(a_hbm.at[here], a_buf.at[c], a_sem.at[c]),
            pltpu.make_async_copy(b_hbm.at[here], b_buf.at[c], b_sem.at[c]),
        )
        for copy in pair:
            copy.start()
        copies.append(pair)
    sums = [None] * (cols // HD)
    for c in range(chunks):
        for copy in copies[c]:
            copy.wait()
        for j in range(cols // HD):
            here = slice(j * HD, (j + 1) * HD)
            term = mm(a_buf[c, :, here], b_buf[c, :, here], (0, 0))
            sums[j] = term if c == 0 else sums[j] + term
    for j in range(cols // HD):
        out_ref[j] = sums[j].astype(out_ref.dtype)


def states(a, b, at, dtype):
    rows, width = a.shape
    cols = width // 2
    chunks = rows // SUB
    buf = pltpu.VMEM((chunks, SUB, cols), BF16)
    return call(
        functools.partial(states_body, at),
        [a, b],
        [HBM, HBM],
        [((cols // HD, HD, HD), dtype, True)],
        rows * cols * HD,
        4 * rows * cols,
        [buf, buf, dma(chunks), dma(chunks)],
    )[0]


def sums_of(a_ref, b_ref, at, cols, blocks, wait):
    sums = [None] * (cols // HD)
    for b in blocks:
        wait(b)
        for j in range(cols // HD):
            here = (pl.ds(b * SUB, SUB), pl.ds(pl.multiple_of(at * cols + j * HD, HD), HD))
            term = mm(a_ref[here], b_ref[here], (0, 0))
            sums[j] = term if sums[j] is None else sums[j] + term
    return sums


def load_body(n_load, at, *refs):
    sources, out_ref, loads, sem = refs[:n_load], refs[n_load], refs[n_load + 1 : -1], refs[-1]
    rows, width = sources[0].shape
    blocks = rows // SUB
    copies = []
    for b in range(blocks):
        copies.append([])
        for n in range(n_load):
            here = pl.ds(b * SUB, SUB)
            copy = pltpu.make_async_copy(sources[n].at[here, :], loads[n].at[here, :], sem.at[n_load * b + n])
            copy.start()
            copies[b].append(copy)

    def wait(b):
        for copy in copies[b]:
            copy.wait()

    for j, total in enumerate(sums_of(loads[0], loads[1], at.y(), width // 2, range(blocks), wait)):
        out_ref[j] = total


def load(sources, at):
    rows, width = sources[0].shape
    n = len(sources)
    return call(
        functools.partial(load_body, n, at),
        sources,
        [HBM] * n,
        [((width // 2 // HD, HD, HD), F32, True)] + [((rows, width), BF16, True)] * n,
        rows * width // 2 * HD,
        4 * n * rows * width,
        [dma(n * (rows // SUB))],
    )


def both_states_body(at, a_ref, b_hbm, sent_ref, own_ref, b_ref, sem):
    rows, width = a_ref.shape
    blocks = rows // SUB
    copies = []
    for b in range(blocks):
        here = pl.ds(b * SUB, SUB)
        copies.append(pltpu.make_async_copy(b_hbm.at[here, :], b_ref.at[here, :], sem.at[b]))
        copies[b].start()
    for side, ref in ((1 - at.y(), sent_ref), (at.y(), own_ref)):
        wait = (lambda b: copies[b].wait()) if ref is sent_ref else (lambda b: None)
        for j, total in enumerate(sums_of(a_ref, b_ref, side, width // 2, range(blocks), wait)):
            ref[j] = total.astype(ref.dtype)


def both_states(a, b, at):
    rows, width = a.shape
    shape = (width // 2 // HD, HD, HD)
    return call(
        functools.partial(both_states_body, at),
        [a, b],
        [WHOLE, HBM],
        [(shape, BF16, True), (shape, F32, True)],
        rows * width * HD,
        2 * rows * width,
        [pltpu.VMEM((rows, width), BF16), dma(rows // SUB)],
    )


def key_inside_body(scale, picks, here_at, g_ref, q_ref, v_ref, out_ref):
    n = len(picks)
    rows, cols = out_ref.shape[0], out_ref.shape[1] // n
    later = lax.broadcasted_iota(jnp.int32, (SUB, SUB), 1) >= lax.broadcasted_iota(jnp.int32, (SUB, SUB), 0)
    for s in range(n):
        for j in range(cols // HD):
            at = pl.ds(pl.multiple_of(here_at.group(picks[s]) * cols + j * HD, HD), HD)
            to = s * cols + j * HD
            state = None
            for b in reversed(range(rows // SUB)):
                here = (pl.ds(b * SUB, SUB), at)
                g, q, v = g_ref[here], q_ref[here], v_ref[here]
                scores = jnp.where(later, mm(v, g, (1, 1)), 0.0).astype(BF16)
                total = mm(scores, q, (1, 0))
                if state is not None:
                    total = total + mm(v, state.astype(BF16), (1, 0))
                out_ref[b * SUB : (b + 1) * SUB, to : to + HD] = total * scale
                if b:
                    term = mm(g, q, (0, 0))
                    state = term if state is None else state + term


def key_inside(g, q, v, at, picks, scale, cols):
    rows = g.shape[0]
    n = len(picks)
    return call(
        functools.partial(key_inside_body, scale, picks, at),
        [g, q, v],
        [WHOLE] * 3,
        [((rows, n * cols), F32, True)],
        rows * n * cols * (2 * SUB + 2 * HD),
        10 * rows * n * cols,
    )[0]


def head_of(ref_own, ref_oth, other, at):
    return jnp.where(other, ref_oth[at], ref_own[at])


def query_body(scale, first, count, at, g_ref, k_ref, v_ref, own_ref, oth_ref, *refs):
    out_hbm, buf, sem = refs[-3:]
    rows = g_ref.shape[0]
    heads_half = own_ref.shape[0]
    earlier = lax.broadcasted_iota(jnp.int32, (SUB, SUB), 0) >= lax.broadcasted_iota(jnp.int32, (SUB, SUB), 1)
    copies = []
    for n in range(count):
        for j in range(2):
            head = (first + n) * 2 + j
            cols = slice(head * HD, (head + 1) * HD)
            other = jnp.int32(head // heads_half) != at.y()
            state = head_of(own_ref, oth_ref, other, head % heads_half).astype(F32)
            for b in range(rows // SUB):
                here = slice(b * SUB, (b + 1) * SUB)
                g, k, v = g_ref[here, cols], k_ref[here, cols], v_ref[here, cols]
                scores = jnp.where(earlier, mm(g, v, (1, 1)), 0.0).astype(BF16)
                total = mm(scores, k, (1, 0)) + mm(g, state.astype(BF16), (1, 0))
                buf[n, here, j * HD : (j + 1) * HD] = (total * scale).astype(BF16)
                if b + 1 < rows // SUB:
                    state = state + mm(v, k, (0, 0))
        copy = pltpu.make_async_copy(buf.at[n], out_hbm.at[:, pl.ds((first + n) * PAIR, PAIR)], sem.at[n])
        copy.start()
        copies.append(copy)
    for copy in copies:
        copy.wait()


def query_side(g, k, v, own, oth, at, scale, first, count, before):
    rows, width = g.shape
    more = [] if before is None else [before]
    return call(
        functools.partial(query_body, scale, first, count, at),
        [g, k, v, own, oth] + more,
        [WHOLE] * 5 + [HBM] * len(more),
        [((rows, width), BF16, False)],
        rows * count * PAIR * (2 * SUB + 2 * HD),
        8 * rows * count * PAIR,
        [pltpu.VMEM((count, rows, PAIR), BF16), dma(count)],
        {5: 0} if more else None,
    )[0]


def turned_body(here_at, in_hbm, out_ref, buf, sem):
    size = out_ref.shape[0] // here_at.n_inner
    cols = max(size, HD)
    copies = []
    for n in range(out_ref.shape[0] // cols):
        copy = pltpu.make_async_copy(in_hbm.at[:, pl.ds(n * cols, cols)], buf.at[n], sem.at[n])
        copy.start()
        copies.append(copy)
    for n, copy in enumerate(copies):
        copy.wait()
        turned = buf[n].T
        for j in range(cols // size):
            at = pl.multiple_of(here_at.position(n * (cols // size) + j) * size, size)
            out_ref[pl.ds(at, size), :] = turned[j * size : (j + 1) * size, :]


def turned_inputs(inputs, at):
    rows, width = inputs.shape
    cols = max(width // at.n_inner, HD)
    return call(
        functools.partial(turned_body, at),
        [inputs],
        [HBM],
        [((width, rows), BF16, True)],
        0,
        4 * rows * width,
        [pltpu.VMEM((width // cols, rows, cols), BF16), dma(width // cols)],
    )[0]


def key_product_body(scale, grad_scale, n_inner, picks, here_at, *refs):
    inside_ref, v_ref, own_ref, oth_ref, turned_ref = refs[:5]
    key_hbm, p_ref, q_ref, buf, sem = refs[-5:]
    n = len(picks)
    heads_half = own_ref.shape[0]
    cols = inside_ref.shape[1] // n
    heads = cols // HD
    copies = []
    for s in range(n):
        group = here_at.group(picks[s])
        for j in range(heads):
            here = slice(s * cols + j * HD, s * cols + (j + 1) * HD)
            head = group * heads + j
            other = (head // heads_half) != here_at.y()
            state = head_of(own_ref, oth_ref, other, lax.rem(head, heads_half))
            part = mm(v_ref[:, pl.ds(pl.multiple_of(head * HD, HD), HD)], state, (1, 0))
            buf[s, :, j * HD : (j + 1) * HD] = (inside_ref[:, here] + part * scale).astype(BF16)
        at = pl.ds(pl.multiple_of(group * cols, cols), cols)
        copy = pltpu.make_async_copy(buf.at[s], key_hbm.at[:, at], sem.at[s])
        copy.start()
        copies.append(copy)
    for s in range(n):
        product = (mm(turned_ref[...], buf[s], (1, 0)) * grad_scale).astype(BF16)
        size = product.shape[0] // n_inner
        for r in range(n_inner):
            p_ref[s, r] = product[r * size : r * size + size // 2]
            q_ref[s, r] = product[r * size + size // 2 : (r + 1) * size]
    for copy in copies:
        copy.wait()


def key_product(inside, v, own, oth, turned, picks, at, scale, grad_scale, n_inner, before):
    n = len(picks)
    rows, width = v.shape
    cols = inside.shape[1] // n
    d = turned.shape[0]
    piece = ((n, n_inner, d // n_inner // 2, cols), BF16, True)
    more = [] if before is None else [before]
    return call(
        functools.partial(key_product_body, scale, grad_scale, n_inner, picks, at),
        [inside, v, own, oth, turned] + more,
        [WHOLE] * 5 + [HBM] * len(more),
        [((rows, width), BF16, False), piece, piece],
        n * cols * rows * (d + HD),
        2 * rows * (d + 4 * n * cols),
        [pltpu.VMEM((n, rows, cols), BF16), dma(n)],
        {5: 0} if more else None,
    )


def adam(grad, master, moment1, moment2):
    new_moment1 = 0.9 * moment1 + 0.1 * grad
    new_moment2 = 0.95 * moment2 + 0.05 * grad * grad
    new_master = master - 0.01 * (new_moment1 / (jnp.sqrt(new_moment2) + 1e-08) + 0.1 * master)
    return new_master, new_moment1, new_moment2


def adam_own_body(at, keep_ref, came_ref, master_ref, m1_ref, m2_ref, grad_ref, weight_ref):
    _, _, part, size = keep_ref.shape
    cols = pl.ds(pl.multiple_of(at.group(0) * size, size), size)
    for j in range(2):
        here = slice(j * part, (j + 1) * part)
        grad = (keep_ref[j, 0] + came_ref[j, 0].astype(F32)).astype(BF16)
        grad_ref[here, :] = grad
        new_master, _, _ = adam(grad.astype(F32), master_ref[here, cols], m1_ref[here, cols], m2_ref[here, cols])
        weight_ref[j, 0] = new_master.astype(BF16)


def adam_own(keep, came, master, moment1, moment2, at):
    _, _, part, cols = keep.shape
    return call(
        functools.partial(adam_own_body, at),
        [keep, came, master, moment1, moment2],
        [WHOLE] * 5,
        [((2 * part, cols), BF16, True), (keep.shape, BF16, True)],
        2 * part * cols,
        48 * part * cols,
    )


def adam_all_body(picks, at, *refs):
    n = len(picks)
    grads, (master_ref, m1_ref, m2_ref) = refs[:n], refs[n : n + 3]
    outs, bufs, sem = refs[n + 3 : n + 6], refs[n + 6 : n + 9], refs[n + 9]
    size = grads[0].shape[1]
    copies = []
    for s in range(n):
        cols = pl.ds(pl.multiple_of(at.group(picks[s]) * size, size), size)
        new = adam(grads[s][...].astype(F32), master_ref[:, cols], m1_ref[:, cols], m2_ref[:, cols])
        for i in range(3):
            bufs[i][s] = new[i]
            copy = pltpu.make_async_copy(bufs[i].at[s], outs[i].at[:, cols], sem.at[s * 3 + i])
            copy.start()
            copies.append(copy)
    for copy in copies:
        copy.wait()


def adam_all(grads, master, moment1, moment2, at, picks):
    n = len(grads)
    rows, cols = grads[0].shape
    return call(
        functools.partial(adam_all_body, picks, at),
        [*grads, master, moment1, moment2],
        [WHOLE] * (n + 3),
        [(master.shape, F32, False)] * 3,
        n * rows * cols,
        26 * n * rows * cols,
        [pltpu.VMEM((n, rows, cols), F32)] * 3 + [dma(3 * n)],
    )


def assemble_body(kinds, at, *refs):
    n = len(kinds)
    pieces, bufs = refs[:n], refs[-n - 1 : -1]
    out_hbm, sem = refs[-n - 2], refs[-1]
    copies = []
    for i, (which, groups, start, count) in enumerate(kinds):
        size = pieces[i].shape[-1]
        for s, k in enumerate(groups):
            cols = pl.ds(pl.multiple_of(at.group(k) * size, size), size)
            for r in range(count):
                block = at.block(start + r)
                if which:
                    bufs[i][s, block // 2] = pieces[i][s, r]
                else:
                    bufs[i][s, block // 2, block % 2] = pieces[i][s, r]
            if which:
                goal = out_hbm.at[:, at.block(start) % 2, which, :, cols]
            else:
                goal = out_hbm.at[:, :, which, :, cols]
            copy = pltpu.make_async_copy(bufs[i].at[s], goal, sem.at[2 * i + s])
            copy.start()
            copies.append(copy)
    for copy in copies:
        copy.wait()


def assemble(pieces, at, before, width):
    n_inner = at.n_inner
    part, cols = pieces[0][0].shape[2:]
    kinds = [kind for _, kind in pieces]
    bufs = [
        pltpu.VMEM((len(groups), n_inner // 2) + (() if which else (2,)) + (part, cols), BF16)
        for which, groups, _, _ in kinds
    ]
    more = [] if before is None else [before]
    return call(
        functools.partial(assemble_body, kinds, at),
        [array for array, _ in pieces] + more,
        [WHOLE] * len(pieces) + [HBM] * len(more),
        [((n_inner // 2, 2, 2, part, width), BF16, False)],
        0,
        4 * sum(array.size for array, _ in pieces),
        bufs + [dma(2 * len(pieces))],
        {len(pieces): 0} if more else None,
    )[0]


def swap(x, axis, bit):
    n = lax.axis_size(axis)
    return lax.ppermute(x, axis, [(i, i ^ (1 << bit)) for i in range(n)])


def reversed_bits(value, n_bits):
    out = 0
    for b in range(n_bits):
        out = out | (((value >> b) & 1) << (n_bits - 1 - b))
    return out


def step_body(level, side, at, total_ref, got_ref, *refs):
    total_out, send_out, outside_out = refs[-3:]
    got = got_ref[...].astype(F32)
    total = total_ref[...] + got
    total_out[...] = total
    send_out[...] = total.astype(BF16)
    if level is None:
        outside_out[...] = jnp.zeros_like(got)
    else:
        outside_out[...] = refs[0][...] + jnp.where(at.bit(*level) == side, got, 0.0)


def step(level, side, at, total, got, *outside):
    outs = [(total.shape, F32, True), (total.shape, BF16, True), (total.shape, F32, True)]
    body = functools.partial(step_body, level, side, at)
    return call(body, [total, got, *outside], [WHOLE] * (2 + len(outside)), outs)


def last_body(level, side, at, outside_ref, got_ref, own_ref, came_ref, give_out, out):
    outside = outside_ref[...] + jnp.where(at.bit(*level) == side, got_ref[...].astype(F32), 0.0)
    mine = at.y() == side
    give_out[...] = (outside + jnp.where(mine, 0.0, own_ref[...])).astype(BF16)
    out[...] = (outside + jnp.where(mine, came_ref[...].astype(F32), 0.0)).astype(BF16)


def last(level, side, at, outside, got, own, came):
    outs = [(own.shape, BF16, True)] * 2
    return call(functools.partial(last_body, level, side, at), [outside, got, own, came], [WHOLE] * 4, outs)


def scan_states(own, sent, reverse, at):
    side = 0 if reverse else 1
    came = swap(sent, "inner", 0)
    after = yield came
    own = own()
    total, send, outside = step(None, side, at, own, came)
    levels = [("inner", b) for b in range(1, at.i_bits)] + [("outer", b) for b in range(at.o_bits)]
    for n, level in enumerate(levels):
        got = swap(tie(send, *after), *level)
        after = yield got
        if n + 1 < len(levels):
            total, send, outside = step(level, side, at, total, got, outside)
    give, kept = last(levels[-1], side, at, outside, got, own, came)
    back = swap(tie(give, *after), "inner", 0)
    yield kept, back


def fold(keep, got, axis):
    size = keep.shape[axis] // 2
    low, high = [
        lax.slice_in_dim(keep, at, at + size, axis=axis).astype(F32)
        + lax.slice_in_dim(got, at, at + size, axis=axis).astype(F32)
        for at in (0, size)
    ]
    return high.astype(BF16), low


def merge(p_keep, p_got, q_keep, q_got):
    (p_send, p), (q_send, q) = fold(p_keep, p_got, 1), fold(q_keep, q_got, 1)
    return jnp.concatenate([p_send, q_send], 0), jnp.concatenate([p, q], 0)


def join_body(axis, a_ref, b_ref, out):
    size = a_ref.shape[axis]
    for side, ref in enumerate((a_ref, b_ref)):
        at = tuple(pl.ds(side * size, size) if a == axis else slice(None) for a in range(len(ref.shape)))
        out[at] = ref[...]


def join(a, b, axis):
    shape = tuple(2 * s if i == axis else s for i, s in enumerate(a.shape))
    return call(functools.partial(join_body, axis), [a, b], [WHOLE] * 2, [(shape, BF16, True)])[0]


def split_body(a_ref, b_ref, p_out, q_out):
    n = a_ref.shape[1]
    for i, out in enumerate((p_out, q_out)):
        out[:, :n] = a_ref[i : i + 1]
        out[:, n:] = b_ref[i : i + 1]


def split(a, b):
    _, n, part, cols = a.shape
    return call(split_body, [a, b], [WHOLE] * 2, [((1, 2 * n, part, cols), BF16, True)] * 2)


def local(inputs, queries, keys, values, out_grad, master, moment1, moment2):
    rows_here, width = queries.shape
    d = inputs.shape[1]
    n_outer = lax.axis_size("outer")
    n_inner = lax.axis_size("inner")
    at = Here(n_outer, n_inner)
    i_bits = at.i_bits
    assert n_outer == 4 and i_bits >= 2
    total_tokens = rows_here * n_outer * n_inner
    att_scale = 1.0 / math.sqrt(HD * total_tokens)
    grad_scale = 1.0 / math.sqrt(total_tokens)
    cols = width // n_outer
    near, far_ = tuple(range(0, n_outer, 2)), tuple(range(1, n_outer, 2))

    qg_sent = states(out_grad, queries, at, BF16)
    loaded = []

    def own_states():
        loaded.extend(load([out_grad, queries, values], at))
        return loaded[0]

    qg = scan_states(own_states, qg_sent, True, at)
    next(qg)
    qg.send([])
    g, q, v = loaded[1:]
    inside_far = key_inside(g, q, v, at, far_, att_scale, cols)
    done = [inside_far]
    turned = inside_near = None
    for _ in range(2, i_bits):
        qg.send(done)
        done = []
        if turned is None:
            inside_near = key_inside(tie(g, inside_far), q, v, at, near, att_scale, cols)
            turned = turned_inputs(tie(inputs, inside_far), at)
            done = [inside_near, turned]
    qg.send(done)
    qg.send([])
    kv_sent, kv_own = both_states(tie(v, inside_near, turned), keys, at)
    qg_mine, qg_other = qg.send([kv_own])
    kv = scan_states(lambda: kv_own, kv_sent, False, at)
    kv_got = next(kv)
    kv_stages = i_bits + 2

    def kv_next(*after):
        nonlocal kv_stages, kv_got
        if kv_stages:
            kv_stages -= 1
            kv_got = kv.send(list(after))
        return kv_got

    ends = (at, att_scale, grad_scale, n_inner)
    key_grad, p_far, q_far = key_product(inside_far, v, qg_mine, qg_other, turned, far_, *ends, None)
    p_got, q_got = swap(p_far, "outer", 0), swap(q_far, "outer", 0)
    key_grad, p, q = key_product(inside_near, v, qg_mine, qg_other, turned, near, *ends, key_grad)

    p_send, p = fold(p, p_got, 0)
    q_send, q = fold(q, q_got, 1)
    p_got, q_got = swap(p_send, "outer", 1), swap(q_send, "inner", 0)
    kv_next(p_send, q_send)
    p_send, p = fold(p, p_got, 1)
    q_send, q = fold(q, q_got, 0)
    p_got, q_got = swap(p_send, "inner", 0), swap(q_send, "outer", 1)
    kv_next(p_send, q_send)
    send, keep = merge(p, p_got, q, q_got)
    for b in range(1, i_bits):
        got = swap(send, "inner", b)
        if b + 1 < i_bits:
            send, keep = fold(keep, got, 1)
            kv_next(send)
    while kv_stages > 1:
        kv_next(send)
    grad, weight = adam_own(keep, got, master, moment1, moment2, at)
    kv_mine, kv_other = kv_next(weight)

    query_grad = None
    pair = 0

    def query_next(count, after):
        nonlocal query_grad, pair
        if pair < width // PAIR:
            args = (tie(kv_mine, after), kv_other, at, att_scale, pair, min(count, width // PAIR - pair))
            query_grad = query_side(out_grad, keys, values, *args, query_grad)
            pair += count
        return query_grad

    for b in reversed(range(1, i_bits)):
        got = swap(weight, "inner", b)
        if b == i_bits - 1:
            grad_x = swap(grad, "outer", 1)
        if b > 1:
            weight = join(weight, got, 1)
    p, q = split(weight, got)
    p_got, q_got = swap(p, "inner", 0), swap(q, "outer", 1)
    grads = [grad, swap(grad, "outer", 0), grad_x, swap(grad_x, "outer", 0)]
    p, q = join(p, p_got, 1), join(q, q_got, 0)
    p_last, q_last = swap(p, "outer", 1), swap(q, "inner", 0)
    p_core, q_core = swap(p, "outer", 0), swap(q, "outer", 0)
    query_next(2, p)
    query_next(2, p)
    new_master, new_moment1, new_moment2 = adam_all(
        [tie(grads[0], p, q)] + grads[1:], master, moment1, moment2, at, (0, 1, 2, 3)
    )
    n = n_inner // 2
    weights = assemble(
        [(p, (0, (0,), 0, 2 * n)), (q, (1, (0, 2), 0, n)), (p_core, (0, (1,), 0, 2 * n)), (q_core, (1, (1, 3), 0, n))],
        at, None, width,
    )
    done = [weights, query_grad, new_master]
    p_core, q_core = swap(tie(p_last, *done), "outer", 0), swap(tie(q_last, *done), "outer", 0)
    weights = assemble([(p_last, (0, (2,), 0, 2 * n)), (q_last, (1, (0, 2), n, n))], at, weights, width)
    weights = assemble([(p_core, (0, (3,), 0, 2 * n)), (q_core, (1, (1, 3), n, n))], at, weights, width)
    return (query_grad, key_grad, new_master, new_moment1, new_moment2, weights.reshape(d, width))


def solution(mesh):
    tokens = P(("outer", "inner"), None)
    rows = P("inner", None)
    return jax.shard_map(
        local,
        mesh=mesh,
        in_specs=(tokens,) * 5 + (rows,) * 3,
        out_specs=(tokens, tokens, rows, rows, rows, P()),
        check_vma=False,
    )
```

```python
import functools
import math

import jax
import jax.numpy as jnp
from jax import lax
from jax.experimental import pallas as pl
from jax.experimental.pallas import tpu as pltpu
from jax.sharding import PartitionSpec as P

HD = 128
SUB = 256
PAIR = 2 * HD
VMEM = 16 * 1024 * 1024
F32 = jnp.float32
BF16 = jnp.bfloat16
WHOLE = pl.BlockSpec(memory_space=pltpu.VMEM)
HBM = pl.BlockSpec(memory_space=pltpu.HBM)


def mm(a, b, contract):
    return lax.dot_general(a, b, ((contract[:1], contract[1:]), ((), ())), preferred_element_type=F32)


def far(x):
    return pltpu.with_memory_space_constraint(x, pltpu.HBM)


def call(body, args, specs, outs, macs=0, moved=0, scratch=(), aliases=None):
    args = [far(a) if spec is HBM else a for a, spec in zip(args, specs)]
    return pl.pallas_call(
        body,
        in_specs=specs,
        out_specs=[WHOLE if near else HBM for _, _, near in outs],
        out_shape=[(jax.ShapeDtypeStruct if near else pltpu.HBM)(shape, dtype) for shape, dtype, near in outs],
        scratch_shapes=list(scratch),
        input_output_aliases=aliases or {},
        compiler_params=pltpu.CompilerParams(vmem_limit_bytes=VMEM),
        cost_estimate=pl.CostEstimate(flops=2 * macs, bytes_accessed=moved, transcendentals=0),
    )(*args)


def dma(n):
    return pltpu.SemaphoreType.DMA((n,))


def tie(x, *after):
    return lax.optimization_barrier((x, *after))[0] if after else x


class Here:
    def __init__(self, n_outer, n_inner):
        self.i_bits, self.o_bits = (n_inner - 1).bit_length(), (n_outer - 1).bit_length()
        self.n_outer, self.n_inner = n_outer, n_inner

    def group(self, k):
        return lax.axis_index("outer") ^ k

    def block(self, p):
        return lax.axis_index("inner") ^ reversed_bits(p, self.i_bits)

    def position(self, block):
        return reversed_bits(lax.axis_index("inner") ^ block, self.i_bits)

    def bit(self, axis, b):
        return (lax.axis_index(axis) >> b) & 1

    def y(self):
        return self.bit("inner", 0)


def states_body(at, a_hbm, b_hbm, out_ref, a_buf, b_buf, a_sem, b_sem):
    chunks, rows, cols = a_buf.shape
    at = pl.multiple_of((1 - at.y()) * cols, cols)
    copies = []
    for c in range(chunks):
        here = (pl.ds(c * rows, rows), pl.ds(at, cols))
        pair = (
            pltpu.make_async_copy(a_hbm.at[here], a_buf.at[c], a_sem.at[c]),
            pltpu.make_async_copy(b_hbm.at[here], b_buf.at[c], b_sem.at[c]),
        )
        for copy in pair:
            copy.start()
        copies.append(pair)
    sums = [None] * (cols // HD)
    for c in range(chunks):
        for copy in copies[c]:
            copy.wait()
        for j in range(cols // HD):
            here = slice(j * HD, (j + 1) * HD)
            term = mm(a_buf[c, :, here], b_buf[c, :, here], (0, 0))
            sums[j] = term if c == 0 else sums[j] + term
    for j in range(cols // HD):
        out_ref[j] = sums[j].astype(out_ref.dtype)


def states(a, b, at, dtype):
    rows, width = a.shape
    cols = width // 2
    chunks = rows // SUB
    buf = pltpu.VMEM((chunks, SUB, cols), BF16)
    return call(
        functools.partial(states_body, at),
        [a, b],
        [HBM, HBM],
        [((cols // HD, HD, HD), dtype, True)],
        rows * cols * HD,
        4 * rows * cols,
        [buf, buf, dma(chunks), dma(chunks)],
    )[0]


def sums_of(a_ref, b_ref, at, cols, blocks, wait):
    sums = [None] * (cols // HD)
    for b in blocks:
        wait(b)
        for j in range(cols // HD):
            here = (pl.ds(b * SUB, SUB), pl.ds(pl.multiple_of(at * cols + j * HD, HD), HD))
            term = mm(a_ref[here], b_ref[here], (0, 0))
            sums[j] = term if sums[j] is None else sums[j] + term
    return sums


def load_body(n_load, at, *refs):
    sources, out_ref, loads, sem = refs[:n_load], refs[n_load], refs[n_load + 1 : -1], refs[-1]
    rows, width = sources[0].shape
    blocks = rows // SUB
    copies = []
    for b in range(blocks):
        copies.append([])
        for n in range(n_load):
            here = pl.ds(b * SUB, SUB)
            copy = pltpu.make_async_copy(sources[n].at[here, :], loads[n].at[here, :], sem.at[n_load * b + n])
            copy.start()
            copies[b].append(copy)

    def wait(b):
        for copy in copies[b]:
            copy.wait()

    for j, total in enumerate(sums_of(loads[0], loads[1], at.y(), width // 2, range(blocks), wait)):
        out_ref[j] = total


def load(sources, at):
    rows, width = sources[0].shape
    n = len(sources)
    return call(
        functools.partial(load_body, n, at),
        sources,
        [HBM] * n,
        [((width // 2 // HD, HD, HD), F32, True)] + [((rows, width), BF16, True)] * n,
        rows * width // 2 * HD,
        4 * n * rows * width,
        [dma(n * (rows // SUB))],
    )


def both_states_body(at, a_ref, b_hbm, sent_ref, own_ref, b_ref, sem):
    rows, width = a_ref.shape
    blocks = rows // SUB
    copies = []
    for b in range(blocks):
        here = pl.ds(b * SUB, SUB)
        copies.append(pltpu.make_async_copy(b_hbm.at[here, :], b_ref.at[here, :], sem.at[b]))
        copies[b].start()
    for side, ref in ((1 - at.y(), sent_ref), (at.y(), own_ref)):
        wait = (lambda b: copies[b].wait()) if ref is sent_ref else (lambda b: None)
        for j, total in enumerate(sums_of(a_ref, b_ref, side, width // 2, range(blocks), wait)):
            ref[j] = total.astype(ref.dtype)


def both_states(a, b, at):
    rows, width = a.shape
    shape = (width // 2 // HD, HD, HD)
    return call(
        functools.partial(both_states_body, at),
        [a, b],
        [WHOLE, HBM],
        [(shape, BF16, True), (shape, F32, True), ((rows, width), BF16, True)],
        rows * width * HD,
        2 * rows * width,
        [dma(rows // SUB)],
    )


def key_inside_body(scale, other, at, g_ref, q_ref, v_ref, out_ref):
    rows, cols = out_ref.shape
    later = lax.broadcasted_iota(jnp.int32, (SUB, SUB), 1) >= lax.broadcasted_iota(jnp.int32, (SUB, SUB), 0)
    for to in range(0, cols, HD):
        from_ = pl.ds(pl.multiple_of((at.y() ^ other) * cols + to, HD), HD)
        state = None
        for b in reversed(range(rows // SUB)):
            here = (pl.ds(b * SUB, SUB), from_)
            g, q, v = g_ref[here], q_ref[here], v_ref[here]
            scores = jnp.where(later, mm(v, g, (1, 1)), 0.0).astype(BF16)
            total = mm(scores, q, (1, 0))
            if state is not None:
                total = total + mm(v, state.astype(BF16), (1, 0))
            out_ref[b * SUB : (b + 1) * SUB, to : to + HD] = total * scale
            if b:
                term = mm(g, q, (0, 0))
                state = term if state is None else state + term


def query_inside_body(scale, other, at, kinds, g_ref, k_ref, v_ref, *refs):
    pieces = refs[: len(kinds)]
    if kinds:
        out_ref, key_hbm, sem = refs[len(kinds) :]
    else:
        (out_ref,) = refs
    rows, cols = out_ref.shape
    copies = []
    for i, (piece, (piece_other, core)) in enumerate(zip(pieces, kinds)):
        size = piece.shape[1]
        group = (at.y() ^ piece_other) * 2 + (at.bit("outer", 0) ^ core)
        to = pl.ds(pl.multiple_of(group * size, size), size)
        copies.append(pltpu.make_async_copy(piece, key_hbm.at[:, to], sem.at[i]))
        copies[i].start()
    earlier = lax.broadcasted_iota(jnp.int32, (SUB, SUB), 0) >= lax.broadcasted_iota(jnp.int32, (SUB, SUB), 1)
    for to in range(0, cols, HD):
        from_ = pl.ds(pl.multiple_of((at.y() ^ other) * cols + to, HD), HD)
        state = None
        for b in range(rows // SUB):
            here = (pl.ds(b * SUB, SUB), from_)
            g, k, v = g_ref[here], k_ref[here], v_ref[here]
            scores = jnp.where(earlier, mm(g, v, (1, 1)), 0.0).astype(BF16)
            total = mm(scores, k, (1, 0))
            if state is not None:
                total = total + mm(g, state.astype(BF16), (1, 0))
            out_ref[b * SUB : (b + 1) * SUB, to : to + HD] = total * scale
            if b + 1 < rows // SUB:
                term = mm(v, k, (0, 0))
                state = term if state is None else state + term
    for copy in copies:
        copy.wait()


def key_inside(g, q, v, at, other, scale):
    rows, width = g.shape
    cols = width // 2
    return call(
        functools.partial(key_inside_body, scale, other, at),
        [g, q, v],
        [WHOLE] * 3,
        [((rows, cols), F32, True)],
        rows * cols * (2 * SUB + 2 * HD),
        10 * rows * cols,
    )[0]


def query_inside(g, k, v, at, other, scale, pieces=()):
    rows, width = g.shape
    cols = width // 2
    kinds = [kind for _, kind in pieces]
    outs = [((rows, cols), F32, True)] + [((rows, width), BF16, False)] * bool(pieces)
    return call(
        functools.partial(query_inside_body, scale, other, at, kinds),
        [g, k, v] + [piece for piece, _ in pieces],
        [WHOLE] * (3 + len(pieces)),
        outs,
        rows * cols * (2 * SUB + 2 * HD),
        10 * rows * cols,
        [dma(len(pieces))] if pieces else [],
    )


def query_body(scale, at, g_ref, in_own, in_oth, own_ref, oth_ref, out_hbm, buf, sem):
    n, rows, cols = buf.shape
    copies = []
    for other, (in_ref, state_ref) in enumerate(((in_own, own_ref), (in_oth, oth_ref))):
        half = at.y() ^ other
        for p in range(n // 2):
            i = other * (n // 2) + p
            for j in range(cols // HD):
                head = p * (cols // HD) + j
                from_ = pl.multiple_of((half * (n // 2) + p) * cols + j * HD, HD)
                part = mm(g_ref[:, pl.ds(from_, HD)], state_ref[head], (1, 0))
                total = in_ref[:, head * HD : (head + 1) * HD] + part * scale
                buf[i, :, j * HD : (j + 1) * HD] = total.astype(BF16)
            to = pl.ds(pl.multiple_of((half * (n // 2) + p) * cols, cols), cols)
            copies.append(pltpu.make_async_copy(buf.at[i], out_hbm.at[:, to], sem.at[i]))
            copies[i].start()
    for copy in copies:
        copy.wait()


def query_side(g, in_own, in_oth, own, oth, at, scale):
    rows, width = g.shape
    n = width // PAIR
    return call(
        functools.partial(query_body, scale, at),
        [g, in_own, in_oth, own, oth],
        [WHOLE] * 5,
        [((rows, width), BF16, False)],
        rows * width * HD,
        8 * rows * width,
        [pltpu.VMEM((n, rows, PAIR), BF16), dma(n)],
    )[0]


def turned_body(here_at, in_hbm, out_ref, buf, sem):
    size = out_ref.shape[0] // here_at.n_inner
    cols = max(size, HD)
    copies = []
    for n in range(out_ref.shape[0] // cols):
        copy = pltpu.make_async_copy(in_hbm.at[:, pl.ds(n * cols, cols)], buf.at[n], sem.at[n])
        copy.start()
        copies.append(copy)
    for n, copy in enumerate(copies):
        copy.wait()
        turned = buf[n].T
        for j in range(cols // size):
            at = pl.multiple_of(here_at.position(n * (cols // size) + j) * size, size)
            out_ref[pl.ds(at, size), :] = turned[j * size : (j + 1) * size, :]


def turned_inputs(inputs, at):
    rows, width = inputs.shape
    cols = max(width // at.n_inner, HD)
    return call(
        functools.partial(turned_body, at),
        [inputs],
        [HBM],
        [((width, rows), BF16, True)],
        0,
        4 * rows * width,
        [pltpu.VMEM((width // cols, rows, cols), BF16), dma(width // cols)],
    )[0]


def key_product_body(scale, grad_scale, at, other, cores, inside_ref, v_ref, state_ref, turned_ref, *refs):
    n = len(cores)
    cols = refs[0].shape[1]
    heads = cols // HD
    half = at.y() ^ other
    for s, core in enumerate(cores):
        key_ref, out = refs[s], refs[n + s]
        place = at.bit("outer", 0) ^ core
        for j in range(heads):
            head = place * heads + j
            here = pl.ds(pl.multiple_of(head * HD, HD), HD)
            from_ = pl.ds(pl.multiple_of((half * 2 * heads + head) * HD, HD), HD)
            part = mm(v_ref[:, from_], state_ref[head], (1, 0))
            key_ref[:, j * HD : (j + 1) * HD] = (inside_ref[:, here] + part * scale).astype(BF16)
        product = (mm(turned_ref[...], key_ref[...], (1, 0)) * grad_scale).astype(BF16)
        size = product.shape[0] // at.n_inner
        for r in range(at.n_inner):
            for i in range(2):
                out[i, r] = product[r * size + i * (size // 2) : r * size + (i + 1) * (size // 2)]


def key_product(inside, v, states, turned, at, other, cores, scale, grad_scale):
    n = len(cores)
    rows, width = v.shape
    cols = width // at.n_outer
    d = turned.shape[0]
    piece = ((2, at.n_inner, d // at.n_inner // 2, cols), BF16, True)
    return call(
        functools.partial(key_product_body, scale, grad_scale, at, other, cores),
        [inside, v, states, turned],
        [WHOLE] * 4,
        [((rows, cols), BF16, True)] * n + [piece] * n,
        n * cols * rows * (d + HD),
        2 * rows * (d + 4 * n * cols),
    )


def cores_body(at, *refs):
    (n_own, n_oth, g_own, g_oth), (p_send, p_keep, q_send, q_keep) = refs[:4], refs[4:]
    far_own = at.bit("outer", 1) ^ at.y()
    p_own = n_own[0].astype(F32) + g_own[0].astype(F32)
    p_oth = n_oth[0].astype(F32) + g_oth[0].astype(F32)
    p_send[0] = jnp.where(far_own == 1, p_own, p_oth).astype(BF16)
    p_keep[0] = jnp.where(far_own == 1, p_oth, p_own)
    n = n_own.shape[1] // 2
    for side, near, got in ((far_own, n_own, g_own), (1 - far_own, n_oth, g_oth)):
        q_keep[side] = near[1, :n].astype(F32) + got[1, :n].astype(F32)
        q_send[side] = (near[1, n:].astype(F32) + got[1, n:].astype(F32)).astype(BF16)


def cores(at, near_own, near_oth, got_own, got_oth):
    _, n, part, cols = near_own.shape
    one, two = (1, n, part, cols), (2, n // 2, part, cols)
    return call(
        functools.partial(cores_body, at),
        [near_own, near_oth, got_own, got_oth],
        [WHOLE] * 4,
        [(one, BF16, True), (one, F32, True), (two, BF16, True), (two, F32, True)],
    )


def adam(grad, master, moment1, moment2):
    new_moment1 = 0.9 * moment1 + 0.1 * grad
    new_moment2 = 0.95 * moment2 + 0.05 * grad * grad
    new_master = master - 0.01 * (new_moment1 / (jnp.sqrt(new_moment2) + 1e-08) + 0.1 * master)
    return new_master, new_moment1, new_moment2


def adam_own_body(at, n, *refs):
    sums, (master_ref, m1_ref, m2_ref, grad_ref, weight_ref) = refs[:n], refs[n:]
    _, _, part, size = sums[0].shape
    cols = pl.ds(pl.multiple_of(at.group(0) * size, size), size)
    for j in range(2):
        here = slice(j * part, (j + 1) * part)
        grad = sum(ref[j, 0].astype(F32) for ref in sums).astype(BF16)
        grad_ref[here, :] = grad
        new_master, _, _ = adam(grad.astype(F32), master_ref[here, cols], m1_ref[here, cols], m2_ref[here, cols])
        weight_ref[j, 0] = new_master.astype(BF16)


def adam_own(sums, master, moment1, moment2, at):
    shape = sums[0].shape
    _, _, part, cols = shape
    return call(
        functools.partial(adam_own_body, at, len(sums)),
        [*sums, master, moment1, moment2],
        [WHOLE] * (len(sums) + 3),
        [((2 * part, cols), BF16, True), (shape, BF16, True)],
        2 * part * cols,
        48 * part * cols,
    )


def adam_all_body(picks, at, *refs):
    n = len(picks)
    grads, (master_ref, m1_ref, m2_ref) = refs[:n], refs[n : n + 3]
    outs, bufs, sem = refs[n + 3 : n + 6], refs[n + 6 : n + 9], refs[n + 9]
    size = grads[0].shape[1]
    copies = []
    for s in range(n):
        cols = pl.ds(pl.multiple_of(at.group(picks[s]) * size, size), size)
        new = adam(grads[s][...].astype(F32), master_ref[:, cols], m1_ref[:, cols], m2_ref[:, cols])
        for i in range(3):
            bufs[i][s] = new[i]
            copy = pltpu.make_async_copy(bufs[i].at[s], outs[i].at[:, cols], sem.at[s * 3 + i])
            copy.start()
            copies.append(copy)
    for copy in copies:
        copy.wait()


def adam_all(grads, master, moment1, moment2, at, picks):
    n = len(grads)
    rows, cols = grads[0].shape
    return call(
        functools.partial(adam_all_body, picks, at),
        [*grads, master, moment1, moment2],
        [WHOLE] * (n + 3),
        [(master.shape, F32, False)] * 3,
        n * rows * cols,
        26 * n * rows * cols,
        [pltpu.VMEM((n, rows, cols), F32)] * 3 + [dma(3 * n)],
    )


def assemble_body(kinds, at, *refs):
    n = len(kinds)
    pieces, bufs = refs[:n], refs[-n - 1 : -1]
    out_hbm, sem = refs[-n - 2], refs[-1]
    copies = []
    for i, (which, groups, start, count) in enumerate(kinds):
        size = pieces[i].shape[-1]
        for s, k in enumerate(groups):
            cols = pl.ds(pl.multiple_of(at.group(k) * size, size), size)
            for r in range(count):
                block = at.block(start + r)
                if which:
                    bufs[i][s, block // 2] = pieces[i][s, r]
                else:
                    bufs[i][s, block // 2, block % 2] = pieces[i][s, r]
            if which:
                goal = out_hbm.at[:, at.block(start) % 2, which, :, cols]
            else:
                goal = out_hbm.at[:, :, which, :, cols]
            copy = pltpu.make_async_copy(bufs[i].at[s], goal, sem.at[2 * i + s])
            copy.start()
            copies.append(copy)
    for copy in copies:
        copy.wait()


def assemble(pieces, at, before, width):
    n_inner = at.n_inner
    part, cols = pieces[0][0].shape[2:]
    kinds = [kind for _, kind in pieces]
    bufs = [
        pltpu.VMEM((len(groups), n_inner // 2) + (() if which else (2,)) + (part, cols), BF16)
        for which, groups, _, _ in kinds
    ]
    more = [] if before is None else [before]
    return call(
        functools.partial(assemble_body, kinds, at),
        [array for array, _ in pieces] + more,
        [WHOLE] * len(pieces) + [HBM] * len(more),
        [((n_inner // 2, 2, 2, part, width), BF16, False)],
        0,
        4 * sum(array.size for array, _ in pieces),
        bufs + [dma(2 * len(pieces))],
        {len(pieces): 0} if more else None,
    )[0]


def swap(x, axis, bit):
    n = lax.axis_size(axis)
    return lax.ppermute(x, axis, [(i, i ^ (1 << bit)) for i in range(n)])


def reversed_bits(value, n_bits):
    out = 0
    for b in range(n_bits):
        out = out | (((value >> b) & 1) << (n_bits - 1 - b))
    return out


def step_body(level, side, at, more, total_ref, got_ref, *refs):
    send_out, outside_out = refs[-2:]
    got = got_ref[...].astype(F32)
    total = total_ref[...] + got
    send_out[...] = total.astype(BF16)
    if more:
        refs[-3][...] = total
    if level is None:
        outside_out[...] = jnp.zeros_like(got)
    else:
        outside_out[...] = refs[0][...] + jnp.where(at.bit(*level) == side, got, 0.0)


def step(level, side, at, total, got, *outside, more=True):
    outs = [(total.shape, F32, True)] * more + [(total.shape, BF16, True), (total.shape, F32, True)]
    body = functools.partial(step_body, level, side, at, more)
    results = call(body, [total, got, *outside], [WHOLE] * (2 + len(outside)), outs)
    return results if more else [None, *results]


def last_body(level, side, at, outside_ref, got_ref, own_ref, came_ref, give_out, out):
    outside = outside_ref[...] + jnp.where(at.bit(*level) == side, got_ref[...].astype(F32), 0.0)
    mine = at.y() == side
    give_out[...] = (outside + jnp.where(mine, 0.0, own_ref[...])).astype(BF16)
    out[...] = (outside + jnp.where(mine, came_ref[...].astype(F32), 0.0)).astype(BF16)


def last(level, side, at, outside, got, own, came):
    outs = [(own.shape, BF16, True)] * 2
    return call(functools.partial(last_body, level, side, at), [outside, got, own, came], [WHOLE] * 4, outs)


def scan_states(own, sent, reverse, at):
    side = 0 if reverse else 1
    came = swap(sent, "inner", 0)
    after = yield came
    own = own()
    came = tie(came, *after)
    total, send, outside = step(None, side, at, own, came)
    levels = [("inner", b) for b in range(1, at.i_bits)] + [("outer", b) for b in range(at.o_bits)]
    for n, level in enumerate(levels):
        got = swap(send, *level)
        after = yield got
        got = tie(got, *after)
        if n + 1 < len(levels):
            total, send, outside = step(level, side, at, total, got, outside, more=n + 2 < len(levels))
    give, kept = last(levels[-1], side, at, outside, got, own, came)
    back = swap(give, "inner", 0)
    yield kept, back


def fold(keep, got, axis):
    size = keep.shape[axis] // 2
    low, high = [
        lax.slice_in_dim(keep, at, at + size, axis=axis).astype(F32)
        + lax.slice_in_dim(got, at, at + size, axis=axis).astype(F32)
        for at in (0, size)
    ]
    return high.astype(BF16), low


def fan_body(n_keep, ways, *refs):
    outs = refs[len(refs) - ways :]
    if n_keep == 2:
        rows = [(refs[0], refs[1]), (refs[2], refs[3])]
        totals = [sum(ref[0].astype(F32) for ref in pair) for pair in rows]
    else:
        totals = [sum(ref[i].astype(F32) for ref in refs[: len(refs) - ways]) for i in range(2)]
    size = outs[0].shape[1]
    for i, total in enumerate(totals):
        for j, out in enumerate(outs):
            out[i] = total[j * size : (j + 1) * size].astype(out.dtype)


def fan(n_keep, ways, *arrays):
    _, n, part, cols = arrays[0].shape
    shape = (2, n // ways, part, cols)
    outs = [(shape, F32 if j == 0 else BF16, True) for j in range(ways)]
    return call(functools.partial(fan_body, n_keep, ways), list(arrays), [WHOLE] * len(arrays), outs)


def swap_all(xs, masks):
    n = lax.axis_size("inner")
    return [lax.ppermute(x, "inner", [(i, i ^ mask) for i in range(n)]) for x, mask in zip(xs, masks)]


def bit_groups(i_bits):
    groups = []
    for b in range(1, i_bits, 2):
        if b + 1 < i_bits:
            groups.append([((i >> 1) << b) | ((i & 1) << (b + 1)) for i in range(1, 4)])
        else:
            groups.append([1 << b])
    return groups


def join_body(axis, *refs):
    out = refs[-1]
    size = refs[0].shape[axis]
    for side, ref in enumerate(refs[:-1]):
        at = tuple(pl.ds(side * size, size) if a == axis else slice(None) for a in range(len(ref.shape)))
        out[at] = ref[...]


def join(axis, *arrays):
    shape = tuple(len(arrays) * s if i == axis else s for i, s in enumerate(arrays[0].shape))
    body = functools.partial(join_body, axis)
    return call(body, list(arrays), [WHOLE] * len(arrays), [(shape, BF16, True)])[0]


def split_body(*refs):
    outs = refs[-2:]
    for j, ref in enumerate(refs[:-2]):
        n = ref.shape[1]
        for i, out in enumerate(outs):
            out[:, j * n : (j + 1) * n] = ref[i : i + 1]


def split(*arrays):
    _, n, part, cols = arrays[0].shape
    return call(
        split_body, list(arrays), [WHOLE] * len(arrays), [((1, len(arrays) * n, part, cols), BF16, True)] * 2
    )


def local(inputs, queries, keys, values, out_grad, master, moment1, moment2):
    rows_here, width = queries.shape
    d = inputs.shape[1]
    n_outer = lax.axis_size("outer")
    n_inner = lax.axis_size("inner")
    at = Here(n_outer, n_inner)
    i_bits = at.i_bits
    assert n_outer == 4 and i_bits >= 2
    total_tokens = rows_here * n_outer * n_inner
    att_scale = 1.0 / math.sqrt(HD * total_tokens)
    grad_scale = 1.0 / math.sqrt(total_tokens)

    qg_sent = states(out_grad, queries, at, BF16)
    loaded = []

    def own_states():
        loaded.extend(load([out_grad, queries, values], at))
        return loaded[0]

    qg = scan_states(own_states, qg_sent, True, at)
    next(qg)
    qg.send([])
    g, q, v = loaded[1:]
    kv_sent, kv_own, k = both_states(v, keys, at)
    done = [kv_own]
    turned = None
    for _ in range(2, i_bits):
        qg.send(done)
        done = []
        if turned is None:
            in_own = key_inside(tie(g, kv_own), q, v, at, 0, att_scale)
            turned = turned_inputs(tie(inputs, kv_own), at)
            done = [in_own, turned]
    qg.send(done)
    qg.send([])
    in_oth = key_inside(tie(g, in_own, turned), q, v, at, 1, att_scale)
    kv = scan_states(lambda: kv_own, kv_sent, False, at)
    kv_got = next(kv)
    kv_stages = i_bits + 2
    qg_own, qg_oth = qg.send([in_oth])

    def kv_next(*after):
        nonlocal kv_stages, kv_got
        if kv_stages:
            kv_stages -= 1
            kv_got = kv.send(list(after))
        return kv_got

    ends = (att_scale, grad_scale)
    in_own = tie(in_own, kv_got)
    far_key, near_key, far_own, near_own = key_product(in_own, v, qg_own, turned, at, 0, (1, 0), *ends)
    keys_own = [(far_key, (0, 1)), (near_key, (0, 0))]
    got_own = swap(far_own, "outer", 0)
    far_key, far_oth = key_product(in_oth, v, qg_oth, turned, at, 1, (1,), *ends)
    got_oth = swap(far_oth, "outer", 0)
    near_key, near_oth = key_product(in_oth, v, qg_oth, turned, at, 1, (0,), *ends)
    pieces = keys_own + [(far_key, (1, 1)), (near_key, (1, 0))]

    p_send, p, q_send, q = cores(at, near_own, near_oth, got_own, got_oth)
    p_got, q_got = swap(p_send, "outer", 1), swap(q_send, "inner", 0)
    query_own, key_grad = query_inside(tie(g, p_send), k, v, at, 0, att_scale, pieces)
    kv_next(p_send, q_send)
    p_send, p = fold(p, p_got, 1)
    q_send, q = fold(q, q_got, 0)
    p_send, q_send = tie(p_send, query_own), tie(q_send, query_own)
    p_got, q_got = swap(p_send, "inner", 0), swap(q_send, "outer", 1)
    (query_oth,) = query_inside(tie(g, p_send, q_send), k, v, at, 1, att_scale)
    kv_next(p_send, q_send)
    groups = bit_groups(i_bits)
    keep, *sends = fan(2, 1 + len(groups[0]), p, p_got, q, q_got)
    sends[0] = tie(sends[0], query_oth)
    came = swap_all(sends, groups[0])
    for masks in groups[1:]:
        keep, *sends = fan(1, 1 + len(masks), keep, *came)
        came = swap_all(sends, masks)
    grad, weight = adam_own([keep, *came], master, moment1, moment2, at)
    while kv_stages > 1:
        kv_now = kv_next(weight)

    grad_x = swap(grad, "outer", 1)
    for masks in reversed(groups[1:]):
        weight = join(1, weight, *swap_all([weight] * len(masks), masks))
    p, q = split(weight, *swap_all([weight] * len(groups[0]), groups[0]))
    p, q = tie(p, grad_x), tie(q, grad_x)
    kv_own, kv_oth = kv_next(p, q)
    p_got, q_got = swap(p, "inner", 0), swap(q, "outer", 1)
    grads = [grad, swap(grad, "outer", 0), grad_x, swap(grad_x, "outer", 0)]
    p, q = join(1, p, p_got), join(0, q, q_got)
    p, q = tie(p, kv_oth), tie(q, kv_oth)
    p_last, q_last = swap(p, "outer", 1), swap(q, "inner", 0)
    p_core, q_core = swap(p, "outer", 0), swap(q, "outer", 0)
    query_grad = query_side(tie(g, p, q), query_own, query_oth, kv_own, kv_oth, at, att_scale)
    new_master, new_moment1, new_moment2 = adam_all(
        [tie(grads[0], p, q)] + grads[1:], master, moment1, moment2, at, (0, 1, 2, 3)
    )
    n = n_inner // 2
    weights = assemble(
        [(p, (0, (0,), 0, 2 * n)), (q, (1, (0, 2), 0, n)), (p_core, (0, (1,), 0, 2 * n)), (q_core, (1, (1, 3), 0, n))],
        at, None, width,
    )
    done = [weights, query_grad, new_master]
    p_core, q_core = swap(tie(p_last, *done), "outer", 0), swap(tie(q_last, *done), "outer", 0)
    weights = assemble([(p_last, (0, (2,), 0, 2 * n)), (q_last, (1, (0, 2), n, n))], at, weights, width)
    weights = assemble([(p_core, (0, (3,), 0, 2 * n)), (q_core, (1, (1, 3), n, n))], at, weights, width)
    return (query_grad, key_grad, new_master, new_moment1, new_moment2, weights.reshape(d, width))


def solution(mesh):
    tokens = P(("outer", "inner"), None)
    rows = P("inner", None)
    return jax.shard_map(
        local,
        mesh=mesh,
        in_specs=(tokens,) * 5 + (rows,) * 3,
        out_specs=(tokens, tokens, rows, rows, rows, P()),
        check_vma=False,
    )
```

```python
import functools
import math

import jax
import jax.numpy as jnp
from jax import lax
from jax.experimental import pallas as pl
from jax.experimental.pallas import tpu as pltpu
from jax.sharding import PartitionSpec as P

HD = 128
SUB = 256
PAIR = 2 * HD
VMEM = 16 * 1024 * 1024
F32 = jnp.float32
BF16 = jnp.bfloat16
WHOLE = pl.BlockSpec(memory_space=pltpu.VMEM)
HBM = pl.BlockSpec(memory_space=pltpu.HBM)


def mm(a, b, contract):
    return lax.dot_general(a, b, ((contract[:1], contract[1:]), ((), ())), preferred_element_type=F32)


def far(x):
    return pltpu.with_memory_space_constraint(x, pltpu.HBM)


def call(body, args, specs, outs, macs=0, moved=0, scratch=(), aliases=None):
    args = [far(a) if spec is HBM else a for a, spec in zip(args, specs)]
    return pl.pallas_call(
        body,
        in_specs=specs,
        out_specs=[WHOLE if near else HBM for _, _, near in outs],
        out_shape=[(jax.ShapeDtypeStruct if near else pltpu.HBM)(shape, dtype) for shape, dtype, near in outs],
        scratch_shapes=list(scratch),
        input_output_aliases=aliases or {},
        compiler_params=pltpu.CompilerParams(vmem_limit_bytes=VMEM),
        cost_estimate=pl.CostEstimate(flops=2 * macs, bytes_accessed=moved, transcendentals=0),
    )(*args)


def dma(n):
    return pltpu.SemaphoreType.DMA((n,))


def tie(x, *after):
    return lax.optimization_barrier((x, *after))[0] if after else x


class Here:
    def __init__(self, n_outer, n_inner):
        self.i_bits, self.o_bits = (n_inner - 1).bit_length(), (n_outer - 1).bit_length()
        self.n_outer, self.n_inner = n_outer, n_inner

    def group(self, k):
        return lax.axis_index("outer") ^ k

    def block(self, p):
        return lax.axis_index("inner") ^ reversed_bits(p, self.i_bits)

    def position(self, block):
        return reversed_bits(lax.axis_index("inner") ^ block, self.i_bits)

    def bit(self, axis, b):
        return (lax.axis_index(axis) >> b) & 1

    def y(self):
        return self.bit("inner", 0)


def states_body(at, a_hbm, b_hbm, out_ref, a_buf, b_buf, a_sem, b_sem):
    chunks, rows, cols = a_buf.shape
    at = pl.multiple_of((1 - at.y()) * cols, cols)
    copies = []
    for c in range(chunks):
        here = (pl.ds(c * rows, rows), pl.ds(at, cols))
        pair = (
            pltpu.make_async_copy(a_hbm.at[here], a_buf.at[c], a_sem.at[c]),
            pltpu.make_async_copy(b_hbm.at[here], b_buf.at[c], b_sem.at[c]),
        )
        for copy in pair:
            copy.start()
        copies.append(pair)
    sums = [None] * (cols // HD)
    for c in range(chunks):
        for copy in copies[c]:
            copy.wait()
        for j in range(cols // HD):
            here = slice(j * HD, (j + 1) * HD)
            term = mm(a_buf[c, :, here], b_buf[c, :, here], (0, 0))
            sums[j] = term if c == 0 else sums[j] + term
    for j in range(cols // HD):
        out_ref[j] = sums[j].astype(out_ref.dtype)


def states(a, b, at, dtype):
    rows, width = a.shape
    cols = width // 2
    chunks = rows // SUB
    buf = pltpu.VMEM((chunks, SUB, cols), BF16)
    return call(
        functools.partial(states_body, at),
        [a, b],
        [HBM, HBM],
        [((cols // HD, HD, HD), dtype, True)],
        rows * cols * HD,
        4 * rows * cols,
        [buf, buf, dma(chunks), dma(chunks)],
    )[0]


def sums_of(a_ref, b_ref, at, cols, blocks, wait):
    sums = [None] * (cols // HD)
    for b in blocks:
        wait(b)
        for j in range(cols // HD):
            here = (pl.ds(b * SUB, SUB), pl.ds(pl.multiple_of(at * cols + j * HD, HD), HD))
            term = mm(a_ref[here], b_ref[here], (0, 0))
            sums[j] = term if sums[j] is None else sums[j] + term
    return sums


def load_body(n_load, at, *refs):
    sources, out_ref, loads, sem = refs[:n_load], refs[n_load], refs[n_load + 1 : -1], refs[-1]
    rows, width = sources[0].shape
    blocks = rows // SUB
    copies = []
    for b in range(blocks):
        copies.append([])
        for n in range(n_load):
            here = pl.ds(b * SUB, SUB)
            copy = pltpu.make_async_copy(sources[n].at[here, :], loads[n].at[here, :], sem.at[n_load * b + n])
            copy.start()
            copies[b].append(copy)

    def wait(b):
        for copy in copies[b]:
            copy.wait()

    for j, total in enumerate(sums_of(loads[0], loads[1], at.y(), width // 2, range(blocks), wait)):
        out_ref[j] = total


def load(sources, at):
    rows, width = sources[0].shape
    n = len(sources)
    return call(
        functools.partial(load_body, n, at),
        sources,
        [HBM] * n,
        [((width // 2 // HD, HD, HD), F32, True)] + [((rows, width), BF16, True)] * n,
        rows * width // 2 * HD,
        4 * n * rows * width,
        [dma(n * (rows // SUB))],
    )


def both_states_body(at, a_ref, b_hbm, sent_ref, own_ref, b_ref, sem):
    rows, width = a_ref.shape
    blocks = rows // SUB
    copies = []
    for b in range(blocks):
        here = pl.ds(b * SUB, SUB)
        copies.append(pltpu.make_async_copy(b_hbm.at[here, :], b_ref.at[here, :], sem.at[b]))
        copies[b].start()
    for side, ref in ((1 - at.y(), sent_ref), (at.y(), own_ref)):
        wait = (lambda b: copies[b].wait()) if ref is sent_ref else (lambda b: None)
        for j, total in enumerate(sums_of(a_ref, b_ref, side, width // 2, range(blocks), wait)):
            ref[j] = total.astype(ref.dtype)


def both_states(a, b, at):
    rows, width = a.shape
    shape = (width // 2 // HD, HD, HD)
    return call(
        functools.partial(both_states_body, at),
        [a, b],
        [WHOLE, HBM],
        [(shape, BF16, True), (shape, F32, True), ((rows, width), BF16, True)],
        rows * width * HD,
        2 * rows * width,
        [dma(rows // SUB)],
    )


def key_inside_body(scale, other, at, g_ref, q_ref, v_ref, out_ref):
    rows, cols = out_ref.shape
    later = lax.broadcasted_iota(jnp.int32, (SUB, SUB), 1) >= lax.broadcasted_iota(jnp.int32, (SUB, SUB), 0)
    for to in range(0, cols, HD):
        from_ = pl.ds(pl.multiple_of((at.y() ^ other) * cols + to, HD), HD)
        state = None
        for b in reversed(range(rows // SUB)):
            here = (pl.ds(b * SUB, SUB), from_)
            g, q, v = g_ref[here], q_ref[here], v_ref[here]
            scores = jnp.where(later, mm(v, g, (1, 1)), 0.0).astype(BF16)
            total = mm(scores, q, (1, 0))
            if state is not None:
                total = total + mm(v, state.astype(BF16), (1, 0))
            out_ref[b * SUB : (b + 1) * SUB, to : to + HD] = total * scale
            if b:
                term = mm(g, q, (0, 0))
                state = term if state is None else state + term


def query_inside_body(scale, other, at, kinds, g_ref, k_ref, v_ref, *refs):
    pieces = refs[: len(kinds)]
    if kinds:
        out_ref, key_hbm, sem = refs[len(kinds) :]
    else:
        (out_ref,) = refs
    rows, cols = out_ref.shape
    copies = []
    for i, (piece, (piece_other, core)) in enumerate(zip(pieces, kinds)):
        size = piece.shape[1]
        group = (at.y() ^ piece_other) * 2 + (at.bit("outer", 0) ^ core)
        to = pl.ds(pl.multiple_of(group * size, size), size)
        copies.append(pltpu.make_async_copy(piece, key_hbm.at[:, to], sem.at[i]))
        copies[i].start()
    earlier = lax.broadcasted_iota(jnp.int32, (SUB, SUB), 0) >= lax.broadcasted_iota(jnp.int32, (SUB, SUB), 1)
    for to in range(0, cols, HD):
        from_ = pl.ds(pl.multiple_of((at.y() ^ other) * cols + to, HD), HD)
        state = None
        for b in range(rows // SUB):
            here = (pl.ds(b * SUB, SUB), from_)
            g, k, v = g_ref[here], k_ref[here], v_ref[here]
            scores = jnp.where(earlier, mm(g, v, (1, 1)), 0.0).astype(BF16)
            total = mm(scores, k, (1, 0))
            if state is not None:
                total = total + mm(g, state.astype(BF16), (1, 0))
            out_ref[b * SUB : (b + 1) * SUB, to : to + HD] = total * scale
            if b + 1 < rows // SUB:
                term = mm(v, k, (0, 0))
                state = term if state is None else state + term
    for copy in copies:
        copy.wait()


def key_inside(g, q, v, at, other, scale):
    rows, width = g.shape
    cols = width // 2
    return call(
        functools.partial(key_inside_body, scale, other, at),
        [g, q, v],
        [WHOLE] * 3,
        [((rows, cols), F32, True)],
        rows * cols * (2 * SUB + 2 * HD),
        10 * rows * cols,
    )[0]


def query_inside(g, k, v, at, other, scale, pieces=()):
    rows, width = g.shape
    cols = width // 2
    kinds = [kind for _, kind in pieces]
    outs = [((rows, cols), F32, True)] + [((rows, width), BF16, False)] * bool(pieces)
    return call(
        functools.partial(query_inside_body, scale, other, at, kinds),
        [g, k, v] + [piece for piece, _ in pieces],
        [WHOLE] * (3 + len(pieces)),
        outs,
        rows * cols * (2 * SUB + 2 * HD),
        10 * rows * cols,
        [dma(len(pieces))] if pieces else [],
    )


def query_body(scale, at, g_ref, in_own, in_oth, own_ref, oth_ref, out_hbm, buf, sem):
    n, rows, cols = buf.shape
    copies = []
    for other, (in_ref, state_ref) in enumerate(((in_own, own_ref), (in_oth, oth_ref))):
        half = at.y() ^ other
        for p in range(n // 2):
            i = other * (n // 2) + p
            for j in range(cols // HD):
                head = p * (cols // HD) + j
                from_ = pl.multiple_of((half * (n // 2) + p) * cols + j * HD, HD)
                part = mm(g_ref[:, pl.ds(from_, HD)], state_ref[head], (1, 0))
                total = in_ref[:, head * HD : (head + 1) * HD] + part * scale
                buf[i, :, j * HD : (j + 1) * HD] = total.astype(BF16)
            to = pl.ds(pl.multiple_of((half * (n // 2) + p) * cols, cols), cols)
            copies.append(pltpu.make_async_copy(buf.at[i], out_hbm.at[:, to], sem.at[i]))
            copies[i].start()
    for copy in copies:
        copy.wait()


def query_side(g, in_own, in_oth, own, oth, at, scale):
    rows, width = g.shape
    n = width // PAIR
    return call(
        functools.partial(query_body, scale, at),
        [g, in_own, in_oth, own, oth],
        [WHOLE] * 5,
        [((rows, width), BF16, False)],
        rows * width * HD,
        8 * rows * width,
        [pltpu.VMEM((n, rows, PAIR), BF16), dma(n)],
    )[0]


def turned_body(here_at, in_hbm, out_ref, buf, sem):
    size = out_ref.shape[0] // here_at.n_inner
    cols = max(size, HD)
    copies = []
    for n in range(out_ref.shape[0] // cols):
        copy = pltpu.make_async_copy(in_hbm.at[:, pl.ds(n * cols, cols)], buf.at[n], sem.at[n])
        copy.start()
        copies.append(copy)
    for n, copy in enumerate(copies):
        copy.wait()
        turned = buf[n].T
        for j in range(cols // size):
            at = pl.multiple_of(here_at.position(n * (cols // size) + j) * size, size)
            out_ref[pl.ds(at, size), :] = turned[j * size : (j + 1) * size, :]


def turned_inputs(inputs, at):
    rows, width = inputs.shape
    cols = max(width // at.n_inner, HD)
    return call(
        functools.partial(turned_body, at),
        [inputs],
        [HBM],
        [((width, rows), BF16, True)],
        0,
        4 * rows * width,
        [pltpu.VMEM((width // cols, rows, cols), BF16), dma(width // cols)],
    )[0]


def key_product_body(scale, grad_scale, at, other, cores, inside_ref, v_ref, state_ref, turned_ref, *refs):
    n = len(cores)
    cols = refs[0].shape[1]
    heads = cols // HD
    half = at.y() ^ other
    for s, core in enumerate(cores):
        key_ref, out = refs[s], refs[n + s]
        place = at.bit("outer", 0) ^ core
        for j in range(heads):
            head = place * heads + j
            here = pl.ds(pl.multiple_of(head * HD, HD), HD)
            from_ = pl.ds(pl.multiple_of((half * 2 * heads + head) * HD, HD), HD)
            part = mm(v_ref[:, from_], state_ref[head], (1, 0))
            key_ref[:, j * HD : (j + 1) * HD] = (inside_ref[:, here] + part * scale).astype(BF16)
        product = (mm(turned_ref[...], key_ref[...], (1, 0)) * grad_scale).astype(BF16)
        size = product.shape[0] // at.n_inner
        for r in range(at.n_inner):
            for i in range(2):
                out[i, r] = product[r * size + i * (size // 2) : r * size + (i + 1) * (size // 2)]


def key_product(inside, v, states, turned, at, other, cores, scale, grad_scale):
    n = len(cores)
    rows, width = v.shape
    cols = width // at.n_outer
    d = turned.shape[0]
    piece = ((2, at.n_inner, d // at.n_inner // 2, cols), BF16, True)
    return call(
        functools.partial(key_product_body, scale, grad_scale, at, other, cores),
        [inside, v, states, turned],
        [WHOLE] * 4,
        [((rows, cols), BF16, True)] * n + [piece] * n,
        n * cols * rows * (d + HD),
        2 * rows * (d + 4 * n * cols),
    )


def cores_body(at, *refs):
    (n_own, n_oth, g_own, g_oth), (p_send, p_keep, q_send, q_keep) = refs[:4], refs[4:]
    far_own = at.bit("outer", 1) ^ at.y()
    p_own = n_own[0].astype(F32) + g_own[0].astype(F32)
    p_oth = n_oth[0].astype(F32) + g_oth[0].astype(F32)
    p_send[0] = jnp.where(far_own == 1, p_own, p_oth).astype(BF16)
    p_keep[0] = jnp.where(far_own == 1, p_oth, p_own)
    n = n_own.shape[1] // 2
    for side, near, got in ((far_own, n_own, g_own), (1 - far_own, n_oth, g_oth)):
        q_keep[side] = near[1, :n].astype(F32) + got[1, :n].astype(F32)
        q_send[side] = (near[1, n:].astype(F32) + got[1, n:].astype(F32)).astype(BF16)


def cores(at, near_own, near_oth, got_own, got_oth):
    _, n, part, cols = near_own.shape
    one, two = (1, n, part, cols), (2, n // 2, part, cols)
    return call(
        functools.partial(cores_body, at),
        [near_own, near_oth, got_own, got_oth],
        [WHOLE] * 4,
        [(one, BF16, True), (one, F32, True), (two, BF16, True), (two, F32, True)],
    )


def adam(grad, master, moment1, moment2):
    new_moment1 = 0.9 * moment1 + 0.1 * grad
    new_moment2 = 0.95 * moment2 + 0.05 * grad * grad
    new_master = master - 0.01 * (new_moment1 / (jnp.sqrt(new_moment2) + 1e-08) + 0.1 * master)
    return new_master, new_moment1, new_moment2


def adam_own_body(at, n, *refs):
    sums, (master_ref, m1_ref, m2_ref, grad_ref, weight_ref) = refs[:n], refs[n:]
    _, _, part, size = sums[0].shape
    cols = pl.ds(pl.multiple_of(at.group(0) * size, size), size)
    for j in range(2):
        here = slice(j * part, (j + 1) * part)
        grad = sum(ref[j, 0].astype(F32) for ref in sums).astype(BF16)
        grad_ref[here, :] = grad
        new_master, _, _ = adam(grad.astype(F32), master_ref[here, cols], m1_ref[here, cols], m2_ref[here, cols])
        weight_ref[j, 0] = new_master.astype(BF16)


def adam_own(sums, master, moment1, moment2, at):
    shape = sums[0].shape
    _, _, part, cols = shape
    return call(
        functools.partial(adam_own_body, at, len(sums)),
        [*sums, master, moment1, moment2],
        [WHOLE] * (len(sums) + 3),
        [((2 * part, cols), BF16, True), (shape, BF16, True)],
        2 * part * cols,
        48 * part * cols,
    )


def adam_all_body(picks, at, *refs):
    n = len(picks)
    grads, (master_ref, m1_ref, m2_ref) = refs[:n], refs[n : n + 3]
    outs, bufs, sem = refs[n + 3 : n + 6], refs[n + 6 : n + 9], refs[n + 9]
    size = grads[0].shape[1]
    copies = []
    for s in range(n):
        cols = pl.ds(pl.multiple_of(at.group(picks[s]) * size, size), size)
        new = adam(grads[s][...].astype(F32), master_ref[:, cols], m1_ref[:, cols], m2_ref[:, cols])
        for i in range(3):
            bufs[i][s] = new[i]
            copy = pltpu.make_async_copy(bufs[i].at[s], outs[i].at[:, cols], sem.at[s * 3 + i])
            copy.start()
            copies.append(copy)
    for copy in copies:
        copy.wait()


def adam_all(grads, master, moment1, moment2, at, picks):
    n = len(grads)
    rows, cols = grads[0].shape
    return call(
        functools.partial(adam_all_body, picks, at),
        [*grads, master, moment1, moment2],
        [WHOLE] * (n + 3),
        [(master.shape, F32, False)] * 3,
        n * rows * cols,
        26 * n * rows * cols,
        [pltpu.VMEM((n, rows, cols), F32)] * 3 + [dma(3 * n)],
    )


def assemble_body(kinds, at, *refs):
    n = len(kinds)
    pieces, bufs = refs[:n], refs[-n - 1 : -1]
    out_hbm, sem = refs[-n - 2], refs[-1]
    copies = []
    for i, (which, groups, start, count) in enumerate(kinds):
        size = pieces[i].shape[-1]
        for s, k in enumerate(groups):
            cols = pl.ds(pl.multiple_of(at.group(k) * size, size), size)
            for r in range(count):
                block = at.block(start + r)
                if which:
                    bufs[i][s, block // 2] = pieces[i][s, r]
                else:
                    bufs[i][s, block // 2, block % 2] = pieces[i][s, r]
            if which:
                goal = out_hbm.at[:, at.block(start) % 2, which, :, cols]
            else:
                goal = out_hbm.at[:, :, which, :, cols]
            copy = pltpu.make_async_copy(bufs[i].at[s], goal, sem.at[2 * i + s])
            copy.start()
            copies.append(copy)
    for copy in copies:
        copy.wait()


def assemble(pieces, at, before, width):
    n_inner = at.n_inner
    part, cols = pieces[0][0].shape[2:]
    kinds = [kind for _, kind in pieces]
    bufs = [
        pltpu.VMEM((len(groups), n_inner // 2) + (() if which else (2,)) + (part, cols), BF16)
        for which, groups, _, _ in kinds
    ]
    more = [] if before is None else [before]
    return call(
        functools.partial(assemble_body, kinds, at),
        [array for array, _ in pieces] + more,
        [WHOLE] * len(pieces) + [HBM] * len(more),
        [((n_inner // 2, 2, 2, part, width), BF16, False)],
        0,
        4 * sum(array.size for array, _ in pieces),
        bufs + [dma(2 * len(pieces))],
        {len(pieces): 0} if more else None,
    )[0]


def swap(x, axis, bit):
    n = lax.axis_size(axis)
    return lax.ppermute(x, axis, [(i, i ^ (1 << bit)) for i in range(n)])


def reversed_bits(value, n_bits):
    out = 0
    for b in range(n_bits):
        out = out | (((value >> b) & 1) << (n_bits - 1 - b))
    return out


def step_body(level, side, at, more, total_ref, got_ref, *refs):
    send_out, outside_out = refs[-2:]
    got = got_ref[...].astype(F32)
    total = total_ref[...] + got
    send_out[...] = total.astype(BF16)
    if more:
        refs[-3][...] = total
    if level is None:
        outside_out[...] = jnp.zeros_like(got)
    else:
        outside_out[...] = refs[0][...] + jnp.where(at.bit(*level) == side, got, 0.0)


def step(level, side, at, total, got, *outside, more=True):
    outs = [(total.shape, F32, True)] * more + [(total.shape, BF16, True), (total.shape, F32, True)]
    body = functools.partial(step_body, level, side, at, more)
    results = call(body, [total, got, *outside], [WHOLE] * (2 + len(outside)), outs)
    return results if more else [None, *results]


def last_body(level, side, at, outside_ref, got_ref, own_ref, came_ref, give_out, out):
    outside = outside_ref[...] + jnp.where(at.bit(*level) == side, got_ref[...].astype(F32), 0.0)
    mine = at.y() == side
    give_out[...] = (outside + jnp.where(mine, 0.0, own_ref[...])).astype(BF16)
    out[...] = (outside + jnp.where(mine, came_ref[...].astype(F32), 0.0)).astype(BF16)


def last(level, side, at, outside, got, own, came):
    outs = [(own.shape, BF16, True)] * 2
    return call(functools.partial(last_body, level, side, at), [outside, got, own, came], [WHOLE] * 4, outs)


def scan_states(own, sent, reverse, at):
    side = 0 if reverse else 1
    came = swap(sent, "inner", 0)
    after = yield came
    own = own()
    came = tie(came, *after)
    total, send, outside = step(None, side, at, own, came)
    levels = [("inner", b) for b in range(1, at.i_bits)] + [("outer", b) for b in range(at.o_bits)]
    for n, level in enumerate(levels):
        got = swap(send, *level)
        after = yield got
        got = tie(got, *after)
        if n + 1 < len(levels):
            total, send, outside = step(level, side, at, total, got, outside, more=n + 2 < len(levels))
    give, kept = last(levels[-1], side, at, outside, got, own, came)
    back = swap(give, "inner", 0)
    yield kept, back


def fold(keep, got, axis):
    size = keep.shape[axis] // 2
    low, high = [
        lax.slice_in_dim(keep, at, at + size, axis=axis).astype(F32)
        + lax.slice_in_dim(got, at, at + size, axis=axis).astype(F32)
        for at in (0, size)
    ]
    return high.astype(BF16), low


def fan_body(n_keep, ways, *refs):
    outs = refs[len(refs) - ways :]
    if n_keep == 2:
        rows = [(refs[0], refs[1]), (refs[2], refs[3])]
        totals = [sum(ref[0].astype(F32) for ref in pair) for pair in rows]
    else:
        totals = [sum(ref[i].astype(F32) for ref in refs[: len(refs) - ways]) for i in range(2)]
    size = outs[0].shape[1]
    for i, total in enumerate(totals):
        for j, out in enumerate(outs):
            out[i] = total[j * size : (j + 1) * size].astype(out.dtype)


def fan(n_keep, ways, *arrays):
    _, n, part, cols = arrays[0].shape
    shape = (2, n // ways, part, cols)
    outs = [(shape, F32 if j == 0 else BF16, True) for j in range(ways)]
    return call(functools.partial(fan_body, n_keep, ways), list(arrays), [WHOLE] * len(arrays), outs)


def swap_all(xs, masks):
    n = lax.axis_size("inner")
    return [lax.ppermute(x, "inner", [(i, i ^ mask) for i in range(n)]) for x, mask in zip(xs, masks)]


def bit_groups(i_bits):
    groups = []
    for b in range(1, i_bits, 2):
        if b + 1 < i_bits:
            groups.append([((i >> 1) << b) | ((i & 1) << (b + 1)) for i in range(1, 4)])
        else:
            groups.append([1 << b])
    return groups


def join_body(axis, *refs):
    out = refs[-1]
    size = refs[0].shape[axis]
    for side, ref in enumerate(refs[:-1]):
        at = tuple(pl.ds(side * size, size) if a == axis else slice(None) for a in range(len(ref.shape)))
        out[at] = ref[...]


def join(axis, *arrays):
    shape = tuple(len(arrays) * s if i == axis else s for i, s in enumerate(arrays[0].shape))
    body = functools.partial(join_body, axis)
    return call(body, list(arrays), [WHOLE] * len(arrays), [(shape, BF16, True)])[0]


def split_body(n_pieces, *refs):
    pieces, grad_ref, (p_out, q_out) = refs[:n_pieces], refs[n_pieces], refs[n_pieces + 1 :]
    for j, ref in enumerate(pieces):
        n, part = ref.shape[1:3]
        p_out[:, j * n : (j + 1) * n] = ref[0:1]
        q_out[:, j * n : (j + 1) * n] = ref[1:2]
    for i in range(2):
        q_out[0, n_pieces * n + i] = grad_ref[i * part : (i + 1) * part]


def split(grad, *arrays):
    _, n, part, cols = arrays[0].shape
    n_pieces = len(arrays)
    shapes = [(1, n_pieces * n, part, cols), (1, n_pieces * n + 2, part, cols)]
    return call(
        functools.partial(split_body, n_pieces),
        [*arrays, grad],
        [WHOLE] * (n_pieces + 1),
        [(shape, BF16, True) for shape in shapes],
    )


def rejoin_body(a_ref, b_ref, out, grad_out):
    n, part = out.shape[1:3]
    out[0:1] = a_ref[:, :n]
    out[1:2] = b_ref[:, :n]
    for i in range(2):
        grad_out[i * part : (i + 1) * part] = b_ref[0, n + i]


def rejoin(a, b):
    _, n, part, cols = a.shape
    outs = [((2, n - 2, part, cols), BF16, True), ((2 * part, cols), BF16, True)]
    return call(rejoin_body, [a, b], [WHOLE] * 2, outs)


def local(inputs, queries, keys, values, out_grad, master, moment1, moment2):
    rows_here, width = queries.shape
    d = inputs.shape[1]
    n_outer = lax.axis_size("outer")
    n_inner = lax.axis_size("inner")
    at = Here(n_outer, n_inner)
    i_bits = at.i_bits
    assert n_outer == 4 and i_bits >= 2
    total_tokens = rows_here * n_outer * n_inner
    att_scale = 1.0 / math.sqrt(HD * total_tokens)
    grad_scale = 1.0 / math.sqrt(total_tokens)

    qg_sent = states(out_grad, queries, at, BF16)
    loaded = []

    def own_states():
        loaded.extend(load([out_grad, queries, values], at))
        return loaded[0]

    qg = scan_states(own_states, qg_sent, True, at)
    next(qg)
    qg.send([])
    g, q, v = loaded[1:]
    kv_sent, kv_own, k = both_states(v, keys, at)
    kv = scan_states(lambda: kv_own, kv_sent, False, at)
    kv_stages = i_bits + 2
    done = [kv_own]
    in_own = kv_got = None
    for _ in range(2, i_bits):
        qg.send(done)
        done = []
        if in_own is None:
            in_own = key_inside(tie(g, kv_own), q, v, at, 0, att_scale)
            kv_got = next(kv)
            done = [in_own] + [kv_got] * 1
    qg.send(done)
    qg.send([])
    in_oth = key_inside(tie(g, in_own), q, v, at, 1, att_scale)
    qg_own, qg_oth = qg.send([in_oth])
    turned = turned_inputs(tie(inputs, in_oth), at)

    def kv_next(*after):
        nonlocal kv_stages, kv_got
        if kv_stages:
            kv_stages -= 1
            kv_got = kv.send(list(after))
        return kv_got

    ends = (att_scale, grad_scale)
    in_own = tie(in_own, kv_next())
    far_key, near_key, far_own, near_own = key_product(in_own, v, qg_own, turned, at, 0, (1, 0), *ends)
    keys_own = [(far_key, (0, 1)), (near_key, (0, 0))]
    got_own = swap(far_own, "outer", 0)
    far_key, far_oth = key_product(in_oth, v, qg_oth, turned, at, 1, (1,), *ends)
    got_oth = swap(far_oth, "outer", 0)
    near_key, near_oth = key_product(in_oth, v, qg_oth, turned, at, 1, (0,), *ends)
    pieces = keys_own + [(far_key, (1, 1)), (near_key, (1, 0))]

    p_send, p, q_send, q = cores(at, near_own, near_oth, got_own, got_oth)
    p_got, q_got = swap(p_send, "outer", 1), swap(q_send, "inner", 0)
    kv_next(p_send, q_send)
    p_send, p = fold(p, p_got, 1)
    q_send, q = fold(q, q_got, 0)
    p_got, q_got = swap(p_send, "inner", 0), swap(q_send, "outer", 1)
    query_own, key_grad = query_inside(tie(g, p_send, q_send), k, v, at, 0, att_scale, pieces)
    kv_next(p_send, q_send, query_own)
    groups = bit_groups(i_bits)
    keep, *sends = fan(2, 1 + len(groups[0]), p, p_got, q, q_got)
    sends[0] = tie(sends[0], query_own)
    came = swap_all(sends, groups[0])
    (query_oth,) = query_inside(tie(g, *sends), k, v, at, 1, att_scale)
    for masks in groups[1:]:
        keep, *sends = fan(1, 1 + len(masks), keep, *came)
        came = swap_all(sends, masks)
    while kv_stages > 1:
        kv_next(query_oth)
    grad, weight = adam_own([keep, *came], master, moment1, moment2, at)
    weight = tie(weight, query_oth)
    kv_own, kv_oth = kv_next(weight)

    for masks in reversed(groups[1:]):
        weight = join(1, weight, *swap_all([weight] * len(masks), masks))
    p, q = split(grad, weight, *swap_all([weight] * len(groups[0]), groups[0]))
    p_got, q_got = swap(p, "inner", 0), swap(q, "outer", 1)
    p = join(1, p, p_got)
    q, grad_x = rejoin(q, q_got)
    p, q, kv_oth = lax.optimization_barrier((p, q, kv_oth))
    p_last, q_last = swap(p, "outer", 1), swap(q, "inner", 0)
    p_core, q_core = swap(p, "outer", 0), swap(q, "outer", 0)
    grads = [grad, swap(grad, "outer", 0), grad_x, swap(grad_x, "outer", 0)]
    query_grad = query_side(tie(g, p, q), query_own, query_oth, kv_own, kv_oth, at, att_scale)
    new_master, new_moment1, new_moment2 = adam_all(
        [tie(grads[0], p, q)] + grads[1:], master, moment1, moment2, at, (0, 1, 2, 3)
    )
    n = n_inner // 2
    weights = assemble(
        [(p, (0, (0,), 0, 2 * n)), (q, (1, (0, 2), 0, n)), (p_core, (0, (1,), 0, 2 * n)), (q_core, (1, (1, 3), 0, n))],
        at, None, width,
    )
    done = [weights, query_grad, new_master]
    p_core, q_core = swap(tie(p_last, *done), "outer", 0), swap(tie(q_last, *done), "outer", 0)
    weights = assemble([(p_last, (0, (2,), 0, 2 * n)), (q_last, (1, (0, 2), n, n))], at, weights, width)
    weights = assemble([(p_core, (0, (3,), 0, 2 * n)), (q_core, (1, (1, 3), n, n))], at, weights, width)
    return (query_grad, key_grad, new_master, new_moment1, new_moment2, weights.reshape(d, width))


def solution(mesh):
    tokens = P(("outer", "inner"), None)
    rows = P("inner", None)
    return jax.shard_map(
        local,
        mesh=mesh,
        in_specs=(tokens,) * 5 + (rows,) * 3,
        out_specs=(tokens, tokens, rows, rows, rows, P()),
        check_vma=False,
    )
```

```python
import functools
import math

import jax
import jax.numpy as jnp
from jax import lax
from jax.experimental import pallas as pl
from jax.experimental.pallas import tpu as pltpu
from jax.sharding import PartitionSpec as P

HD = 128
SUB = 256
PAIR = 2 * HD
VMEM = 16 * 1024 * 1024
F32 = jnp.float32
BF16 = jnp.bfloat16
WHOLE = pl.BlockSpec(memory_space=pltpu.VMEM)
HBM = pl.BlockSpec(memory_space=pltpu.HBM)


def mm(a, b, contract):
    return lax.dot_general(a, b, ((contract[:1], contract[1:]), ((), ())), preferred_element_type=F32)


def far(x):
    return pltpu.with_memory_space_constraint(x, pltpu.HBM)


def call(body, args, specs, outs, macs=0, moved=0, scratch=(), aliases=None):
    args = [far(a) if spec is HBM else a for a, spec in zip(args, specs)]
    return pl.pallas_call(
        body,
        in_specs=specs,
        out_specs=[WHOLE if near else HBM for _, _, near in outs],
        out_shape=[(jax.ShapeDtypeStruct if near else pltpu.HBM)(shape, dtype) for shape, dtype, near in outs],
        scratch_shapes=list(scratch),
        input_output_aliases=aliases or {},
        compiler_params=pltpu.CompilerParams(vmem_limit_bytes=VMEM),
        cost_estimate=pl.CostEstimate(flops=2 * macs, bytes_accessed=moved, transcendentals=0),
    )(*args)


def dma(n):
    return pltpu.SemaphoreType.DMA((n,))


def tie(x, *after):
    return lax.optimization_barrier((x, *after))[0] if after else x


class Here:
    def __init__(self, n_outer, n_inner):
        self.i_bits, self.o_bits = (n_inner - 1).bit_length(), (n_outer - 1).bit_length()
        self.n_outer, self.n_inner = n_outer, n_inner

    def group(self, k):
        return lax.axis_index("outer") ^ k

    def block(self, p):
        return lax.axis_index("inner") ^ reversed_bits(p, self.i_bits)

    def position(self, block):
        return reversed_bits(lax.axis_index("inner") ^ block, self.i_bits)

    def bit(self, axis, b):
        return (lax.axis_index(axis) >> b) & 1

    def y(self):
        return self.bit("inner", 0)


def states_body(at, a_hbm, b_hbm, out_ref, a_buf, b_buf, a_sem, b_sem):
    chunks, rows, cols = a_buf.shape
    at = pl.multiple_of((1 - at.y()) * cols, cols)
    copies = []
    for c in range(chunks):
        here = (pl.ds(c * rows, rows), pl.ds(at, cols))
        pair = (
            pltpu.make_async_copy(a_hbm.at[here], a_buf.at[c], a_sem.at[c]),
            pltpu.make_async_copy(b_hbm.at[here], b_buf.at[c], b_sem.at[c]),
        )
        for copy in pair:
            copy.start()
        copies.append(pair)
    sums = [None] * (cols // HD)
    for c in range(chunks):
        for copy in copies[c]:
            copy.wait()
        for j in range(cols // HD):
            here = slice(j * HD, (j + 1) * HD)
            term = mm(a_buf[c, :, here], b_buf[c, :, here], (0, 0))
            sums[j] = term if c == 0 else sums[j] + term
    for j in range(cols // HD):
        out_ref[j] = sums[j].astype(out_ref.dtype)


def states(a, b, at, dtype):
    rows, width = a.shape
    cols = width // 2
    chunks = rows // SUB
    buf = pltpu.VMEM((chunks, SUB, cols), BF16)
    return call(
        functools.partial(states_body, at),
        [a, b],
        [HBM, HBM],
        [((cols // HD, HD, HD), dtype, True)],
        rows * cols * HD,
        4 * rows * cols,
        [buf, buf, dma(chunks), dma(chunks)],
    )[0]


def sums_of(a_ref, b_ref, at, cols, blocks, wait):
    sums = [None] * (cols // HD)
    for b in blocks:
        wait(b)
        for j in range(cols // HD):
            here = (pl.ds(b * SUB, SUB), pl.ds(pl.multiple_of(at * cols + j * HD, HD), HD))
            term = mm(a_ref[here], b_ref[here], (0, 0))
            sums[j] = term if sums[j] is None else sums[j] + term
    return sums


def load_body(n_load, at, *refs):
    sources, out_ref, loads, sem = refs[:n_load], refs[n_load], refs[n_load + 1 : -1], refs[-1]
    rows, width = sources[0].shape
    blocks = rows // SUB
    copies = []
    for b in range(blocks):
        copies.append([])
        for n in range(n_load):
            here = pl.ds(b * SUB, SUB)
            copy = pltpu.make_async_copy(sources[n].at[here, :], loads[n].at[here, :], sem.at[n_load * b + n])
            copy.start()
            copies[b].append(copy)

    def wait(b):
        for copy in copies[b]:
            copy.wait()

    for j, total in enumerate(sums_of(loads[0], loads[1], at.y(), width // 2, range(blocks), wait)):
        out_ref[j] = total


def load(sources, at):
    rows, width = sources[0].shape
    n = len(sources)
    return call(
        functools.partial(load_body, n, at),
        sources,
        [HBM] * n,
        [((width // 2 // HD, HD, HD), F32, True)] + [((rows, width), BF16, True)] * n,
        rows * width // 2 * HD,
        4 * n * rows * width,
        [dma(n * (rows // SUB))],
    )


def both_states_body(at, a_ref, b_hbm, sent_ref, own_ref, b_ref, sem):
    rows, width = a_ref.shape
    blocks = rows // SUB
    copies = []
    for b in range(blocks):
        here = pl.ds(b * SUB, SUB)
        copies.append(pltpu.make_async_copy(b_hbm.at[here, :], b_ref.at[here, :], sem.at[b]))
        copies[b].start()
    for side, ref in ((1 - at.y(), sent_ref), (at.y(), own_ref)):
        wait = (lambda b: copies[b].wait()) if ref is sent_ref else (lambda b: None)
        for j, total in enumerate(sums_of(a_ref, b_ref, side, width // 2, range(blocks), wait)):
            ref[j] = total.astype(ref.dtype)


def both_states(a, b, at):
    rows, width = a.shape
    shape = (width // 2 // HD, HD, HD)
    return call(
        functools.partial(both_states_body, at),
        [a, b],
        [WHOLE, HBM],
        [(shape, BF16, True), (shape, F32, True), ((rows, width), BF16, True)],
        rows * width * HD,
        2 * rows * width,
        [dma(rows // SUB)],
    )


def key_inside_body(scale, other, at, g_ref, q_ref, v_ref, out_ref):
    rows, cols = out_ref.shape
    later = lax.broadcasted_iota(jnp.int32, (SUB, SUB), 1) >= lax.broadcasted_iota(jnp.int32, (SUB, SUB), 0)
    for to in range(0, cols, HD):
        from_ = pl.ds(pl.multiple_of((at.y() ^ other) * cols + to, HD), HD)
        state = None
        for b in reversed(range(rows // SUB)):
            here = (pl.ds(b * SUB, SUB), from_)
            g, q, v = g_ref[here], q_ref[here], v_ref[here]
            scores = jnp.where(later, mm(v, g, (1, 1)), 0.0).astype(BF16)
            total = mm(scores, q, (1, 0))
            if state is not None:
                total = total + mm(v, state.astype(BF16), (1, 0))
            out_ref[b * SUB : (b + 1) * SUB, to : to + HD] = total * scale
            if b:
                term = mm(g, q, (0, 0))
                state = term if state is None else state + term


def query_inside_body(scale, other, at, kinds, g_ref, k_ref, v_ref, *refs):
    pieces = refs[: len(kinds)]
    if kinds:
        out_ref, key_hbm, sem = refs[len(kinds) :]
    else:
        (out_ref,) = refs
    rows, cols = out_ref.shape
    copies = []
    for i, (piece, (piece_other, core)) in enumerate(zip(pieces, kinds)):
        size = piece.shape[1]
        group = (at.y() ^ piece_other) * 2 + (at.bit("outer", 0) ^ core)
        to = pl.ds(pl.multiple_of(group * size, size), size)
        copies.append(pltpu.make_async_copy(piece, key_hbm.at[:, to], sem.at[i]))
        copies[i].start()
    earlier = lax.broadcasted_iota(jnp.int32, (SUB, SUB), 0) >= lax.broadcasted_iota(jnp.int32, (SUB, SUB), 1)
    for to in range(0, cols, HD):
        from_ = pl.ds(pl.multiple_of((at.y() ^ other) * cols + to, HD), HD)
        state = None
        for b in range(rows // SUB):
            here = (pl.ds(b * SUB, SUB), from_)
            g, k, v = g_ref[here], k_ref[here], v_ref[here]
            scores = jnp.where(earlier, mm(g, v, (1, 1)), 0.0).astype(BF16)
            total = mm(scores, k, (1, 0))
            if state is not None:
                total = total + mm(g, state.astype(BF16), (1, 0))
            out_ref[b * SUB : (b + 1) * SUB, to : to + HD] = total * scale
            if b + 1 < rows // SUB:
                term = mm(v, k, (0, 0))
                state = term if state is None else state + term
    for copy in copies:
        copy.wait()


def key_inside(g, q, v, at, other, scale):
    rows, width = g.shape
    cols = width // 2
    return call(
        functools.partial(key_inside_body, scale, other, at),
        [g, q, v],
        [WHOLE] * 3,
        [((rows, cols), F32, True)],
        rows * cols * (2 * SUB + 2 * HD),
        10 * rows * cols,
    )[0]


def query_inside(g, k, v, at, other, scale, pieces=()):
    rows, width = g.shape
    cols = width // 2
    kinds = [kind for _, kind in pieces]
    outs = [((rows, cols), F32, True)] + [((rows, width), BF16, False)] * bool(pieces)
    return call(
        functools.partial(query_inside_body, scale, other, at, kinds),
        [g, k, v] + [piece for piece, _ in pieces],
        [WHOLE] * (3 + len(pieces)),
        outs,
        rows * cols * (2 * SUB + 2 * HD),
        10 * rows * cols,
        [dma(len(pieces))] if pieces else [],
    )


def query_body(scale, at, g_ref, in_own, in_oth, own_ref, oth_ref, out_hbm, buf, sem):
    n, rows, cols = buf.shape
    copies = []
    for other, (in_ref, state_ref) in enumerate(((in_own, own_ref), (in_oth, oth_ref))):
        half = at.y() ^ other
        for p in range(n // 2):
            i = other * (n // 2) + p
            for j in range(cols // HD):
                head = p * (cols // HD) + j
                from_ = pl.multiple_of((half * (n // 2) + p) * cols + j * HD, HD)
                part = mm(g_ref[:, pl.ds(from_, HD)], state_ref[head], (1, 0))
                total = in_ref[:, head * HD : (head + 1) * HD] + part * scale
                buf[i, :, j * HD : (j + 1) * HD] = total.astype(BF16)
            to = pl.ds(pl.multiple_of((half * (n // 2) + p) * cols, cols), cols)
            copies.append(pltpu.make_async_copy(buf.at[i], out_hbm.at[:, to], sem.at[i]))
            copies[i].start()
    for copy in copies:
        copy.wait()


def turned_body(here_at, in_hbm, out_ref, buf, sem):
    size = out_ref.shape[0] // here_at.n_inner
    cols = max(size, HD)
    copies = []
    for n in range(out_ref.shape[0] // cols):
        copy = pltpu.make_async_copy(in_hbm.at[:, pl.ds(n * cols, cols)], buf.at[n], sem.at[n])
        copy.start()
        copies.append(copy)
    for n, copy in enumerate(copies):
        copy.wait()
        turned = buf[n].T
        for j in range(cols // size):
            at = pl.multiple_of(here_at.position(n * (cols // size) + j) * size, size)
            out_ref[pl.ds(at, size), :] = turned[j * size : (j + 1) * size, :]


def turned_inputs(inputs, at):
    rows, width = inputs.shape
    cols = max(width // at.n_inner, HD)
    return call(
        functools.partial(turned_body, at),
        [inputs],
        [HBM],
        [((width, rows), BF16, True)],
        0,
        4 * rows * width,
        [pltpu.VMEM((width // cols, rows, cols), BF16), dma(width // cols)],
    )[0]


def key_product_body(scale, grad_scale, at, other, cores, inside_ref, v_ref, state_ref, turned_ref, *refs):
    n = len(cores)
    cols = refs[0].shape[1]
    heads = cols // HD
    half = at.y() ^ other
    for s, core in enumerate(cores):
        key_ref, out = refs[s], refs[n + s]
        place = at.bit("outer", 0) ^ core
        for j in range(heads):
            head = place * heads + j
            here = pl.ds(pl.multiple_of(head * HD, HD), HD)
            from_ = pl.ds(pl.multiple_of((half * 2 * heads + head) * HD, HD), HD)
            part = mm(v_ref[:, from_], state_ref[head], (1, 0))
            key_ref[:, j * HD : (j + 1) * HD] = (inside_ref[:, here] + part * scale).astype(BF16)
        product = (mm(turned_ref[...], key_ref[...], (1, 0)) * grad_scale).astype(BF16)
        size = product.shape[0] // at.n_inner
        for r in range(at.n_inner):
            for i in range(2):
                out[i, r] = product[r * size + i * (size // 2) : r * size + (i + 1) * (size // 2)]


def key_product(inside, v, states, turned, at, other, cores, scale, grad_scale):
    n = len(cores)
    rows, width = v.shape
    cols = width // at.n_outer
    d = turned.shape[0]
    piece = ((2, at.n_inner, d // at.n_inner // 2, cols), BF16, True)
    return call(
        functools.partial(key_product_body, scale, grad_scale, at, other, cores),
        [inside, v, states, turned],
        [WHOLE] * 4,
        [((rows, cols), BF16, True)] * n + [piece] * n,
        n * cols * rows * (d + HD),
        2 * rows * (d + 4 * n * cols),
    )


def cores_body(at, *refs):
    (n_own, n_oth, g_own, g_oth), (p_send, p_keep, q_send, q_keep) = refs[:4], refs[4:]
    far_own = at.bit("outer", 1) ^ at.y()
    p_own = n_own[0].astype(F32) + g_own[0].astype(F32)
    p_oth = n_oth[0].astype(F32) + g_oth[0].astype(F32)
    p_send[0] = jnp.where(far_own == 1, p_own, p_oth).astype(BF16)
    p_keep[0] = jnp.where(far_own == 1, p_oth, p_own)
    n = n_own.shape[1] // 2
    for side, near, got in ((far_own, n_own, g_own), (1 - far_own, n_oth, g_oth)):
        q_keep[side] = near[1, :n].astype(F32) + got[1, :n].astype(F32)
        q_send[side] = (near[1, n:].astype(F32) + got[1, n:].astype(F32)).astype(BF16)


def cores(at, near_own, near_oth, got_own, got_oth):
    _, n, part, cols = near_own.shape
    one, two = (1, n, part, cols), (2, n // 2, part, cols)
    return call(
        functools.partial(cores_body, at),
        [near_own, near_oth, got_own, got_oth],
        [WHOLE] * 4,
        [(one, BF16, True), (one, F32, True), (two, BF16, True), (two, F32, True)],
    )


def adam(grad, master, moment1, moment2):
    new_moment1 = 0.9 * moment1 + 0.1 * grad
    new_moment2 = 0.95 * moment2 + 0.05 * grad * grad
    new_master = master - 0.01 * (new_moment1 / (jnp.sqrt(new_moment2) + 1e-08) + 0.1 * master)
    return new_master, new_moment1, new_moment2


def adam_own_body(at, n, *refs):
    sums, (master_ref, m1_ref, m2_ref, grad_ref, weight_ref) = refs[:n], refs[n:]
    _, _, part, size = sums[0].shape
    cols = pl.ds(pl.multiple_of(at.group(0) * size, size), size)
    for j in range(2):
        here = slice(j * part, (j + 1) * part)
        grad = sum(ref[j, 0].astype(F32) for ref in sums).astype(BF16)
        grad_ref[here, :] = grad
        new_master, _, _ = adam(grad.astype(F32), master_ref[here, cols], m1_ref[here, cols], m2_ref[here, cols])
        weight_ref[j, 0] = new_master.astype(BF16)


def adam_own(sums, master, moment1, moment2, at):
    shape = sums[0].shape
    _, _, part, cols = shape
    return call(
        functools.partial(adam_own_body, at, len(sums)),
        [*sums, master, moment1, moment2],
        [WHOLE] * (len(sums) + 3),
        [((2 * part, cols), BF16, True), (shape, BF16, True)],
        2 * part * cols,
        48 * part * cols,
    )


def adam_all_body(picks, at, *refs):
    n = len(picks)
    grads, (master_ref, m1_ref, m2_ref) = refs[:n], refs[n : n + 3]
    outs, bufs, sem = refs[n + 3 : n + 6], refs[n + 6 : n + 9], refs[n + 9]
    size = grads[0].shape[1]
    copies = []
    for s in range(n):
        cols = pl.ds(pl.multiple_of(at.group(picks[s]) * size, size), size)
        new = adam(grads[s][...].astype(F32), master_ref[:, cols], m1_ref[:, cols], m2_ref[:, cols])
        for i in range(3):
            bufs[i][s] = new[i]
            copy = pltpu.make_async_copy(bufs[i].at[s], outs[i].at[:, cols], sem.at[s * 3 + i])
            copy.start()
            copies.append(copy)
    for copy in copies:
        copy.wait()


def adam_all(grads, master, moment1, moment2, at, picks):
    n = len(grads)
    rows, cols = grads[0].shape
    return call(
        functools.partial(adam_all_body, picks, at),
        [*grads, master, moment1, moment2],
        [WHOLE] * (n + 3),
        [(master.shape, F32, False)] * 3,
        n * rows * cols,
        26 * n * rows * cols,
        [pltpu.VMEM((n, rows, cols), F32)] * 3 + [dma(3 * n)],
    )


def assemble_start(kinds, at, pieces, out_hbm, bufs, sem):
    copies = []
    for i, (which, groups, start, count) in enumerate(kinds):
        size = pieces[i].shape[-1]
        for s, k in enumerate(groups):
            cols = pl.ds(pl.multiple_of(at.group(k) * size, size), size)
            for r in range(count):
                block = at.block(start + r)
                if which:
                    bufs[i][s, block // 2] = pieces[i][s, r]
                else:
                    bufs[i][s, block // 2, block % 2] = pieces[i][s, r]
            if which:
                goal = out_hbm.at[:, at.block(start) % 2, which, :, cols]
            else:
                goal = out_hbm.at[:, :, which, :, cols]
            copy = pltpu.make_async_copy(bufs[i].at[s], goal, sem.at[2 * i + s])
            copy.start()
            copies.append(copy)
    return copies


def assemble_body(kinds, at, *refs):
    n = len(kinds)
    for copy in assemble_start(kinds, at, refs[:n], refs[-n - 2], refs[-n - 1 : -1], refs[-1]):
        copy.wait()


def assemble_scratch(pieces, at):
    part, cols = pieces[0][0].shape[2:]
    bufs = [
        pltpu.VMEM((len(groups), at.n_inner // 2) + (() if which else (2,)) + (part, cols), BF16)
        for _, (which, groups, _, _) in pieces
    ]
    return bufs + [dma(2 * len(pieces))]


def finish_body(scale, at, kinds, g_ref, in_own, in_oth, own_ref, oth_ref, *refs):
    n = len(kinds)
    pieces, (out_hbm, weights_hbm, buf, sem) = refs[:n], refs[n : n + 4]
    copies = assemble_start(kinds, at, pieces, weights_hbm, refs[n + 4 : -1], refs[-1])
    query_body(scale, at, g_ref, in_own, in_oth, own_ref, oth_ref, out_hbm, buf, sem)
    for copy in copies:
        copy.wait()


def finish(g, in_own, in_oth, own, oth, at, scale, pieces):
    rows, width = g.shape
    n = width // PAIR
    part = pieces[0][0].shape[2]
    return call(
        functools.partial(finish_body, scale, at, [kind for _, kind in pieces]),
        [g, in_own, in_oth, own, oth, *[array for array, _ in pieces]],
        [WHOLE] * (5 + len(pieces)),
        [((rows, width), BF16, False), ((at.n_inner // 2, 2, 2, part, width), BF16, False)],
        rows * width * HD,
        8 * rows * width,
        [pltpu.VMEM((n, rows, PAIR), BF16), dma(n)] + assemble_scratch(pieces, at),
    )


def assemble(pieces, at, before, width):
    n_inner = at.n_inner
    part, cols = pieces[0][0].shape[2:]
    kinds = [kind for _, kind in pieces]
    more = [] if before is None else [before]
    return call(
        functools.partial(assemble_body, kinds, at),
        [array for array, _ in pieces] + more,
        [WHOLE] * len(pieces) + [HBM] * len(more),
        [((n_inner // 2, 2, 2, part, width), BF16, False)],
        0,
        4 * sum(array.size for array, _ in pieces),
        assemble_scratch(pieces, at),
        {len(pieces): 0} if more else None,
    )[0]


def swap(x, axis, bit):
    n = lax.axis_size(axis)
    return lax.ppermute(x, axis, [(i, i ^ (1 << bit)) for i in range(n)])


def reversed_bits(value, n_bits):
    out = 0
    for b in range(n_bits):
        out = out | (((value >> b) & 1) << (n_bits - 1 - b))
    return out


def step_body(level, side, at, more, total_ref, got_ref, *refs):
    send_out, outside_out = refs[-2:]
    got = got_ref[...].astype(F32)
    total = total_ref[...] + got
    send_out[...] = total.astype(BF16)
    if more:
        refs[-3][...] = total
    if level is None:
        outside_out[...] = jnp.zeros_like(got)
    else:
        outside_out[...] = refs[0][...] + jnp.where(at.bit(*level) == side, got, 0.0)


def step(level, side, at, total, got, *outside, more=True):
    outs = [(total.shape, F32, True)] * more + [(total.shape, BF16, True), (total.shape, F32, True)]
    body = functools.partial(step_body, level, side, at, more)
    results = call(body, [total, got, *outside], [WHOLE] * (2 + len(outside)), outs)
    return results if more else [None, *results]


def last_body(level, side, at, outside_ref, got_ref, own_ref, came_ref, give_out, out):
    outside = outside_ref[...] + jnp.where(at.bit(*level) == side, got_ref[...].astype(F32), 0.0)
    mine = at.y() == side
    give_out[...] = (outside + jnp.where(mine, 0.0, own_ref[...])).astype(BF16)
    out[...] = (outside + jnp.where(mine, came_ref[...].astype(F32), 0.0)).astype(BF16)


def last(level, side, at, outside, got, own, came):
    outs = [(own.shape, BF16, True)] * 2
    return call(functools.partial(last_body, level, side, at), [outside, got, own, came], [WHOLE] * 4, outs)


def scan_states(own, sent, reverse, at):
    side = 0 if reverse else 1
    came = swap(sent, "inner", 0)
    after = yield came
    own = own()
    came = tie(came, *after)
    total, send, outside = step(None, side, at, own, came)
    levels = [("inner", b) for b in range(1, at.i_bits)] + [("outer", b) for b in range(at.o_bits)]
    for n, level in enumerate(levels):
        got = swap(send, *level)
        after = yield got
        got = tie(got, *after)
        if n + 1 < len(levels):
            total, send, outside = step(level, side, at, total, got, outside, more=n + 2 < len(levels))
    give, kept = last(levels[-1], side, at, outside, got, own, came)
    back = swap(give, "inner", 0)
    yield kept, back


def fold(keep, got, axis):
    size = keep.shape[axis] // 2
    low, high = [
        lax.slice_in_dim(keep, at, at + size, axis=axis).astype(F32)
        + lax.slice_in_dim(got, at, at + size, axis=axis).astype(F32)
        for at in (0, size)
    ]
    return high.astype(BF16), low


def fan_body(n_keep, ways, *refs):
    outs = refs[len(refs) - ways :]
    if n_keep == 2:
        rows = [(refs[0], refs[1]), (refs[2], refs[3])]
        totals = [sum(ref[0].astype(F32) for ref in pair) for pair in rows]
    else:
        totals = [sum(ref[i].astype(F32) for ref in refs[: len(refs) - ways]) for i in range(2)]
    size = outs[0].shape[1]
    for i, total in enumerate(totals):
        for j, out in enumerate(outs):
            out[i] = total[j * size : (j + 1) * size].astype(out.dtype)


def fan(n_keep, ways, *arrays):
    _, n, part, cols = arrays[0].shape
    shape = (2, n // ways, part, cols)
    outs = [(shape, F32 if j == 0 else BF16, True) for j in range(ways)]
    return call(functools.partial(fan_body, n_keep, ways), list(arrays), [WHOLE] * len(arrays), outs)


def swap_all(xs, masks):
    n = lax.axis_size("inner")
    return [lax.ppermute(x, "inner", [(i, i ^ mask) for i in range(n)]) for x, mask in zip(xs, masks)]


def bit_groups(i_bits):
    groups = []
    for b in range(1, i_bits, 2):
        if b + 1 < i_bits:
            groups.append([((i >> 1) << b) | ((i & 1) << (b + 1)) for i in range(1, 4)])
        else:
            groups.append([1 << b])
    return groups


def join_body(axis, *refs):
    out = refs[-1]
    size = refs[0].shape[axis]
    for side, ref in enumerate(refs[:-1]):
        at = tuple(pl.ds(side * size, size) if a == axis else slice(None) for a in range(len(ref.shape)))
        out[at] = ref[...]


def join(axis, *arrays):
    shape = tuple(len(arrays) * s if i == axis else s for i, s in enumerate(arrays[0].shape))
    body = functools.partial(join_body, axis)
    return call(body, list(arrays), [WHOLE] * len(arrays), [(shape, BF16, True)])[0]


def split_body(n_pieces, *refs):
    pieces, grad_ref, (p_out, q_out) = refs[:n_pieces], refs[n_pieces], refs[n_pieces + 1 :]
    for j, ref in enumerate(pieces):
        n, part = ref.shape[1:3]
        p_out[:, j * n : (j + 1) * n] = ref[0:1]
        q_out[:, j * n : (j + 1) * n] = ref[1:2]
    for i in range(2):
        q_out[0, n_pieces * n + i] = grad_ref[i * part : (i + 1) * part]


def split(grad, *arrays):
    _, n, part, cols = arrays[0].shape
    n_pieces = len(arrays)
    shapes = [(1, n_pieces * n, part, cols), (1, n_pieces * n + 2, part, cols)]
    return call(
        functools.partial(split_body, n_pieces),
        [*arrays, grad],
        [WHOLE] * (n_pieces + 1),
        [(shape, BF16, True) for shape in shapes],
    )


def rejoin_body(a_ref, b_ref, out, grad_out):
    n, part = out.shape[1:3]
    out[0:1] = a_ref[:, :n]
    out[1:2] = b_ref[:, :n]
    for i in range(2):
        grad_out[i * part : (i + 1) * part] = b_ref[0, n + i]


def rejoin(a, b):
    _, n, part, cols = a.shape
    outs = [((2, n - 2, part, cols), BF16, True), ((2 * part, cols), BF16, True)]
    return call(rejoin_body, [a, b], [WHOLE] * 2, outs)


def local(inputs, queries, keys, values, out_grad, master, moment1, moment2):
    rows_here, width = queries.shape
    d = inputs.shape[1]
    n_outer = lax.axis_size("outer")
    n_inner = lax.axis_size("inner")
    at = Here(n_outer, n_inner)
    i_bits = at.i_bits
    assert n_outer == 4 and i_bits >= 2
    total_tokens = rows_here * n_outer * n_inner
    att_scale = 1.0 / math.sqrt(HD * total_tokens)
    grad_scale = 1.0 / math.sqrt(total_tokens)

    qg_sent = states(out_grad, queries, at, BF16)
    loaded = []

    def own_states():
        loaded.extend(load([out_grad, queries, values], at))
        return loaded[0]

    qg = scan_states(own_states, qg_sent, True, at)
    next(qg)
    qg.send([])
    g, q, v = loaded[1:]
    kv_sent, kv_own, k = both_states(v, keys, at)
    kv = scan_states(lambda: kv_own, kv_sent, False, at)
    kv_stages = i_bits + 2
    done = [kv_own]
    in_own = kv_got = None
    for _ in range(2, i_bits):
        qg.send(done)
        done = []
        if in_own is None:
            in_own = key_inside(tie(g, kv_own), q, v, at, 0, att_scale)
            kv_got = next(kv)
            done = [in_own] + [kv_got] * 1
    qg.send(done)
    qg.send([])
    in_oth = key_inside(tie(g, in_own), q, v, at, 1, att_scale)
    qg_own, qg_oth = qg.send([in_oth])
    turned = turned_inputs(tie(inputs, in_oth), at)

    def kv_next(*after):
        nonlocal kv_stages, kv_got
        if kv_stages:
            kv_stages -= 1
            kv_got = kv.send(list(after))
        return kv_got

    ends = (att_scale, grad_scale)
    in_own = tie(in_own, kv_next())
    far_key, near_key, far_own, near_own = key_product(in_own, v, qg_own, turned, at, 0, (1, 0), *ends)
    keys_own = [(far_key, (0, 1)), (near_key, (0, 0))]
    got_own = swap(far_own, "outer", 0)
    far_key, far_oth = key_product(in_oth, v, qg_oth, turned, at, 1, (1,), *ends)
    got_oth = swap(far_oth, "outer", 0)
    near_key, near_oth = key_product(in_oth, v, qg_oth, turned, at, 1, (0,), *ends)
    pieces = keys_own + [(far_key, (1, 1)), (near_key, (1, 0))]

    p_send, p, q_send, q = cores(at, near_own, near_oth, got_own, got_oth)
    p_got, q_got = swap(p_send, "outer", 1), swap(q_send, "inner", 0)
    kv_next(p_send, q_send)
    p_send, p = fold(p, p_got, 1)
    q_send, q = fold(q, q_got, 0)
    p_got, q_got = swap(p_send, "inner", 0), swap(q_send, "outer", 1)
    query_own, key_grad = query_inside(tie(g, p_send, q_send), k, v, at, 0, att_scale, pieces)
    kv_next(p_send, q_send, query_own)
    groups = bit_groups(i_bits)
    keep, *sends = fan(2, 1 + len(groups[0]), p, p_got, q, q_got)
    sends[0] = tie(sends[0], query_own)
    came = swap_all(sends, groups[0])
    (query_oth,) = query_inside(tie(g, *sends), k, v, at, 1, att_scale)
    for masks in groups[1:]:
        keep, *sends = fan(1, 1 + len(masks), keep, *came)
        came = swap_all(sends, masks)
    while kv_stages > 1:
        kv_next(query_oth)
    grad, weight = adam_own([keep, *came], master, moment1, moment2, at)
    weight = tie(weight, query_oth)
    kv_own, kv_oth = kv_next(weight)

    for masks in reversed(groups[1:]):
        weight = join(1, weight, *swap_all([weight] * len(masks), masks))
    p, q = split(grad, weight, *swap_all([weight] * len(groups[0]), groups[0]))
    p_got, q_got = swap(p, "inner", 0), swap(q, "outer", 1)
    p = join(1, p, p_got)
    q, grad_x = rejoin(q, q_got)
    p, q, kv_oth = lax.optimization_barrier((p, q, kv_oth))
    p_last, q_last = swap(p, "outer", 1), swap(q, "inner", 0)
    p_core, q_core = swap(p, "outer", 0), swap(q, "outer", 0)
    grads = [grad, swap(grad, "outer", 0), grad_x, swap(grad_x, "outer", 0)]
    n = n_inner // 2
    query_grad, weights = finish(
        tie(g, p, q), query_own, query_oth, kv_own, kv_oth, at, att_scale,
        [(p, (0, (0,), 0, 2 * n)), (q, (1, (0, 2), 0, n))],
    )
    new_master, new_moment1, new_moment2 = adam_all(
        [tie(grads[0], weights)] + grads[1:], master, moment1, moment2, at, (0, 1, 2, 3)
    )
    p_last, q_last, p_core, q_core, *_ = lax.optimization_barrier(
        (p_last, q_last, p_core, q_core, weights, query_grad, new_master)
    )
    p_end, q_end = swap(p_last, "outer", 0), swap(q_last, "outer", 0)
    weights = assemble(
        [
            (p_last, (0, (2,), 0, 2 * n)),
            (q_last, (1, (0, 2), n, n)),
            (p_core, (0, (1,), 0, 2 * n)),
            (q_core, (1, (1, 3), 0, n)),
        ],
        at, weights, width,
    )
    weights = assemble([(p_end, (0, (3,), 0, 2 * n)), (q_end, (1, (1, 3), n, n))], at, weights, width)
    return (query_grad, key_grad, new_master, new_moment1, new_moment2, weights.reshape(d, width))


def solution(mesh):
    tokens = P(("outer", "inner"), None)
    rows = P("inner", None)
    return jax.shard_map(
        local,
        mesh=mesh,
        in_specs=(tokens,) * 5 + (rows,) * 3,
        out_specs=(tokens, tokens, rows, rows, rows, P()),
        check_vma=False,
    )
```

```python
import functools
import math

import jax
import jax.numpy as jnp
from jax import lax
from jax.experimental import pallas as pl
from jax.experimental.pallas import tpu as pltpu
from jax.sharding import PartitionSpec as P

HD = 128
SUB = 256
PAIR = 2 * HD
VMEM = 16 * 1024 * 1024
F32 = jnp.float32
BF16 = jnp.bfloat16
WHOLE = pl.BlockSpec(memory_space=pltpu.VMEM)
HBM = pl.BlockSpec(memory_space=pltpu.HBM)


def mm(a, b, contract):
    return lax.dot_general(a, b, ((contract[:1], contract[1:]), ((), ())), preferred_element_type=F32)


def far(x):
    return pltpu.with_memory_space_constraint(x, pltpu.HBM)


def call(body, args, specs, outs, macs=0, moved=0, scratch=(), aliases=None):
    args = [far(a) if spec is HBM else a for a, spec in zip(args, specs)]
    return pl.pallas_call(
        body,
        in_specs=specs,
        out_specs=[WHOLE if near else HBM for _, _, near in outs],
        out_shape=[(jax.ShapeDtypeStruct if near else pltpu.HBM)(shape, dtype) for shape, dtype, near in outs],
        scratch_shapes=list(scratch),
        input_output_aliases=aliases or {},
        compiler_params=pltpu.CompilerParams(vmem_limit_bytes=VMEM),
        cost_estimate=pl.CostEstimate(flops=2 * macs, bytes_accessed=moved, transcendentals=0),
    )(*args)


def dma(n):
    return pltpu.SemaphoreType.DMA((n,))


def tie(x, *after):
    return lax.optimization_barrier((x, *after))[0] if after else x


class Here:
    def __init__(self, n_outer, n_inner):
        self.i_bits, self.o_bits = (n_inner - 1).bit_length(), (n_outer - 1).bit_length()
        self.n_outer, self.n_inner = n_outer, n_inner

    def group(self, k):
        return lax.axis_index("outer") ^ k

    def block(self, p):
        return lax.axis_index("inner") ^ reversed_bits(p, self.i_bits)

    def position(self, block):
        return reversed_bits(lax.axis_index("inner") ^ block, self.i_bits)

    def bit(self, axis, b):
        return (lax.axis_index(axis) >> b) & 1

    def y(self):
        return self.bit("inner", 0)


def states_body(at, a_hbm, b_hbm, out_ref, a_buf, b_buf, a_sem, b_sem):
    chunks, rows, cols = a_buf.shape
    at = pl.multiple_of((1 - at.y()) * cols, cols)
    copies = []
    for c in range(chunks):
        here = (pl.ds(c * rows, rows), pl.ds(at, cols))
        pair = (
            pltpu.make_async_copy(a_hbm.at[here], a_buf.at[c], a_sem.at[c]),
            pltpu.make_async_copy(b_hbm.at[here], b_buf.at[c], b_sem.at[c]),
        )
        for copy in pair:
            copy.start()
        copies.append(pair)
    sums = [None] * (cols // HD)
    for c in range(chunks):
        for copy in copies[c]:
            copy.wait()
        for j in range(cols // HD):
            here = slice(j * HD, (j + 1) * HD)
            term = mm(a_buf[c, :, here], b_buf[c, :, here], (0, 0))
            sums[j] = term if c == 0 else sums[j] + term
    for j in range(cols // HD):
        out_ref[j] = sums[j].astype(out_ref.dtype)


def states(a, b, at, dtype):
    rows, width = a.shape
    cols = width // 2
    chunks = rows // SUB
    buf = pltpu.VMEM((chunks, SUB, cols), BF16)
    return call(
        functools.partial(states_body, at),
        [a, b],
        [HBM, HBM],
        [((cols // HD, HD, HD), dtype, True)],
        rows * cols * HD,
        4 * rows * cols,
        [buf, buf, dma(chunks), dma(chunks)],
    )[0]


def sums_of(a_ref, b_ref, at, cols, blocks, wait):
    sums = [None] * (cols // HD)
    for b in blocks:
        wait(b)
        for j in range(cols // HD):
            here = (pl.ds(b * SUB, SUB), pl.ds(pl.multiple_of(at * cols + j * HD, HD), HD))
            term = mm(a_ref[here], b_ref[here], (0, 0))
            sums[j] = term if sums[j] is None else sums[j] + term
    return sums


def load_body(n_load, at, *refs):
    sources, out_ref, loads, sem = refs[:n_load], refs[n_load], refs[n_load + 1 : -1], refs[-1]
    rows, width = sources[0].shape
    blocks = rows // SUB
    copies = []
    for b in range(blocks):
        copies.append([])
        for n in range(n_load):
            here = pl.ds(b * SUB, SUB)
            copy = pltpu.make_async_copy(sources[n].at[here, :], loads[n].at[here, :], sem.at[n_load * b + n])
            copy.start()
            copies[b].append(copy)

    def wait(b):
        for copy in copies[b]:
            copy.wait()

    for j, total in enumerate(sums_of(loads[0], loads[1], at.y(), width // 2, range(blocks), wait)):
        out_ref[j] = total


def load(sources, at):
    rows, width = sources[0].shape
    n = len(sources)
    return call(
        functools.partial(load_body, n, at),
        sources,
        [HBM] * n,
        [((width // 2 // HD, HD, HD), F32, True)] + [((rows, width), BF16, True)] * n,
        rows * width // 2 * HD,
        4 * n * rows * width,
        [dma(n * (rows // SUB))],
    )


def half_states_body(at, other, n_load, a_ref, b_ref, out_ref, *refs):
    rows, width = a_ref.shape
    blocks = rows // SUB
    source = b_ref
    copies = []
    if n_load:
        source, sem = refs
        for b in range(blocks):
            here = pl.ds(b * SUB, SUB)
            copies.append(pltpu.make_async_copy(b_ref.at[here, :], source.at[here, :], sem.at[b]))
            copies[b].start()
    wait = (lambda b: copies[b].wait()) if n_load else (lambda b: None)
    for j, total in enumerate(sums_of(a_ref, source, at.y() ^ other, width // 2, range(blocks), wait)):
        out_ref[j] = total.astype(out_ref.dtype)


def half_states(a, b, at, other, dtype, n_load):
    rows, width = a.shape
    return call(
        functools.partial(half_states_body, at, other, n_load),
        [a, b],
        [WHOLE, HBM if n_load else WHOLE],
        [((width // 2 // HD, HD, HD), dtype, True)] + [((rows, width), BF16, True)] * n_load,
        rows * width * HD // 2,
        2 * rows * width,
        [dma(rows // SUB)] * n_load,
    )


def key_inside_body(scale, other, at, g_ref, q_ref, v_ref, out_ref):
    rows, cols = out_ref.shape
    later = lax.broadcasted_iota(jnp.int32, (SUB, SUB), 1) >= lax.broadcasted_iota(jnp.int32, (SUB, SUB), 0)
    for to in range(0, cols, HD):
        from_ = pl.ds(pl.multiple_of((at.y() ^ other) * cols + to, HD), HD)
        state = None
        for b in reversed(range(rows // SUB)):
            here = (pl.ds(b * SUB, SUB), from_)
            g, q, v = g_ref[here], q_ref[here], v_ref[here]
            scores = jnp.where(later, mm(v, g, (1, 1)), 0.0).astype(BF16)
            total = mm(scores, q, (1, 0))
            if state is not None:
                total = total + mm(v, state.astype(BF16), (1, 0))
            out_ref[b * SUB : (b + 1) * SUB, to : to + HD] = total * scale
            if b:
                term = mm(g, q, (0, 0))
                state = term if state is None else state + term


def query_inside_body(scale, other, at, kinds, g_ref, k_ref, v_ref, *refs):
    pieces = refs[: len(kinds)]
    if kinds:
        out_ref, key_hbm, sem = refs[len(kinds) :]
    else:
        (out_ref,) = refs
    rows, cols = out_ref.shape
    copies = []
    for i, (piece, (piece_other, core)) in enumerate(zip(pieces, kinds)):
        size = piece.shape[1]
        group = (at.y() ^ piece_other) * 2 + (at.bit("outer", 0) ^ core)
        to = pl.ds(pl.multiple_of(group * size, size), size)
        copies.append(pltpu.make_async_copy(piece, key_hbm.at[:, to], sem.at[i]))
        copies[i].start()
    earlier = lax.broadcasted_iota(jnp.int32, (SUB, SUB), 0) >= lax.broadcasted_iota(jnp.int32, (SUB, SUB), 1)
    for to in range(0, cols, HD):
        from_ = pl.ds(pl.multiple_of((at.y() ^ other) * cols + to, HD), HD)
        state = None
        for b in range(rows // SUB):
            here = (pl.ds(b * SUB, SUB), from_)
            g, k, v = g_ref[here], k_ref[here], v_ref[here]
            scores = jnp.where(earlier, mm(g, v, (1, 1)), 0.0).astype(BF16)
            total = mm(scores, k, (1, 0))
            if state is not None:
                total = total + mm(g, state.astype(BF16), (1, 0))
            out_ref[b * SUB : (b + 1) * SUB, to : to + HD] = total * scale
            if b + 1 < rows // SUB:
                term = mm(v, k, (0, 0))
                state = term if state is None else state + term
    for copy in copies:
        copy.wait()


def key_inside(g, q, v, at, other, scale):
    rows, width = g.shape
    cols = width // 2
    return call(
        functools.partial(key_inside_body, scale, other, at),
        [g, q, v],
        [WHOLE] * 3,
        [((rows, cols), F32, True)],
        rows * cols * (2 * SUB + 2 * HD),
        10 * rows * cols,
    )[0]


def query_inside(g, k, v, at, other, scale, pieces=()):
    rows, width = g.shape
    cols = width // 2
    kinds = [kind for _, kind in pieces]
    outs = [((rows, cols), F32, True)] + [((rows, width), BF16, False)] * bool(pieces)
    return call(
        functools.partial(query_inside_body, scale, other, at, kinds),
        [g, k, v] + [piece for piece, _ in pieces],
        [WHOLE] * (3 + len(pieces)),
        outs,
        rows * cols * (2 * SUB + 2 * HD),
        10 * rows * cols,
        [dma(len(pieces))] if pieces else [],
    )


def query_body(scale, at, g_ref, in_own, in_oth, own_ref, oth_ref, out_hbm, buf, sem):
    n, rows, cols = buf.shape
    copies = []
    for other, (in_ref, state_ref) in enumerate(((in_own, own_ref), (in_oth, oth_ref))):
        half = at.y() ^ other
        for p in range(n // 2):
            i = other * (n // 2) + p
            for j in range(cols // HD):
                head = p * (cols // HD) + j
                from_ = pl.multiple_of((half * (n // 2) + p) * cols + j * HD, HD)
                part = mm(g_ref[:, pl.ds(from_, HD)], state_ref[head], (1, 0))
                total = in_ref[:, head * HD : (head + 1) * HD] + part * scale
                buf[i, :, j * HD : (j + 1) * HD] = total.astype(BF16)
            to = pl.ds(pl.multiple_of((half * (n // 2) + p) * cols, cols), cols)
            copies.append(pltpu.make_async_copy(buf.at[i], out_hbm.at[:, to], sem.at[i]))
            copies[i].start()
    for copy in copies:
        copy.wait()


def turned_body(here_at, in_hbm, out_ref, buf, sem):
    size = out_ref.shape[0] // here_at.n_inner
    cols = max(size, HD)
    copies = []
    for n in range(out_ref.shape[0] // cols):
        copy = pltpu.make_async_copy(in_hbm.at[:, pl.ds(n * cols, cols)], buf.at[n], sem.at[n])
        copy.start()
        copies.append(copy)
    for n, copy in enumerate(copies):
        copy.wait()
        turned = buf[n].T
        for j in range(cols // size):
            at = pl.multiple_of(here_at.position(n * (cols // size) + j) * size, size)
            out_ref[pl.ds(at, size), :] = turned[j * size : (j + 1) * size, :]


def turned_inputs(inputs, at):
    rows, width = inputs.shape
    cols = max(width // at.n_inner, HD)
    return call(
        functools.partial(turned_body, at),
        [inputs],
        [HBM],
        [((width, rows), BF16, True)],
        0,
        4 * rows * width,
        [pltpu.VMEM((width // cols, rows, cols), BF16), dma(width // cols)],
    )[0]


def key_product_body(scale, grad_scale, at, other, cores, inside_ref, v_ref, state_ref, turned_ref, *refs):
    n = len(cores)
    cols = refs[0].shape[1]
    heads = cols // HD
    half = at.y() ^ other
    for s, core in enumerate(cores):
        key_ref, out = refs[s], refs[n + s]
        place = at.bit("outer", 0) ^ core
        for j in range(heads):
            head = place * heads + j
            here = pl.ds(pl.multiple_of(head * HD, HD), HD)
            from_ = pl.ds(pl.multiple_of((half * 2 * heads + head) * HD, HD), HD)
            part = mm(v_ref[:, from_], state_ref[head], (1, 0))
            key_ref[:, j * HD : (j + 1) * HD] = (inside_ref[:, here] + part * scale).astype(BF16)
        product = (mm(turned_ref[...], key_ref[...], (1, 0)) * grad_scale).astype(BF16)
        size = product.shape[0] // at.n_inner
        for r in range(at.n_inner):
            for i in range(2):
                out[i, r] = product[r * size + i * (size // 2) : r * size + (i + 1) * (size // 2)]


def key_product(inside, v, states, turned, at, other, cores, scale, grad_scale):
    n = len(cores)
    rows, width = v.shape
    cols = width // at.n_outer
    d = turned.shape[0]
    piece = ((2, at.n_inner, d // at.n_inner // 2, cols), BF16, True)
    return call(
        functools.partial(key_product_body, scale, grad_scale, at, other, cores),
        [inside, v, states, turned],
        [WHOLE] * 4,
        [((rows, cols), BF16, True)] * n + [piece] * n,
        n * cols * rows * (d + HD),
        2 * rows * (d + 4 * n * cols),
    )


def cores_body(at, *refs):
    (n_own, n_oth, g_own, g_oth), (p_send, p_keep, q_send, q_keep) = refs[:4], refs[4:]
    far_own = at.bit("outer", 1) ^ at.y()
    p_own = n_own[0].astype(F32) + g_own[0].astype(F32)
    p_oth = n_oth[0].astype(F32) + g_oth[0].astype(F32)
    p_send[0] = jnp.where(far_own == 1, p_own, p_oth).astype(BF16)
    p_keep[0] = jnp.where(far_own == 1, p_oth, p_own)
    n = n_own.shape[1] // 2
    for side, near, got in ((far_own, n_own, g_own), (1 - far_own, n_oth, g_oth)):
        q_keep[side] = near[1, :n].astype(F32) + got[1, :n].astype(F32)
        q_send[side] = (near[1, n:].astype(F32) + got[1, n:].astype(F32)).astype(BF16)


def cores(at, near_own, near_oth, got_own, got_oth):
    _, n, part, cols = near_own.shape
    one, two = (1, n, part, cols), (2, n // 2, part, cols)
    return call(
        functools.partial(cores_body, at),
        [near_own, near_oth, got_own, got_oth],
        [WHOLE] * 4,
        [(one, BF16, True), (one, F32, True), (two, BF16, True), (two, F32, True)],
    )


def adam(grad, master, moment1, moment2):
    new_moment1 = 0.9 * moment1 + 0.1 * grad
    new_moment2 = 0.95 * moment2 + 0.05 * grad * grad
    new_master = master - 0.01 * (new_moment1 / (jnp.sqrt(new_moment2) + 1e-08) + 0.1 * master)
    return new_master, new_moment1, new_moment2


def adam_own_body(at, n, *refs):
    sums, (master_ref, m1_ref, m2_ref, grad_ref, weight_ref) = refs[:n], refs[n:]
    _, _, part, size = sums[0].shape
    cols = pl.ds(pl.multiple_of(at.group(0) * size, size), size)
    for j in range(2):
        here = slice(j * part, (j + 1) * part)
        grad = sum(ref[j, 0].astype(F32) for ref in sums).astype(BF16)
        grad_ref[here, :] = grad
        new_master, _, _ = adam(grad.astype(F32), master_ref[here, cols], m1_ref[here, cols], m2_ref[here, cols])
        weight_ref[j, 0] = new_master.astype(BF16)


def adam_own(sums, master, moment1, moment2, at):
    shape = sums[0].shape
    _, _, part, cols = shape
    return call(
        functools.partial(adam_own_body, at, len(sums)),
        [*sums, master, moment1, moment2],
        [WHOLE] * (len(sums) + 3),
        [((2 * part, cols), BF16, True), (shape, BF16, True)],
        2 * part * cols,
        48 * part * cols,
    )


def adam_all_body(picks, at, own_ref, core_ref, master_ref, m1_ref, m2_ref, *refs):
    outs, bufs, sem = refs[:3], refs[3:6], refs[6]
    size = own_ref.shape[2]
    copies = []
    for s, pick in enumerate(picks):
        grad = (own_ref if s < 2 else core_ref)[s % 2].astype(F32)
        cols = pl.ds(pl.multiple_of(at.group(pick) * size, size), size)
        new = adam(grad, master_ref[:, cols], m1_ref[:, cols], m2_ref[:, cols])
        for i in range(3):
            bufs[i][s] = new[i]
            copy = pltpu.make_async_copy(bufs[i].at[s], outs[i].at[:, cols], sem.at[s * 3 + i])
            copy.start()
            copies.append(copy)
    for copy in copies:
        copy.wait()


def adam_all(own, core, master, moment1, moment2, at, picks):
    n = len(picks)
    _, rows, cols = own.shape
    return call(
        functools.partial(adam_all_body, picks, at),
        [own, core, master, moment1, moment2],
        [WHOLE] * 5,
        [(master.shape, F32, False)] * 3,
        n * rows * cols,
        26 * n * rows * cols,
        [pltpu.VMEM((n, rows, cols), F32)] * 3 + [dma(3 * n)],
    )


def assemble_start(kinds, at, pieces, out_hbm, bufs, sem):
    copies = []
    for i, (which, groups, start, count) in enumerate(kinds):
        size = pieces[i].shape[-1]
        for s, k in enumerate(groups):
            cols = pl.ds(pl.multiple_of(at.group(k) * size, size), size)
            for r in range(count):
                block = at.block(start + r)
                if which:
                    bufs[i][s, block // 2] = pieces[i][s, r]
                else:
                    bufs[i][s, block // 2, block % 2] = pieces[i][s, r]
            if which:
                goal = out_hbm.at[:, at.block(start) % 2, which, :, cols]
            else:
                goal = out_hbm.at[:, :, which, :, cols]
            copy = pltpu.make_async_copy(bufs[i].at[s], goal, sem.at[2 * i + s])
            copy.start()
            copies.append(copy)
    return copies


def assemble_body(kinds, at, *refs):
    n = len(kinds)
    for copy in assemble_start(kinds, at, refs[:n], refs[-n - 2], refs[-n - 1 : -1], refs[-1]):
        copy.wait()


def assemble_scratch(pieces, at):
    part, cols = pieces[0][0].shape[2:]
    bufs = [
        pltpu.VMEM((len(groups), at.n_inner // 2) + (() if which else (2,)) + (part, cols), BF16)
        for _, (which, groups, _, _) in pieces
    ]
    return bufs + [dma(2 * len(pieces))]


def finish_body(scale, at, kinds, g_ref, in_own, in_oth, own_ref, oth_ref, *refs):
    n = len(kinds)
    pieces, (out_hbm, weights_hbm, buf, sem) = refs[:n], refs[n : n + 4]
    copies = assemble_start(kinds, at, pieces, weights_hbm, refs[n + 4 : -1], refs[-1])
    query_body(scale, at, g_ref, in_own, in_oth, own_ref, oth_ref, out_hbm, buf, sem)
    for copy in copies:
        copy.wait()


def finish(g, in_own, in_oth, own, oth, at, scale, pieces):
    rows, width = g.shape
    n = width // PAIR
    part = pieces[0][0].shape[2]
    return call(
        functools.partial(finish_body, scale, at, [kind for _, kind in pieces]),
        [g, in_own, in_oth, own, oth, *[array for array, _ in pieces]],
        [WHOLE] * (5 + len(pieces)),
        [((rows, width), BF16, False), ((at.n_inner // 2, 2, 2, part, width), BF16, False)],
        rows * width * HD,
        8 * rows * width,
        [pltpu.VMEM((n, rows, PAIR), BF16), dma(n)] + assemble_scratch(pieces, at),
    )


def assemble(pieces, at, before, width):
    n_inner = at.n_inner
    part, cols = pieces[0][0].shape[2:]
    kinds = [kind for _, kind in pieces]
    more = [] if before is None else [before]
    return call(
        functools.partial(assemble_body, kinds, at),
        [array for array, _ in pieces] + more,
        [WHOLE] * len(pieces) + [HBM] * len(more),
        [((n_inner // 2, 2, 2, part, width), BF16, False)],
        0,
        4 * sum(array.size for array, _ in pieces),
        assemble_scratch(pieces, at),
        {len(pieces): 0} if more else None,
    )[0]


def swap(x, axis, bit):
    n = lax.axis_size(axis)
    return lax.ppermute(x, axis, [(i, i ^ (1 << bit)) for i in range(n)])


def reversed_bits(value, n_bits):
    out = 0
    for b in range(n_bits):
        out = out | (((value >> b) & 1) << (n_bits - 1 - b))
    return out


def step_body(level, side, at, more, total_ref, got_ref, *refs):
    send_out, outside_out = refs[-2:]
    got = got_ref[...].astype(F32)
    total = total_ref[...] + got
    send_out[...] = total.astype(BF16)
    if more:
        refs[-3][...] = total
    if level is None:
        outside_out[...] = jnp.zeros_like(got)
    else:
        outside_out[...] = refs[0][...] + jnp.where(at.bit(*level) == side, got, 0.0)


def step(level, side, at, total, got, *outside, more=True):
    outs = [(total.shape, F32, True)] * more + [(total.shape, BF16, True), (total.shape, F32, True)]
    body = functools.partial(step_body, level, side, at, more)
    results = call(body, [total, got, *outside], [WHOLE] * (2 + len(outside)), outs)
    return results if more else [None, *results]


def last_body(level, side, at, outside_ref, got_ref, own_ref, came_ref, give_out, out):
    outside = outside_ref[...] + jnp.where(at.bit(*level) == side, got_ref[...].astype(F32), 0.0)
    mine = at.y() == side
    give_out[...] = (outside + jnp.where(mine, 0.0, own_ref[...])).astype(BF16)
    out[...] = (outside + jnp.where(mine, came_ref[...].astype(F32), 0.0)).astype(BF16)


def last(level, side, at, outside, got, own, came):
    outs = [(own.shape, BF16, True)] * 2
    return call(functools.partial(last_body, level, side, at), [outside, got, own, came], [WHOLE] * 4, outs)


def scan_states(own, sent, reverse, at):
    side = 0 if reverse else 1
    came = swap(sent, "inner", 0)
    after = yield came
    own = own()
    came = tie(came, *after)
    total, send, outside = step(None, side, at, own, came)
    levels = [("inner", b) for b in range(1, at.i_bits)] + [("outer", b) for b in range(at.o_bits)]
    for n, level in enumerate(levels):
        got = swap(send, *level)
        after = yield got
        got = tie(got, *after)
        if n + 1 < len(levels):
            total, send, outside = step(level, side, at, total, got, outside, more=n + 2 < len(levels))
    give, kept = last(levels[-1], side, at, outside, got, own, came)
    back = swap(give, "inner", 0)
    yield kept, back


def fold(keep, got, axis):
    size = keep.shape[axis] // 2
    low, high = [
        lax.slice_in_dim(keep, at, at + size, axis=axis).astype(F32)
        + lax.slice_in_dim(got, at, at + size, axis=axis).astype(F32)
        for at in (0, size)
    ]
    return high.astype(BF16), low


def fan_body(n_keep, ways, *refs):
    outs = refs[len(refs) - ways :]
    if n_keep == 2:
        rows = [(refs[0], refs[1]), (refs[2], refs[3])]
        totals = [sum(ref[0].astype(F32) for ref in pair) for pair in rows]
    else:
        totals = [sum(ref[i].astype(F32) for ref in refs[: len(refs) - ways]) for i in range(2)]
    size = outs[0].shape[1]
    for i, total in enumerate(totals):
        for j, out in enumerate(outs):
            out[i] = total[j * size : (j + 1) * size].astype(out.dtype)


def fan(n_keep, ways, *arrays):
    _, n, part, cols = arrays[0].shape
    shape = (2, n // ways, part, cols)
    outs = [(shape, F32 if j == 0 else BF16, True) for j in range(ways)]
    return call(functools.partial(fan_body, n_keep, ways), list(arrays), [WHOLE] * len(arrays), outs)


def swap_all(xs, masks):
    n = lax.axis_size("inner")
    return [lax.ppermute(x, "inner", [(i, i ^ mask) for i in range(n)]) for x, mask in zip(xs, masks)]


def bit_groups(i_bits):
    groups = []
    for b in range(1, i_bits, 2):
        if b + 1 < i_bits:
            groups.append([((i >> 1) << b) | ((i & 1) << (b + 1)) for i in range(1, 4)])
        else:
            groups.append([1 << b])
    return groups


def join_body(axis, *refs):
    out = refs[-1]
    size = refs[0].shape[axis]
    for side, ref in enumerate(refs[:-1]):
        at = tuple(pl.ds(side * size, size) if a == axis else slice(None) for a in range(len(ref.shape)))
        out[at] = ref[...]


def join(axis, *arrays):
    shape = tuple(len(arrays) * s if i == axis else s for i, s in enumerate(arrays[0].shape))
    body = functools.partial(join_body, axis)
    return call(body, list(arrays), [WHOLE] * len(arrays), [(shape, BF16, True)])[0]


def split_body(n_pieces, *refs):
    pieces, grad_ref, (p_out, q_out) = refs[:n_pieces], refs[n_pieces], refs[n_pieces + 1 :]
    for j, ref in enumerate(pieces):
        n, part = ref.shape[1:3]
        p_out[:, j * n : (j + 1) * n] = ref[0:1]
        q_out[:, j * n : (j + 1) * n] = ref[1:2]
    for i in range(2):
        q_out[0, n_pieces * n + i] = grad_ref[i * part : (i + 1) * part]


def split(grad, *arrays):
    _, n, part, cols = arrays[0].shape
    n_pieces = len(arrays)
    shapes = [(1, n_pieces * n, part, cols), (1, n_pieces * n + 2, part, cols)]
    return call(
        functools.partial(split_body, n_pieces),
        [*arrays, grad],
        [WHOLE] * (n_pieces + 1),
        [(shape, BF16, True) for shape in shapes],
    )


def rejoin_body(a_ref, b_ref, out, grads_out):
    n, part = out.shape[1:3]
    for j, ref in enumerate((a_ref, b_ref)):
        out[j : j + 1] = ref[:, :n]
        for i in range(2):
            grads_out[j, i * part : (i + 1) * part] = ref[0, n + i]


def rejoin(a, b):
    _, n, part, cols = a.shape
    outs = [((2, n - 2, part, cols), BF16, True), ((2, 2 * part, cols), BF16, True)]
    return call(rejoin_body, [a, b], [WHOLE] * 2, outs)


def local(inputs, queries, keys, values, out_grad, master, moment1, moment2):
    rows_here, width = queries.shape
    d = inputs.shape[1]
    n_outer = lax.axis_size("outer")
    n_inner = lax.axis_size("inner")
    at = Here(n_outer, n_inner)
    i_bits = at.i_bits
    assert n_outer == 4 and i_bits >= 2
    total_tokens = rows_here * n_outer * n_inner
    att_scale = 1.0 / math.sqrt(HD * total_tokens)
    grad_scale = 1.0 / math.sqrt(total_tokens)

    qg_sent = states(out_grad, queries, at, BF16)
    loaded = []

    def own_states():
        loaded.extend(load([out_grad, queries, values], at))
        return loaded[0]

    qg = scan_states(own_states, qg_sent, True, at)
    next(qg)
    qg.send([])
    g, q, v = loaded[1:]
    kv_sent, k = half_states(v, keys, at, 1, BF16, 1)
    (kv_own,) = half_states(v, tie(k, kv_sent), at, 0, F32, 0)
    kv = scan_states(lambda: kv_own, kv_sent, False, at)
    kv_stages = i_bits + 2
    done = [kv_sent]
    in_own = kv_got = None
    for _ in range(2, i_bits):
        qg.send(done)
        done = []
        if in_own is None:
            in_own = key_inside(tie(g, kv_sent), q, v, at, 0, att_scale)
            kv_got = next(kv)
            turned = turned_inputs(tie(inputs, in_own), at)
            done = [in_own, turned] + [kv_got] * 1
    qg.send(done)
    qg.send([])
    in_oth = key_inside(tie(g, in_own), q, v, at, 1, att_scale)
    qg_own, qg_oth = qg.send([in_oth])

    def kv_next(*after):
        nonlocal kv_stages, kv_got
        if kv_stages:
            kv_stages -= 1
            kv_got = kv.send(list(after))
        return kv_got

    ends = (att_scale, grad_scale)
    in_own = tie(in_own, kv_next())
    far_key, near_key, far_own, near_own = key_product(in_own, v, qg_own, turned, at, 0, (1, 0), *ends)
    keys_own = [(far_key, (0, 1)), (near_key, (0, 0))]
    got_own = swap(far_own, "outer", 0)
    far_key, far_oth = key_product(in_oth, v, qg_oth, turned, at, 1, (1,), *ends)
    got_oth = swap(far_oth, "outer", 0)
    near_key, near_oth = key_product(in_oth, v, qg_oth, turned, at, 1, (0,), *ends)
    pieces = keys_own + [(far_key, (1, 1)), (near_key, (1, 0))]

    p_send, p, q_send, q = cores(at, near_own, near_oth, got_own, got_oth)
    p_got, q_got = swap(p_send, "outer", 1), swap(q_send, "inner", 0)
    kv_next(p_send, q_send)
    p_send, p = fold(p, p_got, 1)
    q_send, q = fold(q, q_got, 0)
    p_got, q_got = swap(p_send, "inner", 0), swap(q_send, "outer", 1)
    query_own, key_grad = query_inside(tie(g, p_send, q_send), k, v, at, 0, att_scale, pieces)
    kv_next(p_send, q_send, query_own)
    groups = bit_groups(i_bits)
    keep, *sends = fan(2, 1 + len(groups[0]), p, p_got, q, q_got)
    sends[0] = tie(sends[0], query_own)
    came = swap_all(sends, groups[0])
    (query_oth,) = query_inside(tie(g, *sends), k, v, at, 1, att_scale)
    for masks in groups[1:]:
        keep, *sends = fan(1, 1 + len(masks), keep, *came)
        came = swap_all(sends, masks)
    while kv_stages > 1:
        kv_next(query_oth)
    grad, weight = adam_own([keep, *came], master, moment1, moment2, at)
    weight = tie(weight, query_oth)
    kv_own, kv_oth = kv_next(weight)

    for masks in reversed(groups[1:]):
        weight = join(1, weight, *swap_all([weight] * len(masks), masks))
    p, q = split(grad, weight, *swap_all([weight] * len(groups[0]), groups[0]))
    p_got, q_got = swap(p, "inner", 0), swap(q, "outer", 1)
    p = join(1, p, p_got)
    q, grads = rejoin(q, q_got)
    p, q, kv_oth = lax.optimization_barrier((p, q, kv_oth))
    p_last, q_last = swap(p, "outer", 1), swap(q, "inner", 0)
    p_core, q_core = swap(p, "outer", 0), swap(q, "outer", 0)
    grads_core = swap(grads, "outer", 0)
    n = n_inner // 2
    query_grad, weights = finish(
        tie(g, p, q), query_own, query_oth, kv_own, kv_oth, at, att_scale,
        [(p, (0, (0,), 0, 2 * n)), (q, (1, (0, 2), 0, n))],
    )
    new_master, new_moment1, new_moment2 = adam_all(
        tie(grads, weights), grads_core, master, moment1, moment2, at, (0, 2, 1, 3)
    )
    p_last, q_last, p_core, q_core, *_ = lax.optimization_barrier(
        (p_last, q_last, p_core, q_core, weights, query_grad, new_master)
    )
    p_end, q_end = swap(p_last, "outer", 0), swap(q_last, "outer", 0)
    weights = assemble(
        [
            (p_last, (0, (2,), 0, 2 * n)),
            (q_last, (1, (0, 2), n, n)),
            (p_core, (0, (1,), 0, 2 * n)),
            (q_core, (1, (1, 3), 0, n)),
        ],
        at, weights, width,
    )
    weights = assemble([(p_end, (0, (3,), 0, 2 * n)), (q_end, (1, (1, 3), n, n))], at, weights, width)
    return (query_grad, key_grad, new_master, new_moment1, new_moment2, weights.reshape(d, width))


def solution(mesh):
    tokens = P(("outer", "inner"), None)
    rows = P("inner", None)
    return jax.shard_map(
        local,
        mesh=mesh,
        in_specs=(tokens,) * 5 + (rows,) * 3,
        out_specs=(tokens, tokens, rows, rows, rows, P()),
        check_vma=False,
    )
```

```python
import functools
import math

import jax
import jax.numpy as jnp
from jax import lax
from jax.experimental import pallas as pl
from jax.experimental.pallas import tpu as pltpu
from jax.sharding import PartitionSpec as P

HD = 128
SUB = 256
PAIR = 2 * HD
VMEM = 16 * 1024 * 1024
F32 = jnp.float32
BF16 = jnp.bfloat16
WHOLE = pl.BlockSpec(memory_space=pltpu.VMEM)
HBM = pl.BlockSpec(memory_space=pltpu.HBM)


def mm(a, b, contract):
    return lax.dot_general(a, b, ((contract[:1], contract[1:]), ((), ())), preferred_element_type=F32)


def far(x):
    return pltpu.with_memory_space_constraint(x, pltpu.HBM)


def call(body, args, specs, outs, macs=0, moved=0, scratch=(), aliases=None):
    args = [far(a) if spec is HBM else a for a, spec in zip(args, specs)]
    return pl.pallas_call(
        body,
        in_specs=specs,
        out_specs=[WHOLE if near else HBM for _, _, near in outs],
        out_shape=[(jax.ShapeDtypeStruct if near else pltpu.HBM)(shape, dtype) for shape, dtype, near in outs],
        scratch_shapes=list(scratch),
        input_output_aliases=aliases or {},
        compiler_params=pltpu.CompilerParams(vmem_limit_bytes=VMEM),
        cost_estimate=pl.CostEstimate(flops=2 * macs, bytes_accessed=moved, transcendentals=0),
    )(*args)


def dma(n):
    return pltpu.SemaphoreType.DMA((n,))


def tie(x, *after):
    return lax.optimization_barrier((x, *after))[0] if after else x


class Here:
    def __init__(self, n_outer, n_inner):
        self.i_bits, self.o_bits = (n_inner - 1).bit_length(), (n_outer - 1).bit_length()
        self.n_outer, self.n_inner = n_outer, n_inner

    def group(self, k):
        return lax.axis_index("outer") ^ k

    def block(self, p):
        return lax.axis_index("inner") ^ reversed_bits(p, self.i_bits)

    def position(self, block):
        return reversed_bits(lax.axis_index("inner") ^ block, self.i_bits)

    def bit(self, axis, b):
        return (lax.axis_index(axis) >> b) & 1

    def y(self):
        return self.bit("inner", 0)


def states_body(at, a_hbm, b_hbm, out_ref, a_buf, b_buf, a_sem, b_sem):
    chunks, rows, cols = a_buf.shape[0] // SUB, SUB, a_buf.shape[1]
    at = pl.multiple_of((1 - at.y()) * cols, cols)
    copies = []
    for c in range(chunks):
        here = (pl.ds(c * rows, rows), pl.ds(at, cols))
        pair = (
            pltpu.make_async_copy(a_hbm.at[here], a_buf.at[pl.ds(c * rows, rows), :], a_sem.at[c]),
            pltpu.make_async_copy(b_hbm.at[here], b_buf.at[pl.ds(c * rows, rows), :], b_sem.at[c]),
        )
        for copy in pair:
            copy.start()
        copies.append(pair)
    sums = [None] * (cols // HD)
    for c in range(chunks):
        for copy in copies[c]:
            copy.wait()
        for j in range(cols // HD):
            here = (slice(c * rows, (c + 1) * rows), slice(j * HD, (j + 1) * HD))
            term = mm(a_buf[here], b_buf[here], (0, 0))
            sums[j] = term if c == 0 else sums[j] + term
    for j in range(cols // HD):
        out_ref[j] = sums[j].astype(out_ref.dtype)


def states(a, b, at, dtype):
    rows, width = a.shape
    cols = width // 2
    chunks = rows // SUB
    return call(
        functools.partial(states_body, at),
        [a, b],
        [HBM, HBM],
        [((cols // HD, HD, HD), dtype, True)] + [((rows, cols), BF16, True)] * 2,
        rows * cols * HD,
        4 * rows * cols,
        [dma(chunks), dma(chunks)],
    )


def sums_of(a_ref, b_ref, at, cols, blocks, wait):
    sums = [None] * (cols // HD)
    for b in blocks:
        wait(b)
        for j in range(cols // HD):
            here = (pl.ds(b * SUB, SUB), pl.ds(pl.multiple_of(at * cols + j * HD, HD), HD))
            term = mm(a_ref[here], b_ref[here], (0, 0))
            sums[j] = term if sums[j] is None else sums[j] + term
    return sums


def load_body(n_load, at, *refs):
    sources, out_ref, loads, sem = refs[:n_load], refs[n_load], refs[n_load + 1 : -1], refs[-1]
    rows, width = sources[0].shape
    blocks = rows // SUB
    copies = []
    for b in range(blocks):
        copies.append([])
        for n in range(n_load):
            here, cols = pl.ds(b * SUB, SUB), loads[n].shape[1]
            part = pl.ds(pl.multiple_of(at.y() * cols, cols), cols) if n < 2 else slice(None)
            copy = pltpu.make_async_copy(sources[n].at[here, part], loads[n].at[here, :], sem.at[n_load * b + n])
            copy.start()
            copies[b].append(copy)

    def wait(b):
        for copy in copies[b]:
            copy.wait()

    for j, total in enumerate(sums_of(loads[0], loads[1], 0, width // 2, range(blocks), wait)):
        out_ref[j] = total


def load(sources, at):
    rows, width = sources[0].shape
    n = len(sources)
    return call(
        functools.partial(load_body, n, at),
        sources,
        [HBM] * n,
        [((width // 2 // HD, HD, HD), F32, True)]
        + [((rows, width // 2 if i < 2 else width), BF16, True) for i in range(n)],
        rows * width // 2 * HD,
        4 * n * rows * width,
        [dma(n * (rows // SUB))],
    )


def half_states_body(at, other, n_load, a_ref, b_ref, out_ref, *refs):
    rows, width = a_ref.shape
    blocks = rows // SUB
    source = b_ref
    copies = []
    if n_load:
        source, sem = refs
        for b in range(blocks):
            here = pl.ds(b * SUB, SUB)
            copies.append(pltpu.make_async_copy(b_ref.at[here, :], source.at[here, :], sem.at[b]))
            copies[b].start()
    wait = (lambda b: copies[b].wait()) if n_load else (lambda b: None)
    for j, total in enumerate(sums_of(a_ref, source, at.y() ^ other, width // 2, range(blocks), wait)):
        out_ref[j] = total.astype(out_ref.dtype)


def half_states(a, b, at, other, dtype, n_load):
    rows, width = a.shape
    return call(
        functools.partial(half_states_body, at, other, n_load),
        [a, b],
        [WHOLE, HBM if n_load else WHOLE],
        [((width // 2 // HD, HD, HD), dtype, True)] + [((rows, width), BF16, True)] * n_load,
        rows * width * HD // 2,
        2 * rows * width,
        [dma(rows // SUB)] * n_load,
    )


def key_inside_body(scale, other, at, g_ref, q_ref, v_ref, out_ref):
    rows, cols = out_ref.shape
    later = lax.broadcasted_iota(jnp.int32, (SUB, SUB), 1) >= lax.broadcasted_iota(jnp.int32, (SUB, SUB), 0)
    for to in range(0, cols, HD):
        from_ = pl.ds(pl.multiple_of((at.y() ^ other) * cols + to, HD), HD)
        state = None
        for b in reversed(range(rows // SUB)):
            here, there = (pl.ds(b * SUB, SUB), pl.ds(to, HD)), (pl.ds(b * SUB, SUB), from_)
            g, q, v = g_ref[here], q_ref[here], v_ref[there]
            scores = jnp.where(later, mm(v, g, (1, 1)), 0.0).astype(BF16)
            total = mm(scores, q, (1, 0))
            if state is not None:
                total = total + mm(v, state.astype(BF16), (1, 0))
            out_ref[b * SUB : (b + 1) * SUB, to : to + HD] = total * scale
            if b:
                term = mm(g, q, (0, 0))
                state = term if state is None else state + term


def query_inside_body(scale, other, at, kinds, g_ref, k_ref, v_ref, *refs):
    pieces = refs[: len(kinds)]
    if kinds:
        out_ref, key_hbm, sem = refs[len(kinds) :]
    else:
        (out_ref,) = refs
    rows, cols = out_ref.shape
    copies = []
    for i, (piece, (piece_other, core)) in enumerate(zip(pieces, kinds)):
        size = piece.shape[1]
        group = (at.y() ^ piece_other) * 2 + (at.bit("outer", 0) ^ core)
        to = pl.ds(pl.multiple_of(group * size, size), size)
        copies.append(pltpu.make_async_copy(piece, key_hbm.at[:, to], sem.at[i]))
        copies[i].start()
    earlier = lax.broadcasted_iota(jnp.int32, (SUB, SUB), 0) >= lax.broadcasted_iota(jnp.int32, (SUB, SUB), 1)
    for to in range(0, cols, HD):
        from_ = pl.ds(pl.multiple_of((at.y() ^ other) * cols + to, HD), HD)
        state = None
        for b in range(rows // SUB):
            here, there = (pl.ds(b * SUB, SUB), pl.ds(to, HD)), (pl.ds(b * SUB, SUB), from_)
            g, k, v = g_ref[here], k_ref[there], v_ref[there]
            scores = jnp.where(earlier, mm(g, v, (1, 1)), 0.0).astype(BF16)
            total = mm(scores, k, (1, 0))
            if state is not None:
                total = total + mm(g, state.astype(BF16), (1, 0))
            out_ref[b * SUB : (b + 1) * SUB, to : to + HD] = total * scale
            if b + 1 < rows // SUB:
                term = mm(v, k, (0, 0))
                state = term if state is None else state + term
    for copy in copies:
        copy.wait()


def key_inside(g, q, v, at, other, scale):
    rows, width = v.shape
    cols = width // 2
    return call(
        functools.partial(key_inside_body, scale, other, at),
        [g, q, v],
        [WHOLE] * 3,
        [((rows, cols), F32, True)],
        rows * cols * (2 * SUB + 2 * HD),
        10 * rows * cols,
    )[0]


def query_inside(g, k, v, at, other, scale, pieces=()):
    rows, width = v.shape
    cols = width // 2
    kinds = [kind for _, kind in pieces]
    outs = [((rows, cols), F32, True)] + [((rows, width), BF16, False)] * bool(pieces)
    return call(
        functools.partial(query_inside_body, scale, other, at, kinds),
        [g, k, v] + [piece for piece, _ in pieces],
        [WHOLE] * (3 + len(pieces)),
        outs,
        rows * cols * (2 * SUB + 2 * HD),
        10 * rows * cols,
        [dma(len(pieces))] if pieces else [],
    )


def query_body(scale, at, g_own, g_oth, in_own, in_oth, own_ref, oth_ref, out_hbm, buf, sem):
    n, rows, cols = buf.shape
    copies = []
    for other, (g_ref, in_ref, state_ref) in enumerate(((g_own, in_own, own_ref), (g_oth, in_oth, oth_ref))):
        half = at.y() ^ other
        for p in range(n // 2):
            i = other * (n // 2) + p
            for j in range(cols // HD):
                head = p * (cols // HD) + j
                part = mm(g_ref[:, head * HD : (head + 1) * HD], state_ref[head], (1, 0))
                total = in_ref[:, head * HD : (head + 1) * HD] + part * scale
                buf[i, :, j * HD : (j + 1) * HD] = total.astype(BF16)
            to = pl.ds(pl.multiple_of((half * (n // 2) + p) * cols, cols), cols)
            copies.append(pltpu.make_async_copy(buf.at[i], out_hbm.at[:, to], sem.at[i]))
            copies[i].start()
    for copy in copies:
        copy.wait()


def turned_body(here_at, in_hbm, out_ref, buf, sem):
    size = out_ref.shape[0] // here_at.n_inner
    cols = max(size, HD)
    copies = []
    for n in range(out_ref.shape[0] // cols):
        copy = pltpu.make_async_copy(in_hbm.at[:, pl.ds(n * cols, cols)], buf.at[n], sem.at[n])
        copy.start()
        copies.append(copy)
    for n, copy in enumerate(copies):
        copy.wait()
        turned = buf[n].T
        for j in range(cols // size):
            at = pl.multiple_of(here_at.position(n * (cols // size) + j) * size, size)
            out_ref[pl.ds(at, size), :] = turned[j * size : (j + 1) * size, :]


def turned_inputs(inputs, at):
    rows, width = inputs.shape
    cols = max(width // at.n_inner, HD)
    return call(
        functools.partial(turned_body, at),
        [inputs],
        [HBM],
        [((width, rows), BF16, True)],
        0,
        4 * rows * width,
        [pltpu.VMEM((width // cols, rows, cols), BF16), dma(width // cols)],
    )[0]


def key_product_body(scale, grad_scale, at, other, cores, inside_ref, v_ref, state_ref, turned_ref, *refs):
    n = len(cores)
    cols = refs[0].shape[1]
    heads = cols // HD
    half = at.y() ^ other
    for s, core in enumerate(cores):
        key_ref, out = refs[s], refs[n + s]
        place = at.bit("outer", 0) ^ core
        for j in range(heads):
            head = place * heads + j
            here = pl.ds(pl.multiple_of(head * HD, HD), HD)
            from_ = pl.ds(pl.multiple_of((half * 2 * heads + head) * HD, HD), HD)
            part = mm(v_ref[:, from_], state_ref[head], (1, 0))
            key_ref[:, j * HD : (j + 1) * HD] = (inside_ref[:, here] + part * scale).astype(BF16)
        product = (mm(turned_ref[...], key_ref[...], (1, 0)) * grad_scale).astype(BF16)
        size = product.shape[0] // at.n_inner
        for r in range(at.n_inner):
            for i in range(2):
                out[i, r] = product[r * size + i * (size // 2) : r * size + (i + 1) * (size // 2)]


def key_product(inside, v, states, turned, at, other, cores, scale, grad_scale):
    n = len(cores)
    rows, width = v.shape
    cols = width // at.n_outer
    d = turned.shape[0]
    piece = ((2, at.n_inner, d // at.n_inner // 2, cols), BF16, True)
    return call(
        functools.partial(key_product_body, scale, grad_scale, at, other, cores),
        [inside, v, states, turned],
        [WHOLE] * 4,
        [((rows, cols), BF16, True)] * n + [piece] * n,
        n * cols * rows * (d + HD),
        2 * rows * (d + 4 * n * cols),
    )


def cores_body(at, *refs):
    (n_own, n_oth, g_own, g_oth), (p_send, p_keep, q_send, q_keep) = refs[:4], refs[4:]
    far_own = at.bit("outer", 1) ^ at.y()
    p_own = n_own[0].astype(F32) + g_own[0].astype(F32)
    p_oth = n_oth[0].astype(F32) + g_oth[0].astype(F32)
    p_send[0] = jnp.where(far_own == 1, p_own, p_oth).astype(BF16)
    p_keep[0] = jnp.where(far_own == 1, p_oth, p_own)
    n = n_own.shape[1] // 2
    for side, near, got in ((far_own, n_own, g_own), (1 - far_own, n_oth, g_oth)):
        q_keep[side] = near[1, :n].astype(F32) + got[1, :n].astype(F32)
        q_send[side] = (near[1, n:].astype(F32) + got[1, n:].astype(F32)).astype(BF16)


def cores(at, near_own, near_oth, got_own, got_oth):
    _, n, part, cols = near_own.shape
    one, two = (1, n, part, cols), (2, n // 2, part, cols)
    return call(
        functools.partial(cores_body, at),
        [near_own, near_oth, got_own, got_oth],
        [WHOLE] * 4,
        [(one, BF16, True), (one, F32, True), (two, BF16, True), (two, F32, True)],
    )


def adam(grad, master, moment1, moment2):
    new_moment1 = 0.9 * moment1 + 0.1 * grad
    new_moment2 = 0.95 * moment2 + 0.05 * grad * grad
    new_master = master - 0.01 * (new_moment1 / (jnp.sqrt(new_moment2) + 1e-08) + 0.1 * master)
    return new_master, new_moment1, new_moment2


def adam_own_body(at, n, *refs):
    sums, (master_ref, m1_ref, m2_ref, grad_ref, weight_ref) = refs[:n], refs[n:]
    _, _, part, size = sums[0].shape
    cols = pl.ds(pl.multiple_of(at.group(0) * size, size), size)
    for j in range(2):
        here = slice(j * part, (j + 1) * part)
        grad = sum(ref[j, 0].astype(F32) for ref in sums).astype(BF16)
        grad_ref[here, :] = grad
        new_master, _, _ = adam(grad.astype(F32), master_ref[here, cols], m1_ref[here, cols], m2_ref[here, cols])
        weight_ref[j, 0] = new_master.astype(BF16)


def adam_own(sums, master, moment1, moment2, at):
    shape = sums[0].shape
    _, _, part, cols = shape
    return call(
        functools.partial(adam_own_body, at, len(sums)),
        [*sums, master, moment1, moment2],
        [WHOLE] * (len(sums) + 3),
        [((2 * part, cols), BF16, True), (shape, BF16, True)],
        2 * part * cols,
        48 * part * cols,
    )


def adam_all_body(picks, at, own_ref, core_ref, master_ref, m1_ref, m2_ref, *refs):
    outs, bufs, sem = refs[:3], refs[3:6], refs[6]
    size = own_ref.shape[2]
    copies = []
    for s, pick in enumerate(picks):
        grad = (own_ref if s < 2 else core_ref)[s % 2].astype(F32)
        cols = pl.ds(pl.multiple_of(at.group(pick) * size, size), size)
        new = adam(grad, master_ref[:, cols], m1_ref[:, cols], m2_ref[:, cols])
        for i in range(3):
            bufs[i][s] = new[i]
            copy = pltpu.make_async_copy(bufs[i].at[s], outs[i].at[:, cols], sem.at[s * 3 + i])
            copy.start()
            copies.append(copy)
    for copy in copies:
        copy.wait()


def adam_all(own, core, master, moment1, moment2, at, picks):
    n = len(picks)
    _, rows, cols = own.shape
    return call(
        functools.partial(adam_all_body, picks, at),
        [own, core, master, moment1, moment2],
        [WHOLE] * 5,
        [(master.shape, F32, False)] * 3,
        n * rows * cols,
        26 * n * rows * cols,
        [pltpu.VMEM((n, rows, cols), F32)] * 3 + [dma(3 * n)],
    )


def assemble_start(kinds, at, pieces, out_hbm, bufs, sem):
    copies = []
    for i, (which, groups, start, count) in enumerate(kinds):
        size = pieces[i].shape[-1]
        for s, k in enumerate(groups):
            cols = pl.ds(pl.multiple_of(at.group(k) * size, size), size)
            for r in range(count):
                block = at.block(start + r)
                if which:
                    bufs[i][s, block // 2] = pieces[i][s, r]
                else:
                    bufs[i][s, block // 2, block % 2] = pieces[i][s, r]
            if which:
                goal = out_hbm.at[:, at.block(start) % 2, which, :, cols]
            else:
                goal = out_hbm.at[:, :, which, :, cols]
            copy = pltpu.make_async_copy(bufs[i].at[s], goal, sem.at[2 * i + s])
            copy.start()
            copies.append(copy)
    return copies


def assemble_body(kinds, at, *refs):
    n = len(kinds)
    for copy in assemble_start(kinds, at, refs[:n], refs[-n - 2], refs[-n - 1 : -1], refs[-1]):
        copy.wait()


def assemble_scratch(pieces, at):
    part, cols = pieces[0][0].shape[2:]
    bufs = [
        pltpu.VMEM((len(groups), at.n_inner // 2) + (() if which else (2,)) + (part, cols), BF16)
        for _, (which, groups, _, _) in pieces
    ]
    return bufs + [dma(2 * len(pieces))]


def finish_body(scale, at, kinds, g_own, g_oth, in_own, in_oth, own_ref, oth_ref, *refs):
    n = len(kinds)
    pieces, (out_hbm, weights_hbm, buf, sem) = refs[:n], refs[n : n + 4]
    copies = assemble_start(kinds, at, pieces, weights_hbm, refs[n + 4 : -1], refs[-1])
    query_body(scale, at, g_own, g_oth, in_own, in_oth, own_ref, oth_ref, out_hbm, buf, sem)
    for copy in copies:
        copy.wait()


def finish(g_own, g_oth, in_own, in_oth, own, oth, at, scale, pieces):
    rows, width = g_own.shape[0], 2 * g_own.shape[1]
    n = width // PAIR
    part = pieces[0][0].shape[2]
    return call(
        functools.partial(finish_body, scale, at, [kind for _, kind in pieces]),
        [g_own, g_oth, in_own, in_oth, own, oth, *[array for array, _ in pieces]],
        [WHOLE] * (6 + len(pieces)),
        [((rows, width), BF16, False), ((at.n_inner // 2, 2, 2, part, width), BF16, False)],
        rows * width * HD,
        8 * rows * width,
        [pltpu.VMEM((n, rows, PAIR), BF16), dma(n)] + assemble_scratch(pieces, at),
    )


def assemble(pieces, at, before, width):
    n_inner = at.n_inner
    part, cols = pieces[0][0].shape[2:]
    kinds = [kind for _, kind in pieces]
    more = [] if before is None else [before]
    return call(
        functools.partial(assemble_body, kinds, at),
        [array for array, _ in pieces] + more,
        [WHOLE] * len(pieces) + [HBM] * len(more),
        [((n_inner // 2, 2, 2, part, width), BF16, False)],
        0,
        4 * sum(array.size for array, _ in pieces),
        assemble_scratch(pieces, at),
        {len(pieces): 0} if more else None,
    )[0]


def swap(x, axis, bit):
    n = lax.axis_size(axis)
    return lax.ppermute(x, axis, [(i, i ^ (1 << bit)) for i in range(n)])


def reversed_bits(value, n_bits):
    out = 0
    for b in range(n_bits):
        out = out | (((value >> b) & 1) << (n_bits - 1 - b))
    return out


def step_body(level, side, at, more, total_ref, got_ref, *refs):
    send_out, outside_out = refs[-2:]
    got = got_ref[...].astype(F32)
    total = total_ref[...] + got
    send_out[...] = total.astype(BF16)
    if more:
        refs[-3][...] = total
    if level is None:
        outside_out[...] = jnp.zeros_like(got)
    else:
        outside_out[...] = refs[0][...] + jnp.where(at.bit(*level) == side, got, 0.0)


def step(level, side, at, total, got, *outside, more=True):
    outs = [(total.shape, F32, True)] * more + [(total.shape, BF16, True), (total.shape, F32, True)]
    body = functools.partial(step_body, level, side, at, more)
    results = call(body, [total, got, *outside], [WHOLE] * (2 + len(outside)), outs)
    return results if more else [None, *results]


def last_body(level, side, at, outside_ref, got_ref, own_ref, came_ref, give_out, out):
    outside = outside_ref[...] + jnp.where(at.bit(*level) == side, got_ref[...].astype(F32), 0.0)
    mine = at.y() == side
    give_out[...] = (outside + jnp.where(mine, 0.0, own_ref[...])).astype(BF16)
    out[...] = (outside + jnp.where(mine, came_ref[...].astype(F32), 0.0)).astype(BF16)


def last(level, side, at, outside, got, own, came):
    outs = [(own.shape, BF16, True)] * 2
    return call(functools.partial(last_body, level, side, at), [outside, got, own, came], [WHOLE] * 4, outs)


def scan_states(own, sent, reverse, at):
    side = 0 if reverse else 1
    came = swap(sent, "inner", 0)
    after = yield came
    own = own()
    came = tie(came, *after)
    total, send, outside = step(None, side, at, own, came)
    levels = [("inner", b) for b in range(1, at.i_bits)] + [("outer", b) for b in range(at.o_bits)]
    for n, level in enumerate(levels):
        got = swap(send, *level)
        after = yield got
        got = tie(got, *after)
        if n + 1 < len(levels):
            total, send, outside = step(level, side, at, total, got, outside, more=n + 2 < len(levels))
    give, kept = last(levels[-1], side, at, outside, got, own, came)
    back = swap(give, "inner", 0)
    yield kept, back


def fold(keep, got, axis):
    size = keep.shape[axis] // 2
    low, high = [
        lax.slice_in_dim(keep, at, at + size, axis=axis).astype(F32)
        + lax.slice_in_dim(got, at, at + size, axis=axis).astype(F32)
        for at in (0, size)
    ]
    return high.astype(BF16), low


def fan_body(n_keep, ways, *refs):
    outs = refs[len(refs) - ways :]
    if n_keep == 2:
        rows = [(refs[0], refs[1]), (refs[2], refs[3])]
        totals = [sum(ref[0].astype(F32) for ref in pair) for pair in rows]
    else:
        totals = [sum(ref[i].astype(F32) for ref in refs[: len(refs) - ways]) for i in range(2)]
    size = outs[0].shape[1]
    for i, total in enumerate(totals):
        for j, out in enumerate(outs):
            out[i] = total[j * size : (j + 1) * size].astype(out.dtype)


def fan(n_keep, ways, *arrays):
    _, n, part, cols = arrays[0].shape
    shape = (2, n // ways, part, cols)
    outs = [(shape, F32 if j == 0 else BF16, True) for j in range(ways)]
    return call(functools.partial(fan_body, n_keep, ways), list(arrays), [WHOLE] * len(arrays), outs)


def swap_all(xs, masks):
    n = lax.axis_size("inner")
    return [lax.ppermute(x, "inner", [(i, i ^ mask) for i in range(n)]) for x, mask in zip(xs, masks)]


def bit_groups(i_bits):
    groups = []
    for b in range(1, i_bits, 2):
        if b + 1 < i_bits:
            groups.append([((i >> 1) << b) | ((i & 1) << (b + 1)) for i in range(1, 4)])
        else:
            groups.append([1 << b])
    return groups


def join_body(axis, *refs):
    out = refs[-1]
    size = refs[0].shape[axis]
    for side, ref in enumerate(refs[:-1]):
        at = tuple(pl.ds(side * size, size) if a == axis else slice(None) for a in range(len(ref.shape)))
        out[at] = ref[...]


def join(axis, *arrays):
    shape = tuple(len(arrays) * s if i == axis else s for i, s in enumerate(arrays[0].shape))
    body = functools.partial(join_body, axis)
    return call(body, list(arrays), [WHOLE] * len(arrays), [(shape, BF16, True)])[0]


def split_body(n_pieces, *refs):
    pieces, grad_ref, (p_out, q_out) = refs[:n_pieces], refs[n_pieces], refs[n_pieces + 1 :]
    for j, ref in enumerate(pieces):
        n, part = ref.shape[1:3]
        p_out[:, j * n : (j + 1) * n] = ref[0:1]
        q_out[:, j * n : (j + 1) * n] = ref[1:2]
    for i in range(2):
        q_out[0, n_pieces * n + i] = grad_ref[i * part : (i + 1) * part]


def split(grad, *arrays):
    _, n, part, cols = arrays[0].shape
    n_pieces = len(arrays)
    shapes = [(1, n_pieces * n, part, cols), (1, n_pieces * n + 2, part, cols)]
    return call(
        functools.partial(split_body, n_pieces),
        [*arrays, grad],
        [WHOLE] * (n_pieces + 1),
        [(shape, BF16, True) for shape in shapes],
    )


def rejoin_body(a_ref, b_ref, out, grads_out):
    n, part = out.shape[1:3]
    for j, ref in enumerate((a_ref, b_ref)):
        out[j : j + 1] = ref[:, :n]
        for i in range(2):
            grads_out[j, i * part : (i + 1) * part] = ref[0, n + i]


def rejoin(a, b):
    _, n, part, cols = a.shape
    outs = [((2, n - 2, part, cols), BF16, True), ((2, 2 * part, cols), BF16, True)]
    return call(rejoin_body, [a, b], [WHOLE] * 2, outs)


def local(inputs, queries, keys, values, out_grad, master, moment1, moment2):
    rows_here, width = queries.shape
    d = inputs.shape[1]
    n_outer = lax.axis_size("outer")
    n_inner = lax.axis_size("inner")
    at = Here(n_outer, n_inner)
    i_bits = at.i_bits
    assert n_outer == 4 and i_bits >= 2
    total_tokens = rows_here * n_outer * n_inner
    att_scale = 1.0 / math.sqrt(HD * total_tokens)
    grad_scale = 1.0 / math.sqrt(total_tokens)

    qg_sent, g_oth, q_oth = states(out_grad, queries, at, BF16)
    loaded = []

    def own_states():
        loaded.extend(load([out_grad, queries, values, keys], at))
        return loaded[0]

    qg = scan_states(own_states, qg_sent, True, at)
    next(qg)
    qg.send([])
    g, q, v, k = loaded[1:]
    (kv_sent,) = half_states(v, k, at, 1, BF16, 0)
    (kv_own,) = half_states(v, tie(k, kv_sent), at, 0, F32, 0)
    kv = scan_states(lambda: kv_own, kv_sent, False, at)
    kv_stages = i_bits + 2
    done = [kv_sent]
    in_own = kv_got = None
    for _ in range(2, i_bits):
        qg.send(done)
        done = []
        if in_own is None:
            in_own = key_inside(tie(g, kv_sent), q, v, at, 0, att_scale)
            kv_got = next(kv)
            turned = turned_inputs(tie(inputs, in_own), at)
            done = [in_own, turned] + [kv_got] * 1
    qg.send(done)
    qg.send([])
    in_oth = key_inside(tie(g_oth, in_own), q_oth, v, at, 1, att_scale)
    qg_own, qg_oth = qg.send([in_oth])

    def kv_next(*after):
        nonlocal kv_stages, kv_got
        if kv_stages:
            kv_stages -= 1
            kv_got = kv.send(list(after))
        return kv_got

    ends = (att_scale, grad_scale)
    in_own = tie(in_own, kv_next())
    far_key, near_key, far_own, near_own = key_product(in_own, v, qg_own, turned, at, 0, (1, 0), *ends)
    keys_own = [(far_key, (0, 1)), (near_key, (0, 0))]
    got_own = swap(far_own, "outer", 0)
    far_key, far_oth = key_product(in_oth, v, qg_oth, turned, at, 1, (1,), *ends)
    got_oth = swap(far_oth, "outer", 0)
    near_key, near_oth = key_product(in_oth, v, qg_oth, turned, at, 1, (0,), *ends)
    pieces = keys_own + [(far_key, (1, 1)), (near_key, (1, 0))]

    p_send, p, q_send, q = cores(at, near_own, near_oth, got_own, got_oth)
    p_got, q_got = swap(p_send, "outer", 1), swap(q_send, "inner", 0)
    kv_next(p_send, q_send)
    p_send, p = fold(p, p_got, 1)
    q_send, q = fold(q, q_got, 0)
    p_got, q_got = swap(p_send, "inner", 0), swap(q_send, "outer", 1)
    query_own, key_grad = query_inside(tie(g, p_send, q_send), k, v, at, 0, att_scale, pieces)
    kv_next(p_send, q_send, query_own)
    groups = bit_groups(i_bits)
    keep, *sends = fan(2, 1 + len(groups[0]), p, p_got, q, q_got)
    sends[0] = tie(sends[0], query_own)
    came = swap_all(sends, groups[0])
    (query_oth,) = query_inside(tie(g_oth, *sends), k, v, at, 1, att_scale)
    for masks in groups[1:]:
        keep, *sends = fan(1, 1 + len(masks), keep, *came)
        came = swap_all(sends, masks)
    while kv_stages > 1:
        kv_next(query_oth)
    grad, weight = adam_own([keep, *came], master, moment1, moment2, at)
    weight = tie(weight, query_oth)
    kv_own, kv_oth = kv_next(weight)

    for masks in reversed(groups[1:]):
        weight = join(1, weight, *swap_all([weight] * len(masks), masks))
    p, q = split(grad, weight, *swap_all([weight] * len(groups[0]), groups[0]))
    p_got, q_got = swap(p, "inner", 0), swap(q, "outer", 1)
    p = join(1, p, p_got)
    q, grads = rejoin(q, q_got)
    p, q, kv_oth = lax.optimization_barrier((p, q, kv_oth))
    p_last, q_last = swap(p, "outer", 1), swap(q, "inner", 0)
    p_core, q_core = swap(p, "outer", 0), swap(q, "outer", 0)
    grads_core = swap(grads, "outer", 0)
    n = n_inner // 2
    query_grad, weights = finish(
        tie(g, p, q), g_oth, query_own, query_oth, kv_own, kv_oth, at, att_scale,
        [(p, (0, (0,), 0, 2 * n)), (q, (1, (0, 2), 0, n))],
    )
    new_master, new_moment1, new_moment2 = adam_all(
        tie(grads, weights), grads_core, master, moment1, moment2, at, (0, 2, 1, 3)
    )
    p_last, q_last, p_core, q_core, *_ = lax.optimization_barrier(
        (p_last, q_last, p_core, q_core, weights, query_grad, new_master)
    )
    p_end, q_end = swap(p_last, "outer", 0), swap(q_last, "outer", 0)
    weights = assemble(
        [
            (p_last, (0, (2,), 0, 2 * n)),
            (q_last, (1, (0, 2), n, n)),
            (p_core, (0, (1,), 0, 2 * n)),
            (q_core, (1, (1, 3), 0, n)),
        ],
        at, weights, width,
    )
    weights = assemble([(p_end, (0, (3,), 0, 2 * n)), (q_end, (1, (1, 3), n, n))], at, weights, width)
    return (query_grad, key_grad, new_master, new_moment1, new_moment2, weights.reshape(d, width))


def solution(mesh):
    tokens = P(("outer", "inner"), None)
    rows = P("inner", None)
    return jax.shard_map(
        local,
        mesh=mesh,
        in_specs=(tokens,) * 5 + (rows,) * 3,
        out_specs=(tokens, tokens, rows, rows, rows, P()),
        check_vma=False,
    )
```
